32 devices in a mesh: wide: 4 (over z), pair: 4 (over y, x), chip: 2 (over core).
Axes of the slice: x: 2, y: 2, z: 4, core: 2. Of those that a mesh axis runs over, the one named last changes fastest.
Arguments:
- expression: bfloat16 [8192, 7000], P(('wide', 'pair', 'chip')), may hold values from 0 to 6, as said below
- noise: float32 [8192, 100], P(('wide', 'pair', 'chip')), may hold values from -6 to 6
- study: int32 [8192], P(('wide', 'pair', 'chip')), may hold values from 0 to 7
- measured_gene_mask: int32 [8, 7000], replicated, may hold values 0 or 1
- encoder_input_weight: bfloat16 [7000, 800], P(('pair', 'chip'), 'wide'), may hold values from -0.0625 to 0.0625
- enc_mid: bfloat16 [800, 800], P(('pair', 'chip'), 'wide'), may hold values from -0.21875 to 0.21875
- heads: bfloat16 [200, 800], P(('pair', 'chip'), 'wide'), may hold values from -0.21875 to 0.21875
- dec_in: bfloat16 [100, 800], P(None, 'wide'), may hold values from -0.625 to 0.625
- dec_mid: bfloat16 [800, 800], P(('pair', 'chip'), 'wide'), may hold values from -0.21875 to 0.21875
- dec_out: bfloat16 [7000, 800], P(('pair', 'chip'), 'wide'), may hold values from -0.21875 to 0.21875
- norm_params: bfloat16 [8, 800], P(('pair', 'chip'), 'wide'), may hold values from 0.5 to 1.5
- head_bias: float32 [200], replicated, may hold values from -3 to 3
- out_bias: float32 [7000], replicated, may hold values from -3 to 3
- running_stats: float32 [8, 800], P(('pair', 'chip'), 'wide'), may hold values from 0.5 to 1.5
Outputs:
- loss: float32 [], replicated
- input_grad: float32 [8192, 7000], P(('wide', 'pair', 'chip'))
- enc_in_grad: float32 [7000, 800], P(('pair', 'chip'), 'wide')
- enc_mid_grad: float32 [800, 800], P(('pair', 'chip'), 'wide')
- heads_grad: float32 [200, 800], P(('pair', 'chip'), 'wide')
- dec_in_grad: float32 [100, 800], P(None, 'wide')
- dec_mid_grad: float32 [800, 800], P(('pair', 'chip'), 'wide')
- dec_out_grad: float32 [7000, 800], P(('pair', 'chip'), 'wide')
- norm_grad: float32 [8, 800], P(('pair', 'chip'), 'wide')
- head_bias_grad: float32 [200], replicated
- out_bias_grad: float32 [7000], replicated
- running_next: float32 [8, 800], P(('pair', 'chip'), 'wide')
The draws below stay inside these ranges and needn't reach their ends.
Inputs may be any that keep to these rules, and one draw needn't show every extreme that they name: Non-negative expression values.
All inputs are finite; a program needn't handle non-finite values.
Results may differ from the reference program's by a relative error of at most 0.014.
Values may be sent and summed in bfloat16 or wider, within the bound.
No kernel may reach another device: no remote copies, remote signals or barrier semaphores. Data moves between devices by JAX's collectives and lax.ppermute only.
A program may use at most 448 MiB of HBM per device.

```python
import jax
import jax.numpy as jnp
from jax import lax

GENE_COUNT = 7000
UNITS = 800
LATENT = 100
STUDY_COUNT = 8
CELL_COUNT = 8192


def draw_expression(key, part):
    cell_key = jax.random.fold_in(key, 0)
    entry_key = jax.random.fold_in(key, 2)
    cell_scale = jnp.exp(jax.random.uniform(cell_key, (CELL_COUNT, 1), jnp.float32, jnp.log(0.3), jnp.log(3.0)))
    entries = jax.random.uniform(entry_key, (CELL_COUNT, GENE_COUNT), jnp.float32, 0.0, 2.0)
    values = cell_scale * entries
    return values.astype(jnp.bfloat16)


def with_ends(drawn, stream_key, least, top_value):
    longest = drawn.shape.index(max(drawn.shape))
    spots = []
    for shift in (0, 1):
        where = [jax.random.randint(jax.random.fold_in(stream_key, axis), (), 0, length) for axis, length in enumerate(drawn.shape)]
        where[longest] = (where[longest] + shift) % drawn.shape[longest]
        spots.append(tuple(where))
    return drawn.at[spots[0]].set(least).at[spots[1]].set(top_value)


def block_levels(stream_key, extent, cuts, least, largest):
    level = 1.0
    for dim, parts in cuts:
        heights = jax.random.uniform(jax.random.fold_in(jax.random.fold_in(stream_key, 6), dim), (parts,), jnp.float32, least / len(cuts), largest / len(cuts))
        level = level * jnp.repeat(jnp.exp(heights), extent[dim] // parts).reshape((-1,) + (1,) * (len(extent) - 1 - dim))
    return level


def centred(own_key, shape, scale, bound, shards=(), kind=jnp.bfloat16):
    values = scale * jax.random.normal(own_key, shape, jnp.float32)
    if shards:
        values = values * block_levels(own_key, shape, shards, -0.22, 0.18)
    return jnp.clip(values, -bound, bound).astype(kind)


def setup_inputs(seed: int = 0) -> dict:
    keys = jax.random.split(jax.random.key(seed), 15)
    expression = draw_expression(jax.random.fold_in(keys[14], 71), 0)
    noise = centred(keys[1], (CELL_COUNT, LATENT), 1.0, 6.0, ((0, 32),), jnp.float32)
    study = with_ends(jax.random.randint(keys[2], (CELL_COUNT,), 0, STUDY_COUNT), jax.random.fold_in(keys[2], 1), 0, STUDY_COUNT - 1).astype(jnp.int32)
    measured_gene_mask = with_ends((jax.random.randint(keys[3], (STUDY_COUNT, GENE_COUNT), 0, 4) < 3).astype(jnp.int32), jax.random.fold_in(keys[3], 1), 0, 1)
    encoder_input_weight = centred(keys[4], (GENE_COUNT, UNITS), GENE_COUNT ** -0.5, 0.0625, ((0, 8), (1, 4)))
    enc_mid = centred(keys[5], (UNITS, UNITS), UNITS ** -0.5, 0.21875, ((0, 8), (1, 4)))
    heads = centred(keys[6], (2 * LATENT, UNITS), UNITS ** -0.5, 0.21875, ((0, 8), (1, 4)))
    dec_in = centred(keys[7], (LATENT, UNITS), LATENT ** -0.5, 0.625, ((1, 4),))
    dec_mid = centred(keys[8], (UNITS, UNITS), UNITS ** -0.5, 0.21875, ((0, 8), (1, 4)))
    dec_out = centred(keys[9], (GENE_COUNT, UNITS), UNITS ** -0.5, 0.21875, ((0, 8), (1, 4)))
    norm_params = jnp.clip(1.0 + 0.1 * jax.random.normal(keys[10], (8, UNITS), jnp.float32), 0.5, 1.5).astype(jnp.bfloat16)
    head_bias = centred(keys[11], (2 * LATENT,), 0.5, 3.0, (), jnp.float32)
    out_bias = centred(keys[12], (GENE_COUNT,), 0.5, 3.0, (), jnp.float32)
    running_stats = jnp.clip(0.5 + 1.0 * jax.random.uniform(keys[13], (8, UNITS), jnp.float32) ** block_levels(keys[13], (8, UNITS), ((0, 8), (1, 4)), -0.2, 0.2), 0.5, 1.5)
    return dict(expression=expression, noise=noise, study=study, measured_gene_mask=measured_gene_mask, encoder_input_weight=encoder_input_weight, enc_mid=enc_mid, heads=heads, dec_in=dec_in, dec_mid=dec_mid, dec_out=dec_out, norm_params=norm_params, head_bias=head_bias, out_bias=out_bias, running_stats=running_stats)


@jax.custom_vjp
def low(v):
    return lax.optimization_barrier(v.astype(jnp.bfloat16)).astype(jnp.float32)

@jax.custom_vjp
def low_back(v):
    return v

def low_keep(v):
    return (low(v), None)

def low_pass(kept, grad):
    return (grad,)

def back_keep(v):
    return (v, None)

def back_low(kept, grad):
    return (low(grad),)
low.defvjp(low_keep, low_pass)
low_back.defvjp(back_keep, back_low)
ALPHA = 0.005
EPSILON = 1e-05
MOMENTUM = 0.1

def matmul(left, right):
    return jnp.dot(left, right, precision=lax.Precision.HIGHEST, preferred_element_type=jnp.float32)

def normalize(pre_act, gain, shift):
    centre = lax.optimization_barrier(jnp.mean(pre_act, axis=0))
    variance = lax.optimization_barrier(jnp.mean(jnp.square(pre_act - centre), axis=0))
    scaled = (pre_act - centre) * lax.rsqrt(variance + EPSILON)
    return (scaled * gain + shift, centre, variance)

def reference(expression, noise, study, measured_gene_mask, encoder_input_weight, enc_mid, heads, dec_in, dec_mid, dec_out, norm_params, head_bias, out_bias, running_stats):
    count_all = expression.shape[0]
    keep = measured_gene_mask[study].astype(jnp.float32)
    noise_f = noise.astype(jnp.float32)

    def forward(expr_f, w_enc_in, w_enc_mid, w_heads, w_dec_in, w_dec_mid, w_dec_out, norm_f, bias_heads, bias_out):
        gains = norm_f[:4]
        shifts = norm_f[4:]
        pre_one = low_back(matmul(expr_f, w_enc_in))
        normed, centre_one, spread_one = normalize(pre_one, gains[0], shifts[0])
        hidden_one = low(jax.nn.silu(normed))
        pre_two = low_back(matmul(hidden_one, w_enc_mid))
        normed, centre_two, spread_two = normalize(pre_two, gains[1], shifts[1])
        hidden_two = low(jax.nn.silu(normed))
        encoded = low_back(matmul(hidden_two, w_heads.T) + bias_heads)
        latent_mean = encoded[:, :LATENT]
        logvar = encoded[:, LATENT:]
        code = low(latent_mean + jnp.exp(0.5 * logvar) * noise_f)
        pre_three = low_back(matmul(code, w_dec_in))
        normed, centre_three, spread_three = normalize(pre_three, gains[2], shifts[2])
        hidden_three = low(jax.nn.silu(normed))
        pre_four = low_back(matmul(hidden_three, w_dec_mid))
        normed, centre_four, spread_four = normalize(pre_four, gains[3], shifts[3])
        hidden_four = low(jax.nn.silu(normed))
        out_pre = low_back(matmul(hidden_four, w_dec_out.T) + bias_out)
        recon = jax.nn.softplus(out_pre)
        diff = recon - expr_f
        recon_term = 0.5 * lax.optimization_barrier(jnp.sum(keep * diff * diff, axis=1))
        kl_term = 0.5 * lax.optimization_barrier(jnp.sum(jnp.exp(logvar) + latent_mean * latent_mean - 1.0 - logvar, axis=1))
        loss = jnp.mean(recon_term + ALPHA * kl_term)
        centres = jnp.stack([centre_one, centre_two, centre_three, centre_four])
        spreads = jnp.stack([spread_one, spread_two, spread_three, spread_four])
        return (loss, (centres, spreads))
    params = (expression.astype(jnp.float32), encoder_input_weight.astype(jnp.float32), enc_mid.astype(jnp.float32), heads.astype(jnp.float32), dec_in.astype(jnp.float32), dec_mid.astype(jnp.float32), dec_out.astype(jnp.float32), norm_params.astype(jnp.float32), head_bias.astype(jnp.float32), out_bias.astype(jnp.float32))
    loss, pullback, stats = jax.vjp(forward, *params, has_aux=True)
    grads = pullback(jnp.ones_like(loss))
    centres, spreads = stats
    unbiased = spreads * (count_all / (count_all - 1.0))
    running_next = (1.0 - MOMENTUM) * running_stats + MOMENTUM * jnp.concatenate([centres, unbiased], axis=0)
    input_grad = grads[0] * count_all
    return (loss, input_grad, grads[1], grads[2], grads[3], grads[4], grads[5], grads[6], grads[7], grads[8], grads[9], running_next)
```

```python
import jax
import jax.numpy as jnp
from jax import lax
from jax.sharding import PartitionSpec as P

ALPHA = 0.005
EPSILON = 1e-05
MOMENTUM = 0.1
LONGEST_RING = 8
ALL = ("wide", "pair", "chip")
BF = jnp.bfloat16
F32 = jnp.float32


def dot(left, right, dims):
    return lax.dot_general(left, right, (dims, ((), ())), preferred_element_type=F32)


def nn(left, right):
    return dot(left, right, ((1,), (0,)))


def nt(left, right):
    return dot(left, right, ((1,), (1,)))


def tn(left, right):
    return dot(left, right, ((0,), (0,)))


def swap_pair(value, bits):
    count = lax.axis_size("pair")
    return lax.ppermute(value, "pair", [(i, i ^ bits) for i in range(count)])


def swap_chip(value):
    return lax.ppermute(value, "chip", [(0, 1), (1, 0)])


def next_wide(value):
    count = lax.axis_size("wide")
    return lax.ppermute(value, "wide", [(i, (i + 1) % count) for i in range(count)])


def half_of(units):
    return max(units // 2 // 8 * 8, 1)


def spread_pair(block):
    cut = half_of(block.shape[0])
    by_x = swap_pair(block, 1)
    by_y = swap_pair(block, 2)
    upper = swap_pair(by_y[:cut], 1)
    lower = swap_pair(by_x[cut:], 2)
    return [block, by_x, by_y, jnp.concatenate([upper, lower], axis=0)]


def gather_ring(block):
    count = lax.axis_size("wide")
    if count > LONGEST_RING:
        line = lax.all_gather(block, "wide", axis=0, tiled=True)
        spread = [jnp.split(item, count) for item in spread_pair(jnp.concatenate(mirror(line)))]
        return list(zip(*spread))
    ring = [block]
    for _ in range(count - 1):
        ring.append(next_wide(ring[-1]))
    return [spread_pair(item) for item in ring]


def sum_pair(parts):
    own, for_x, for_y, for_diag = parts
    cut = half_of(own.shape[0])
    diag = for_diag.astype(BF)
    upper = swap_pair(diag[:cut], 1)
    lower = swap_pair(diag[cut:], 2)
    for_y = jnp.concatenate([for_y[:cut] + upper.astype(F32), for_y[cut:]], axis=0).astype(BF)
    for_x = jnp.concatenate([for_x[:cut], for_x[cut:] + lower.astype(F32)], axis=0).astype(BF)
    from_x = swap_pair(for_x, 1)
    from_y = swap_pair(for_y, 2)
    return own + from_x.astype(F32) + from_y.astype(F32)


def scatter_ring(make_parts):
    count = lax.axis_size("wide")
    if count > LONGEST_RING:
        parts = [jnp.concatenate(item) for item in zip(*[make_parts(s) for s in range(count)])]
        line = jnp.concatenate(mirror(sum_pair(parts))).astype(BF)
        return lax.psum_scatter(line, "wide", scatter_dimension=0, tiled=True).astype(F32)
    total = sum_pair(make_parts(1 % count))
    for step in range(2, count + 1):
        arrived = next_wide(total.astype(BF))
        total = sum_pair(make_parts(step % count)) + arrived.astype(F32)
    return total


def mirror(value):
    count = lax.axis_size("wide")
    me = lax.axis_index("wide")
    shaped = value.reshape((count, value.shape[0] // count) + value.shape[1:])
    return [
        lax.dynamic_index_in_dim(shaped, lax.rem(me - s + count, count), 0, keepdims=False)
        for s in range(count)
    ]


def share(value):
    count = lax.axis_size(ALL)
    return lax.all_to_all(
        jnp.broadcast_to(value[None], (count,) + value.shape), ALL, 0, 0, tiled=True
    )


def normalize(pre_act, gain, shift):
    cells = pre_act.shape[1]
    count = lax.axis_size(ALL)
    local_mean = jnp.mean(pre_act, axis=1)
    local_square = jnp.sum(jnp.square(pre_act - local_mean[:, None]), axis=1)
    every = share(jnp.stack([local_mean, local_square]))
    centre = jnp.mean(every[:, 0], axis=0)
    squares = jnp.sum(every[:, 1], axis=0) + cells * jnp.sum(
        jnp.square(every[:, 0] - centre), axis=0
    )
    variance = squares / (cells * count)
    inverse = lax.rsqrt(variance + EPSILON)
    scaled = (pre_act - centre[:, None]) * inverse[:, None]
    normed = scaled * gain[:, None] + shift[:, None]
    return normed, scaled, inverse, centre, variance


def norm_backward(upstream, normed, scaled, inverse, gain, extra=None):
    count_all = upstream.shape[1] * lax.axis_size(ALL)
    gate = jax.nn.sigmoid(normed)
    back_normed = upstream * gate * (1.0 + normed * (1.0 - gate))
    sums = jnp.stack([jnp.sum(back_normed, axis=1), jnp.sum(back_normed * scaled, axis=1)])
    if extra is not None:
        sums = jnp.concatenate([sums.reshape(-1), extra])
    every = jnp.sum(share(sums), axis=0)
    units = upstream.shape[0]
    flat = every.reshape(-1)
    shift_sum, gain_sum = flat[:units], flat[units : 2 * units]
    back_pre = (gain * inverse)[:, None] * (
        back_normed - shift_sum[:, None] / count_all - scaled * (gain_sum / count_all)[:, None]
    )
    return back_pre.astype(BF), gain_sum, shift_sum, flat[2 * units :]


def on_device(
    expression,
    noise,
    study,
    measured_gene_mask,
    encoder_input_weight,
    enc_mid,
    heads,
    dec_in,
    dec_mid,
    dec_out,
    norm_params,
    head_bias,
    out_bias,
    running_stats,
):
    wide_count = lax.axis_size("wide")
    row_split = lax.axis_size(("pair", "chip"))
    pair_count = lax.axis_size("pair")
    cells, genes = expression.shape
    count_all = cells * lax.axis_size(ALL)
    inv_count = 1.0 / count_all
    latent = dec_in.shape[0]
    block_genes, block_units = encoder_input_weight.shape
    units = block_units * wide_count
    pair = lax.axis_index("pair")
    chip = lax.axis_index("chip")
    block_id = pair * 2 + chip

    enc_blocks = gather_ring(encoder_input_weight.T)

    piece = -(-latent // row_split)
    piece_start = jnp.minimum(piece * block_id, latent - piece)
    dec_in_piece = lax.dynamic_slice_in_dim(dec_in, piece_start, piece, 0)
    packed = jnp.concatenate(
        [enc_mid.T, dec_mid.T, heads.T, dec_in_piece.T, norm_params.T], axis=1
    )
    mine = lax.all_gather(packed, ("wide", "pair"))
    other = swap_chip(mine)
    first = jnp.where(chip == 0, mine, other)
    second = jnp.where(chip == 0, other, mine)
    mid = jnp.stack([first, second], axis=1)
    mid = mid.reshape(wide_count, row_split, block_units, packed.shape[1])
    mid_rows = enc_mid.shape[0]
    head_rows = heads.shape[0]

    def pick(start, size):
        part = mid[:, :, :, start : start + size]
        return part.transpose(0, 2, 1, 3).reshape(units, row_split * size)

    w_enc_mid = pick(0, mid_rows)
    w_dec_mid = pick(mid_rows, mid_rows)
    w_heads = pick(2 * mid_rows, head_rows)
    in_all = pick(2 * mid_rows + head_rows, piece)
    lead = piece * (row_split - 1)
    w_dec_in = jnp.concatenate(
        [in_all[:, :lead], in_all[:, row_split * piece - (latent - lead) :]], axis=1
    )
    norm_full = pick(2 * mid_rows + head_rows + piece, 1).astype(F32)
    gains = [norm_full[:, k] for k in range(4)]
    shifts = [norm_full[:, 4 + k] for k in range(4)]

    by_block = expression.T.reshape(pair_count, 2, block_genes, cells)

    def block_pair(rel, which):
        return lax.dynamic_slice(
            by_block, (pair ^ rel, which, 0, 0), (1, 1, block_genes, cells)
        ).reshape(block_genes, cells)

    x_mine = [block_pair(rel, chip) for rel in range(pair_count)]
    x_send = jnp.stack([block_pair(rel, 1 - chip) for rel in range(pair_count)])
    x_recv = swap_chip(x_send)
    x_chip = [jnp.concatenate([x_mine[r], x_recv[r]], axis=1) for r in range(pair_count)]

    labels = measured_gene_mask.shape[0]
    indicator = (jnp.arange(labels, dtype=jnp.int32)[:, None] == study[None, :]).astype(BF)
    indicator = jnp.concatenate([indicator, swap_chip(indicator)], axis=1)

    rel_pre = []
    for s in range(wide_count):
        rel_pre.append(sum(nn(enc_blocks[s][r], x_chip[r]) for r in range(pair_count)))
    part_one = jnp.concatenate(rel_pre, axis=0)
    pre_one = part_one[:, :cells] + swap_chip(part_one[:, cells:])
    pre_one = jnp.concatenate(mirror(pre_one), axis=0)
    normed_one, scaled_one, inverse_one, centre_one, spread_one = normalize(
        pre_one, gains[0], shifts[0]
    )
    hidden_one = jax.nn.silu(normed_one).astype(BF)

    dec_blocks = gather_ring(lax.optimization_barrier((dec_out.T, rel_pre[-1]))[0])

    pre_two = nn(w_enc_mid, hidden_one)
    normed_two, scaled_two, inverse_two, centre_two, spread_two = normalize(
        pre_two, gains[1], shifts[1]
    )
    hidden_two = jax.nn.silu(normed_two).astype(BF)
    encoded = tn(w_heads, hidden_two) + head_bias[:, None]
    latent_mean = encoded[:latent]
    logvar = encoded[latent:]
    noise_t = noise.T
    spread_factor = jnp.exp(0.5 * logvar)
    code = (latent_mean + spread_factor * noise_t).astype(BF)
    pre_three = nn(w_dec_in, code)
    normed_three, scaled_three, inverse_three, centre_three, spread_three = normalize(
        pre_three, gains[2], shifts[2]
    )
    hidden_three = jax.nn.silu(normed_three).astype(BF)
    pre_four = nn(w_dec_mid, hidden_three)
    normed_four, scaled_four, inverse_four, centre_four, spread_four = normalize(
        pre_four, gains[3], shifts[3]
    )
    hidden_four = jax.nn.silu(normed_four).astype(BF)

    h_chip = mirror(jnp.concatenate([hidden_four, swap_chip(hidden_four)], axis=1))
    h_rel = jnp.concatenate(h_chip, axis=0)
    recon_sum = 0.0
    back_out = []
    kept_diff = []
    bias_sums = []
    back_rel = 0.0
    for r in range(pair_count):
        start = ((pair ^ r) * 2 + chip) * block_genes
        w_r = jnp.concatenate([dec_blocks[s][r] for s in range(wide_count)], axis=0)
        bias_r = lax.dynamic_slice_in_dim(out_bias, start, block_genes, 0)
        mask_r = lax.dynamic_slice_in_dim(measured_gene_mask, start, block_genes, 1).astype(BF)
        keep = tn(mask_r, indicator)
        out_pre = tn(w_r, h_rel) + bias_r[:, None]
        small = jnp.exp(-jnp.abs(out_pre))
        recon = jnp.maximum(out_pre, 0.0) + jnp.log1p(small)
        gate = jnp.where(out_pre >= 0, 1.0, small) / (1.0 + small)
        diff = recon - x_chip[r].astype(F32)
        kd = keep * diff
        recon_sum = recon_sum + jnp.sum(kd * diff)
        b_r = (kd * gate * inv_count).astype(BF)
        bias_sums.append(jnp.sum(b_r.astype(F32), axis=1))
        back_out.append(b_r)
        kept_diff.append(kd)
        back_rel = back_rel + nn(w_r, b_r)
    exp_logvar = jnp.exp(logvar)
    kl_sum = jnp.sum(exp_logvar + latent_mean * latent_mean - 1.0 - logvar)
    loss_local = 0.5 * recon_sum + (0.5 * ALPHA) * kl_sum

    back_four = back_rel[:, :cells] + swap_chip(back_rel[:, cells:])
    back_four = jnp.concatenate(mirror(back_four), axis=0)

    bias_rows = jnp.zeros((row_split, block_genes), F32)
    for r in range(pair_count):
        bias_rows = lax.dynamic_update_slice_in_dim(
            bias_rows, bias_sums[r][None], (pair ^ r) * 2 + chip, 0
        )
    bp_four, gain_four, shift_four, rest = norm_backward(
        back_four,
        normed_four,
        scaled_four,
        inverse_four,
        gains[3],
        jnp.concatenate([bias_rows.reshape(-1), loss_local[None]]),
    )
    out_bias_grad = rest[:genes]
    loss = rest[genes] * inv_count

    dec_out_grad = scatter_ring(
        lambda s: [nt(h_chip[s], back_out[r]) for r in range(pair_count)]
    )

    grad_dec_mid = nt(bp_four, hidden_three)
    back_three = tn(w_dec_mid, bp_four)
    bp_three, gain_three, shift_three, _ = norm_backward(
        back_three, normed_three, scaled_three, inverse_three, gains[2]
    )
    grad_dec_in = nt(bp_three, code)
    back_code = tn(w_dec_in, bp_three)
    back_mean = back_code + ALPHA * inv_count * latent_mean
    back_logvar = (
        back_code * noise_t * spread_factor * 0.5
        + (ALPHA * 0.5 * inv_count) * (exp_logvar - 1.0)
    )
    back_enc = jnp.concatenate([back_mean, back_logvar], axis=0).astype(BF)
    head_sum = jnp.sum(back_enc.astype(F32), axis=1)
    grad_heads = nt(hidden_two, back_enc)
    back_two = nn(w_heads, back_enc)
    bp_two, gain_two, shift_two, head_bias_grad = norm_backward(
        back_two, normed_two, scaled_two, inverse_two, gains[1], head_sum
    )
    grad_enc_mid = nt(bp_two, hidden_one)
    back_one = tn(w_enc_mid, bp_two)
    bp_one, gain_one, shift_one, _ = norm_backward(
        back_one, normed_one, scaled_one, inverse_one, gains[0]
    )

    d_chip = mirror(jnp.concatenate([bp_one, swap_chip(bp_one)], axis=1))
    enc_in_grad = scatter_ring(lambda s: [nt(d_chip[s], x_chip[r]) for r in range(pair_count)])
    d_rel = jnp.concatenate(d_chip, axis=0)
    own_rows = []
    other_rows = []
    for r in range(pair_count):
        w_r = jnp.concatenate([enc_blocks[s][r] for s in range(wide_count)], axis=0)
        grad_r = tn(w_r, d_rel) * count_all - kept_diff[r]
        own_rows.append(grad_r[:, :cells])
        other_rows.append(grad_r[:, cells:].astype(BF))
    came = swap_chip(jnp.stack(other_rows))
    rows = jnp.zeros((row_split, block_genes, cells), F32)
    for r in range(pair_count):
        base = (pair ^ r) * 2
        rows = lax.dynamic_update_slice_in_dim(rows, own_rows[r][None], base + chip, 0)
        rows = lax.dynamic_update_slice_in_dim(
            rows, came[r][None].astype(F32), base + 1 - chip, 0
        )
    input_grad = rows.reshape(genes, cells).T

    def to_blocks(grad, width):
        return grad.reshape(wide_count, block_units, row_split, width).transpose(0, 2, 1, 3)

    pad = piece * row_split - latent
    dec_in_wide = jnp.pad(grad_dec_in, ((0, 0), (0, pad)))
    first_pack = jnp.concatenate(
        [to_blocks(grad_dec_mid, mid_rows), to_blocks(dec_in_wide, piece)], axis=3
    ).astype(BF)
    second_pack = jnp.concatenate(
        [to_blocks(grad_enc_mid, mid_rows), to_blocks(grad_heads, head_rows)], axis=3
    ).astype(BF)

    def scatter_all(pack):
        flat = pack.reshape((wide_count * row_split,) + pack.shape[2:])
        return lax.psum_scatter(flat, ALL, scatter_dimension=0, tiled=True)[0].astype(F32)

    first_sum = scatter_all(first_pack)
    second_sum = scatter_all(second_pack)
    in_pieces = lax.all_gather(first_sum[:, mid_rows:], ("pair", "chip"))
    dec_in_grad = in_pieces.transpose(0, 2, 1).reshape(row_split * piece, block_units)[:latent]

    wide_index = lax.axis_index("wide")
    per_row = 8 // row_split

    def mine_of(rows_full):
        stacked = jnp.stack(rows_full)
        return lax.dynamic_slice(
            stacked, (block_id * per_row, wide_index * block_units), (per_row, block_units)
        )

    norm_grad = mine_of(
        [gain_one, gain_two, gain_three, gain_four, shift_one, shift_two, shift_three, shift_four]
    )
    unbias = count_all / (count_all - 1.0)
    stats = mine_of(
        [
            centre_one,
            centre_two,
            centre_three,
            centre_four,
            spread_one * unbias,
            spread_two * unbias,
            spread_three * unbias,
            spread_four * unbias,
        ]
    )
    running_next = (1.0 - MOMENTUM) * running_stats + MOMENTUM * stats
    return (
        loss,
        input_grad,
        enc_in_grad.T,
        second_sum[:, :mid_rows].T,
        second_sum[:, mid_rows:].T,
        dec_in_grad,
        first_sum[:, :mid_rows].T,
        dec_out_grad.T,
        norm_grad,
        head_bias_grad,
        out_bias_grad,
        running_next,
    )


def solution(mesh):
    split = P(("pair", "chip"), "wide")
    by_cell = P(("wide", "pair", "chip"), None)
    return jax.shard_map(
        on_device,
        mesh=mesh,
        in_specs=(
            by_cell,
            by_cell,
            P(("wide", "pair", "chip")),
            P(),
            split,
            split,
            split,
            P(None, "wide"),
            split,
            split,
            split,
            P(),
            P(),
            split,
        ),
        out_specs=(
            P(),
            by_cell,
            split,
            split,
            split,
            P(None, "wide"),
            split,
            split,
            split,
            P(),
            P(),
            split,
        ),
        check_vma=False,
    )
```

```python
import functools

import jax
import jax.numpy as jnp
from jax import lax
from jax.experimental import pallas as pl
from jax.experimental.pallas import tpu as pltpu
from jax.sharding import PartitionSpec as P

ALPHA = 0.005
EPSILON = 1e-05
MOMENTUM = 0.1
LONGEST_RING = 4
ROUNDS = 4
ALL = ("wide", "pair", "chip")
BF = jnp.bfloat16
F32 = jnp.float32


def dot(left, right, dims):
    return lax.dot_general(left, right, (dims, ((), ())), preferred_element_type=F32)


def nn(left, right):
    return dot(left, right, ((1,), (0,)))


def nt(left, right):
    return dot(left, right, ((1,), (1,)))


def tn(left, right):
    return dot(left, right, ((0,), (0,)))


def swap_pair(value, bits):
    count = lax.axis_size("pair")
    return lax.ppermute(value, "pair", [(i, i ^ bits) for i in range(count)])


def swap_chip(value):
    return lax.ppermute(value, "chip", [(0, 1), (1, 0)])


def next_wide(value, hops=1):
    count = lax.axis_size("wide")
    return lax.ppermute(value, "wide", [(i, (i + hops) % count) for i in range(count)])


def half_of(units):
    return max(units // 2 // 8 * 8, 1)


def gate(value):
    return lax.optimization_barrier(value)


def spread_pair(block):
    cut = half_of(block.shape[0])
    by_x = swap_pair(block, 1)
    by_y = swap_pair(block, 2)
    upper = swap_pair(by_y[:cut], 1)
    lower = swap_pair(by_x[cut:], 2)
    return [block, by_x, by_y, jnp.concatenate([upper, lower], axis=0)]


def gather_ring(block, prepare, second):
    count = lax.axis_size("wide")
    if count > LONGEST_RING:
        line = lax.all_gather(block, "wide", axis=0, tiled=True)
        spread = [jnp.split(item, count) for item in spread_pair(jnp.concatenate(mirror(line)))]
        blocks = list(zip(*spread))
        (rel, whole), early = prepare()
        products = [sum(nn(left, right) for left, right in zip(row, rel)) for row in blocks]
        return blocks, products, lax.all_gather(second, "wide", axis=0, tiled=True), rel, (whole,) + early
    cut = half_of(block.shape[0])
    ring, by_x, by_y, by_diag, products, seconds = [block], [], [], [], [], [second]
    for step in range(count + 1):
        moved = {}
        if step < count:
            moved["x"] = swap_pair(ring[step], 1)
            moved["y"] = swap_pair(ring[step], 2)
        if step < count - 1:
            moved["z"] = next_wide(ring[step])
        if 0 < step < count:
            moved["d"] = next_wide(seconds[step - 1])
        if step == count - 1:
            moved["e"] = early
        if step > 0:
            moved["u"] = swap_pair(by_y[step - 1][:cut], 1)
            moved["l"] = swap_pair(by_x[step - 1][cut:], 2)
        if step == 0:
            moved["s"], early = prepare()
        if step > 1:
            done = step - 2
            row = [ring[done], by_x[done], by_y[done], by_diag[done]]
            moved["p"] = sum(nn(left, right) for left, right in zip(row, rel))
        moved = gate(moved)
        if "z" in moved:
            ring.append(moved["z"])
        if "d" in moved:
            seconds.append(moved["d"])
        if "x" in moved:
            by_x.append(moved["x"])
            by_y.append(moved["y"])
        if "u" in moved:
            by_diag.append(jnp.concatenate([moved["u"], moved["l"]], axis=0))
        if "s" in moved:
            rel, whole = moved["s"]
        if "e" in moved:
            early = moved["e"]
        if "p" in moved:
            products.append(moved["p"])
    blocks = list(zip(ring, by_x, by_y, by_diag))
    products.append(sum(nn(left, right) for left, right in zip(blocks[-1], rel)))
    second = jnp.concatenate(mirror(jnp.concatenate(seconds)))
    return blocks, products, second, rel, (whole,) + tuple(early)


def unpack_kernel(where_ref, mine_ref, other_ref, *outs, starts, places):
    chip = where_ref[0]
    count, pairs = mine_ref.shape[:2]
    for w in range(count):
        for p in range(pairs):

            def put(ref, c):
                for out, start, place in zip(outs, starts, places):
                    at, width = place[2 * p + c]
                    out[w, :, at : at + width] = ref[w, p, :, start : start + width]

            for c in range(2):

                @pl.when(chip == c)
                def _():
                    put(mine_ref, c)
                    put(other_ref, 1 - c)


def unpack_small(mine, other, widths, totals):
    count, pairs = lax.axis_size("wide"), lax.axis_size("pair")
    shape = (count, pairs) + mine.shape[1:]
    where = lax.axis_index("chip").astype(jnp.int32)[None]
    starts = [sum(widths[:i]) for i in range(len(widths))]
    places = [
        [(min(block * width, total - width), width) for block in range(2 * pairs)]
        for width, total in zip(widths, totals)
    ]
    vmem = pl.BlockSpec(memory_space=pltpu.VMEM)
    outs = pl.pallas_call(
        functools.partial(unpack_kernel, starts=starts, places=places),
        in_specs=[pl.BlockSpec(memory_space=pltpu.SMEM), vmem, vmem],
        out_specs=[vmem] * len(widths),
        out_shape=[jax.ShapeDtypeStruct((count, shape[2], total), BF) for total in totals],
        compiler_params=pltpu.CompilerParams(vmem_limit_bytes=32 * 1024 * 1024),
        name="unpack_small",
    )(where, mine.reshape(shape), other.reshape(shape))
    return [item.reshape(count * shape[2], -1) for item in outs]


def scatter_wide(blocks):
    count = lax.axis_size("wide")
    if count > LONGEST_RING:
        order = jnp.stack(blocks[-1:] + blocks[:-1])
        line = jnp.stack(mirror(order.reshape((-1,) + order.shape[2:])))
        return gate(lax.psum_scatter(line, "wide", scatter_dimension=0, tiled=True))[0].astype(F32)
    parts = [next_wide(item.astype(BF), -k) for k, item in enumerate(blocks[:-1], 1)]
    return blocks[-1].astype(F32) + sum(item.astype(F32) for item in parts)


def add_low(*terms):
    return sum(item.astype(F32) for item in terms).astype(BF)


def far_first(value):
    blocks = mirror(value)
    return blocks[1:] + blocks[:1]


def mirror(value):
    count = lax.axis_size("wide")
    me = lax.axis_index("wide")
    shaped = value.reshape((count, value.shape[0] // count) + value.shape[1:])
    return [
        lax.dynamic_index_in_dim(shaped, lax.rem(me - s + count, count), 0, keepdims=False)
        for s in range(count)
    ]


def share(value, axes=ALL):
    count = lax.axis_size(axes)
    return lax.all_to_all(
        jnp.broadcast_to(value[None], (count,) + value.shape), axes, 0, 0, tiled=True
    )


def pack_kernel(*refs):
    out_ref = refs[-1]
    chips, wide, pairs, units, _ = out_ref.shape
    start = 0
    for left_ref, right_ref in zip(refs[:-1:2], refs[1:-1:2]):
        rows = right_ref.shape[0] // (pairs * chips)
        product = nt(left_ref[...], right_ref[...])
        for w in range(wide):
            for p in range(pairs):
                for c in range(chips):
                    at = (p * chips + c) * rows
                    piece = product[w * units : (w + 1) * units, at : at + rows]
                    out_ref[c, w, p, :, start : start + rows] = piece.astype(BF)
        start += rows
    out_ref[:, :, :, :, start:] = jnp.zeros(out_ref.shape[:4] + (out_ref.shape[4] - start,), BF)


def pack_grads(*operands):
    wide, pairs = lax.axis_size("wide"), lax.axis_size("pair")
    shape = (2, wide, pairs, operands[0].shape[0] // wide, 256)
    return pl.pallas_call(
        pack_kernel,
        out_shape=jax.ShapeDtypeStruct(shape, BF),
        compiler_params=pltpu.CompilerParams(vmem_limit_bytes=40 * 1024 * 1024),
        name="pack_grads",
    )(*operands)


def add_chip(blocks):
    chip = lax.axis_index("chip")
    keep = lax.dynamic_index_in_dim(blocks, chip, 0, keepdims=False)
    send = lax.dynamic_index_in_dim(blocks, 1 - chip, 0, keepdims=False)
    return add_low(keep, swap_chip(send))


def input_kernel(*refs, scale):
    weights, (d_ref, kept_ref, own_ref, send_ref) = refs[:-4], refs[-4:]
    cells = own_ref.shape[1]
    grad = tn(weights[0][...], d_ref[0])
    for s, weight in enumerate(weights[1:], 1):
        grad = grad + tn(weight[...], d_ref[s])
    grad = grad * scale - kept_ref[...].astype(F32)
    own_ref[...] = grad[:, :cells].astype(BF)
    send_ref[...] = grad[:, cells:].astype(BF)


def input_rows(weights, d_rel, kept, scale):
    genes, cells = kept.shape
    half = jax.ShapeDtypeStruct((genes, cells // 2), BF)
    return pl.pallas_call(
        functools.partial(input_kernel, scale=scale),
        out_shape=[half, half],
        compiler_params=pltpu.CompilerParams(vmem_limit_bytes=32 * 1024 * 1024),
        name="input_rows",
    )(*weights, d_rel, kept)


def place_kernel(where_ref, own_ref, came_ref, out_ref):
    pair, chip = where_ref[0], where_ref[1]
    pairs = own_ref.shape[0]
    rows = out_ref.shape[0] // (2 * pairs)
    for p in range(pairs):
        rel = pair ^ p
        for c in range(2):
            at = pl.ds((2 * p + c) * rows, rows)

            @pl.when(chip == c)
            def _():
                out_ref[at, :] = own_ref[rel, :rows, :].astype(F32)

            @pl.when(chip != c)
            def _():
                out_ref[at, :] = came_ref[rel, :rows, :].astype(F32)


def place_rows(own, came, genes):
    where = jnp.stack([lax.axis_index("pair"), lax.axis_index("chip")]).astype(jnp.int32)
    return pl.pallas_call(
        place_kernel,
        in_specs=[
            pl.BlockSpec(memory_space=pltpu.SMEM),
            pl.BlockSpec(memory_space=pltpu.VMEM),
            pl.BlockSpec(memory_space=pltpu.VMEM),
        ],
        out_specs=pl.BlockSpec(memory_space=pltpu.VMEM),
        out_shape=jax.ShapeDtypeStruct((genes, own.shape[2]), F32),
        compiler_params=pltpu.CompilerParams(vmem_limit_bytes=40 * 1024 * 1024),
        name="place_rows",
    )(where, own, came)


def normalize(pre_act, gain, shift, rider=()):
    cells = pre_act.shape[1]
    count = lax.axis_size(ALL)
    local_mean = jnp.mean(pre_act, axis=1)
    local_square = jnp.sum(jnp.square(pre_act - local_mean[:, None]), axis=1)
    every, rider = gate((share(jnp.stack([local_mean, local_square])), rider))
    centre = jnp.mean(every[:, 0], axis=0)
    squares = jnp.sum(every[:, 1], axis=0) + cells * jnp.sum(
        jnp.square(every[:, 0] - centre), axis=0
    )
    variance = squares / (cells * count)
    inverse = lax.rsqrt(variance + EPSILON)
    scaled = (pre_act - centre[:, None]) * inverse[:, None]
    normed = scaled * gain[:, None] + shift[:, None]
    return normed, scaled, inverse, centre, variance, rider


def norm_backward(upstream, normed, scaled, inverse, gain, extra=None, pieces=None, rider=()):
    count = lax.axis_size(ALL)
    units, cells = upstream.shape
    count_all = cells * count
    gate_value = jax.nn.sigmoid(normed)
    back_normed = upstream * gate_value * (1.0 + normed * (1.0 - gate_value))
    sums = [jnp.sum(back_normed, axis=1), jnp.sum(back_normed * scaled, axis=1)]
    if extra is not None:
        sums.append(extra)
    sums = jnp.concatenate(sums)
    sent = jnp.broadcast_to(sums[None], (count,) + sums.shape)
    if pieces is not None:
        sent = jnp.concatenate([sent, pieces], axis=1)
    every, rider = gate((lax.all_to_all(sent, ALL, 0, 0, tiled=True), rider))
    both = jnp.sum(every[:, : 2 * units], axis=0)
    shift_sum, gain_sum = both[:units], both[units:]
    back_pre = (gain * inverse)[:, None] * (
        back_normed - (shift_sum / count_all)[:, None] - scaled * (gain_sum / count_all)[:, None]
    )
    return back_pre.astype(BF), gain_sum, shift_sum, every[:, 2 * units :], rider


def output_kernel(
    pair_ref,
    h_ref,
    weight_ref,
    x_ref,
    mask_ref,
    indicator_ref,
    bias_ref,
    far_ref,
    back_ref,
    kept_ref,
    bias_sum_ref,
    loss_ref,
    *refs,
    inv_count,
):
    grad_refs, (out_ref, keep_ref, low_ref) = refs[:-3], refs[-3:]
    step = pl.program_id(0)
    units, cells = h_ref.shape
    genes = x_ref.shape[1]
    weight = weight_ref[:, 0].reshape(units, genes)
    out_ref[...] = tn(weight, h_ref[...])
    keep_ref[...] = tn(mask_ref[0], indicator_ref[...])

    @pl.when(step == 0)
    def _():
        loss_ref[...] = jnp.zeros_like(loss_ref)

    rows = 64

    def chunk(i, total):
        at = pl.ds(pl.multiple_of(i * rows, rows), rows)
        out_pre = out_ref[at, :] + bias_ref[0, at, :]
        small = jnp.exp(-jnp.abs(out_pre))
        recon = jnp.maximum(out_pre, 0.0) + jnp.log1p(small)
        slope = jnp.where(out_pre >= 0, 1.0, small) / (1.0 + small)
        diff = recon - x_ref[0, at, :].astype(F32)
        kept = keep_ref[at, :] * diff
        low = (kept * slope * inv_count).astype(BF)
        kept_ref[0, at, :] = kept.astype(BF)
        low_ref[at, :] = low
        return total + jnp.sum(kept * diff, axis=0, keepdims=True)

    loss_ref[...] += lax.fori_loop(0, genes // rows, chunk, jnp.zeros((1, cells), F32), unroll=True)
    low = low_ref[...]
    bias_sum_ref[0] = nt(jnp.ones((8, cells), BF), low)
    grad = nt(far_ref[...], low).astype(BF)
    rows = units // ROUNDS
    for r in range(len(grad_refs) // ROUNDS):

        @pl.when(step == r)
        def _():
            for k in range(ROUNDS):
                grad_refs[r * ROUNDS + k][...] = grad[k * rows : (k + 1) * rows]

    back = nn(weight, low)

    @pl.when(step == 0)
    def _():
        back_ref[...] = back

    @pl.when(step > 0)
    def _():
        back_ref[...] += back


def output_layer(pair, hidden, hidden_far, weight, x_all, mask, indicator, bias, inv_count):
    units, cells = hidden.shape
    wide, pairs, block_units, genes = weight.shape
    labels = mask.shape[1]
    return pl.pallas_call(
        functools.partial(output_kernel, inv_count=inv_count),
        grid_spec=pltpu.PrefetchScalarGridSpec(
            num_scalar_prefetch=1,
            grid=(pairs,),
            in_specs=[
                pl.BlockSpec((units, cells), lambda r, me: (0, 0)),
                pl.BlockSpec((wide, 1, block_units, genes), lambda r, me: (0, me[0] ^ r, 0, 0)),
                pl.BlockSpec((1, genes, cells), lambda r, me: (me[0] ^ r, 0, 0)),
                pl.BlockSpec((1, labels, genes), lambda r, me: (me[0] ^ r, 0, 0)),
                pl.BlockSpec((labels, cells), lambda r, me: (0, 0)),
                pl.BlockSpec((1, genes, 1), lambda r, me: (me[0] ^ r, 0, 0)),
                pl.BlockSpec((units, cells), lambda r, me: (0, 0)),
            ],
            out_specs=[
                pl.BlockSpec((units, cells), lambda r, me: (0, 0)),
                pl.BlockSpec((1, genes, cells), lambda r, me: (r, 0, 0)),
                pl.BlockSpec((1, 8, genes), lambda r, me: (me[0] ^ r, 0, 0)),
                pl.BlockSpec((1, cells), lambda r, me: (0, 0)),
            ]
            + [pl.BlockSpec((units // ROUNDS, genes), lambda r, me: (0, 0))] * (pairs * ROUNDS),
            scratch_shapes=[
                pltpu.VMEM((genes, cells), F32),
                pltpu.VMEM((genes, cells), F32),
                pltpu.VMEM((genes, cells), BF),
            ],
        ),
        out_shape=[
            jax.ShapeDtypeStruct((units, cells), F32),
            jax.ShapeDtypeStruct((pairs, genes, cells), BF),
            jax.ShapeDtypeStruct((pairs, 8, genes), F32),
            jax.ShapeDtypeStruct((1, cells), F32),
        ]
        + [jax.ShapeDtypeStruct((units // ROUNDS, genes), BF)] * (pairs * ROUNDS),
        compiler_params=pltpu.CompilerParams(vmem_limit_bytes=48 * 1024 * 1024),
        cost_estimate=pl.CostEstimate(
            flops=6 * units * cells * genes * pairs,
            bytes_accessed=8 * units * genes * pairs,
            transcendentals=3 * cells * genes * pairs,
        ),
        name="output_layer",
    )(pair[None], hidden, weight, x_all, mask, indicator, bias, hidden_far)


def on_device(
    expression,
    noise,
    study,
    measured_gene_mask,
    encoder_input_weight,
    enc_mid,
    heads,
    dec_in,
    dec_mid,
    dec_out,
    norm_params,
    head_bias,
    out_bias,
    running_stats,
):
    wide_count = lax.axis_size("wide")
    row_split = lax.axis_size(("pair", "chip"))
    pair_count = lax.axis_size("pair")
    cells, genes = expression.shape
    count_all = cells * lax.axis_size(ALL)
    inv_count = 1.0 / count_all
    latent = dec_in.shape[0]
    block_genes, block_units = encoder_input_weight.shape
    units = block_units * wide_count
    pair = lax.axis_index("pair")
    chip = lax.axis_index("chip")
    block_id = pair * 2 + chip

    piece = -(-latent // row_split)
    piece_start = jnp.minimum(piece * block_id, latent - piece)
    dec_in_piece = lax.dynamic_slice_in_dim(dec_in, piece_start, piece, 0)
    packed = jnp.concatenate(
        [enc_mid.T, dec_mid.T, heads.T, dec_in_piece.T, norm_params.T], axis=1
    )
    packed = jnp.pad(packed, ((0, 0), (0, 256 - packed.shape[1])))
    mid_rows = enc_mid.shape[0]
    head_rows = heads.shape[0]
    widths = (mid_rows, mid_rows, head_rows, piece, norm_params.shape[0])
    totals = (units, units, 2 * latent, latent, 8)
    padded = -(-block_genes // 128) * 128
    extra = padded - block_genes
    def own_blocks(rows, axis):
        shape = rows.shape[:axis] + (pair_count, 2, block_genes) + rows.shape[axis + 1 :]
        cut = lax.dynamic_index_in_dim(rows.reshape(shape), chip, axis + 1, keepdims=False)
        widths = [(0, 0)] * cut.ndim
        widths[axis + 1] = (0, extra)
        return jnp.pad(cut, widths)

    def prepare():
        by_block = jnp.pad(
            expression.T.reshape(pair_count, 2, block_genes, cells),
            ((0, 0), (0, 0), (0, extra), (0, 0)),
        )
        x_mine = lax.dynamic_index_in_dim(by_block, chip, 1, keepdims=False)
        x_send = lax.dynamic_index_in_dim(by_block, 1 - chip, 1, keepdims=False)
        whole = jnp.concatenate([x_mine, swap_chip(x_send)], axis=2)
        rel = [
            lax.dynamic_index_in_dim(whole, pair ^ r, 0, keepdims=False) for r in range(pair_count)
        ]
        labels = measured_gene_mask.shape[0]
        indicator = (jnp.arange(labels, dtype=jnp.int32)[:, None] == study[None, :]).astype(BF)
        indicator = jnp.concatenate([indicator, swap_chip(indicator)], axis=1)
        mask_all = own_blocks(measured_gene_mask.astype(BF), 1).transpose(1, 0, 2)
        bias_all = own_blocks(out_bias, 0)[:, :, None]
        return (rel, whole), (indicator, mask_all, bias_all)

    enc_block = jnp.pad(encoder_input_weight.T, ((0, 0), (0, extra)))
    dec_block = jnp.pad(dec_out.T, ((0, 0), (0, extra)))
    mine = lax.all_gather(packed, ("wide", "pair"))
    enc_blocks, rel_pre, dec_line, x_rel, early = gather_ring(enc_block, prepare, dec_block)
    x_all, indicator, mask_all, bias_all = early
    w_enc_mid, w_dec_mid, w_heads, w_dec_in, norm_full = unpack_small(
        mine, swap_chip(mine), widths, totals
    )
    norm_full = norm_full.astype(F32)
    gains = [norm_full[:, k] for k in range(4)]
    shifts = [norm_full[:, 4 + k] for k in range(4)]
    part_one = jnp.concatenate(rel_pre, axis=0)
    pre_one = part_one[:, :cells] + swap_chip(part_one[:, cells:])
    pre_one = jnp.concatenate(mirror(pre_one), axis=0)
    dec_all = lax.all_gather(
        gate((dec_line, mine))[0].reshape(wide_count, block_units, padded), "pair", axis=1
    )
    normed_one, scaled_one, inverse_one, centre_one, spread_one, _ = normalize(
        pre_one, gains[0], shifts[0]
    )
    hidden_one = jax.nn.silu(normed_one).astype(BF)

    pre_two = nn(w_enc_mid, hidden_one)
    normed_two, scaled_two, inverse_two, centre_two, spread_two, _ = normalize(
        pre_two, gains[1], shifts[1]
    )
    hidden_two = jax.nn.silu(normed_two).astype(BF)
    encoded = tn(w_heads, hidden_two) + head_bias[:, None]
    latent_mean = encoded[:latent]
    logvar = encoded[latent:]
    noise_t = noise.T
    spread_factor = jnp.exp(0.5 * logvar)
    code = (latent_mean + spread_factor * noise_t).astype(BF)
    pre_three = nn(w_dec_in, code)
    normed_three, scaled_three, inverse_three, centre_three, spread_three, _ = normalize(
        pre_three, gains[2], shifts[2]
    )
    hidden_three = jax.nn.silu(normed_three).astype(BF)
    pre_four = nn(w_dec_mid, hidden_three)
    normed_four, scaled_four, inverse_four, centre_four, spread_four, _ = normalize(
        pre_four, gains[3], shifts[3]
    )
    hidden_four = jax.nn.silu(normed_four).astype(BF)

    h_chip = jnp.concatenate([hidden_four, swap_chip(hidden_four)], axis=1)
    x_near = [swap_pair(x_rel[r], r) for r in range(1, pair_count - 1)]
    back_all, kept_diff, bias_sums, recon_sums, *dec_parts = output_layer(
        pair.astype(jnp.int32),
        h_chip,
        jnp.concatenate(far_first(h_chip)),
        dec_all,
        x_all,
        mask_all,
        indicator,
        bias_all,
        inv_count,
    )
    back_all, x_near = gate((back_all, x_near))
    exp_logvar = jnp.exp(logvar)
    kl_sum = jnp.sum(exp_logvar + latent_mean * latent_mean - 1.0 - logvar)
    loss_local = 0.5 * jnp.sum(recon_sums) + (0.5 * ALPHA) * kl_sum
    back_four = back_all[:, :cells] + swap_chip(back_all[:, cells:])

    bias_rows = jnp.zeros((pair_count, 2, block_genes), F32)
    bias_rows = lax.dynamic_update_slice_in_dim(
        bias_rows, bias_sums[:, :1, :block_genes], chip, 1
    ).reshape(-1)
    devices = lax.axis_size(ALL)
    share_size = -(-genes // (devices * 8)) * 8
    bias_rows = jnp.pad(bias_rows, (0, devices * share_size - genes)).reshape(devices, share_size)
    x_cut = padded // ROUNDS
    dec_sums, dec_line, x_far = [], [], []

    def send(k):
        moved = {
            "g": [swap_pair(dec_parts[r * ROUNDS + k], r) for r in range(1, pair_count)],
            "x": swap_pair(x_rel[3][k * x_cut : (k + 1) * x_cut], 3),
        }
        if k > 0 and wide_count <= LONGEST_RING:
            moved["z"] = next_wide(dec_sums[k - 1].astype(BF), -k)
        return moved

    def receive(k, moved):
        total = dec_parts[k].astype(F32) + sum(item.astype(F32) for item in moved["g"])
        dec_sums.append(total)
        x_far.append(moved["x"])
        if "z" in moved:
            dec_line.append(moved["z"])

    bp_four, gain_four, shift_four, rest, moved = norm_backward(
        back_four,
        normed_four,
        scaled_four,
        inverse_four,
        gains[3],
        loss_local[None],
        bias_rows,
        rider=send(0),
    )
    receive(0, moved)
    loss = jnp.sum(rest[:, 0]) * inv_count
    bias_share = jnp.sum(rest[:, 1:], axis=0)

    back_three = tn(w_dec_mid, bp_four)
    bp_three, gain_three, shift_three, rest, moved = norm_backward(
        back_three, normed_three, scaled_three, inverse_three, gains[2], bias_share, rider=send(1)
    )
    receive(1, moved)
    out_bias_grad = rest.reshape(-1)[:genes]
    back_code = tn(w_dec_in, bp_three)
    back_mean = back_code + ALPHA * inv_count * latent_mean
    back_logvar = (
        back_code * noise_t * spread_factor * 0.5
        + (ALPHA * 0.5 * inv_count) * (exp_logvar - 1.0)
    )
    back_enc = jnp.concatenate([back_mean, back_logvar], axis=0).astype(BF)
    head_sum = jnp.sum(back_enc.astype(F32), axis=1)
    back_two = nn(w_heads, back_enc)
    bp_two, gain_two, shift_two, rest, moved = norm_backward(
        back_two, normed_two, scaled_two, inverse_two, gains[1], head_sum, rider=send(2)
    )
    receive(2, moved)
    head_bias_grad = jnp.sum(rest, axis=0)

    back_one = tn(w_enc_mid, bp_two)
    pad = piece * row_split - latent
    packs = add_chip(
        pack_grads(
            bp_four,
            hidden_three,
            bp_two,
            hidden_one,
            hidden_two,
            back_enc,
            bp_three,
            jnp.pad(code, ((0, pad), (0, 0))),
        )
    )
    packs = [
        lax.dynamic_index_in_dim(packs, pair ^ r, 1, keepdims=False) for r in range(pair_count)
    ]
    bp_one, gain_one, shift_one, _, moved = norm_backward(
        back_one,
        normed_one,
        scaled_one,
        inverse_one,
        gains[0],
        rider=send(3),
    )
    receive(3, moved)
    if wide_count > LONGEST_RING:
        dec_sums = jnp.concatenate(dec_sums)
        dec_sums = [
            dec_sums[k * block_units : (k + 1) * block_units] for k in range(wide_count)
        ]
        dec_out_grad = scatter_wide(dec_sums)
    else:
        dec_out_grad = dec_sums[-1] + sum(item.astype(F32) for item in dec_line)
    x_plane = [x_rel[0]] + x_near + [jnp.concatenate(x_far)]

    d_near = gate([bp_one] + [swap_pair(bp_one, r) for r in range(1, pair_count)])
    d_plane = jnp.stack(d_near)
    d_plane = jnp.concatenate([d_plane, swap_chip(d_plane)], axis=2)
    far_units = [far_first(d_plane[r]) for r in range(pair_count)]
    enc_in_grad = scatter_wide(
        [
            sum(nt(far_units[r][k], x_plane[r]) for r in range(pair_count))
            for k in range(wide_count)
        ]
    )
    late_blocks, kept_diff, packs, d_rel = gate((enc_blocks, kept_diff, packs, far_units[0]))
    packs = add_low(packs[0], *[swap_pair(packs[r], r) for r in range(1, pair_count)])
    mid_sum = scatter_wide(far_first(packs.reshape(units, packs.shape[2])))
    d_rel = jnp.stack(d_rel[-1:] + d_rel[:-1])
    if wide_count > LONGEST_RING:
        late_blocks = [[jnp.concatenate(item) for item in zip(*late_blocks)]]
        d_rel = d_rel.reshape(1, units, 2 * cells)
    own_rows, send_rows = zip(
        *[
            input_rows([row[r] for row in late_blocks], d_rel, kept_diff[r], count_all)
            for r in range(pair_count)
        ]
    )
    own_rows, send_rows = jnp.stack(own_rows), jnp.stack(send_rows)
    input_grad = place_rows(own_rows, swap_chip(send_rows), genes).T
    dec_mid_grad = mid_sum[:, :mid_rows]
    enc_mid_grad = mid_sum[:, mid_rows : 2 * mid_rows]
    in_start = 2 * mid_rows + head_rows
    heads_grad = mid_sum[:, 2 * mid_rows : in_start]
    in_pieces = share(mid_sum[:, in_start : in_start + piece], ("pair", "chip"))
    dec_in_grad = in_pieces.transpose(0, 2, 1).reshape(row_split * piece, block_units)[:latent]
    input_grad, enc_in_grad = gate((input_grad, enc_in_grad))
    enc_in_grad = enc_in_grad[:, :block_genes]

    wide_index = lax.axis_index("wide")
    per_row = 8 // row_split

    def mine_of(rows_full):
        stacked = jnp.stack(rows_full)
        return lax.dynamic_slice(
            stacked, (block_id * per_row, wide_index * block_units), (per_row, block_units)
        )

    norm_grad = mine_of(
        [gain_one, gain_two, gain_three, gain_four, shift_one, shift_two, shift_three, shift_four]
    )
    unbias = count_all / (count_all - 1.0)
    stats = mine_of(
        [
            centre_one,
            centre_two,
            centre_three,
            centre_four,
            spread_one * unbias,
            spread_two * unbias,
            spread_three * unbias,
            spread_four * unbias,
        ]
    )
    running_next = (1.0 - MOMENTUM) * running_stats + MOMENTUM * stats
    return (
        loss,
        input_grad,
        enc_in_grad.T,
        enc_mid_grad.T,
        heads_grad.T,
        dec_in_grad,
        dec_mid_grad.T,
        dec_out_grad[:, :block_genes].T,
        norm_grad,
        head_bias_grad,
        out_bias_grad,
        running_next,
    )


def solution(mesh):
    split = P(("pair", "chip"), "wide")
    by_cell = P(("wide", "pair", "chip"), None)
    return jax.shard_map(
        on_device,
        mesh=mesh,
        in_specs=(
            by_cell,
            by_cell,
            P(("wide", "pair", "chip")),
            P(),
            split,
            split,
            split,
            P(None, "wide"),
            split,
            split,
            split,
            P(),
            P(),
            split,
        ),
        out_specs=(
            P(),
            by_cell,
            split,
            split,
            split,
            P(None, "wide"),
            split,
            split,
            split,
            P(),
            P(),
            split,
        ),
        check_vma=False,
    )
```

```python
import functools

import jax
import jax.numpy as jnp
from jax import lax
from jax.experimental import pallas as pl
from jax.experimental.pallas import tpu as pltpu
from jax.sharding import PartitionSpec as P

ALPHA = 0.005
EPSILON = 1e-05
MOMENTUM = 0.1
LONGEST_RING = 4
ALL = ("wide", "pair", "chip")
BF = jnp.bfloat16
F32 = jnp.float32


def dot(left, right, dims):
    return lax.dot_general(left, right, (dims, ((), ())), preferred_element_type=F32)


def nn(left, right):
    return dot(left, right, ((1,), (0,)))


def nt(left, right):
    return dot(left, right, ((1,), (1,)))


def tn(left, right):
    return dot(left, right, ((0,), (0,)))


def swap_pair(value, bits):
    count = lax.axis_size("pair")
    return lax.ppermute(value, "pair", [(i, i ^ bits) for i in range(count)])


def swap_chip(value):
    return lax.ppermute(value, "chip", [(0, 1), (1, 0)])


def next_wide(value, hops=1):
    count = lax.axis_size("wide")
    return lax.ppermute(value, "wide", [(i, (i + hops) % count) for i in range(count)])


def half_of(units):
    return max(units // 2 // 8 * 8, 1)


def gate(value):
    return lax.optimization_barrier(value)


def spread_pair(block):
    cut = half_of(block.shape[0])
    by_x = swap_pair(block, 1)
    by_y = swap_pair(block, 2)
    upper = swap_pair(by_y[:cut], 1)
    lower = swap_pair(by_x[cut:], 2)
    return [block, by_x, by_y, jnp.concatenate([upper, lower], axis=0)]


def product_kernel(pair_ref, x_ref, own_ref, by_x_ref, by_y_ref, *refs):
    pair = pair_ref[0]
    diag_refs, out_ref = refs[:-1], refs[-1]
    out = nn(own_ref[...], x_ref[pair]) + nn(by_x_ref[...], x_ref[pair ^ 1])
    out = out + nn(by_y_ref[...], x_ref[pair ^ 2])
    start = 0
    for ref in diag_refs:
        stop = start + ref.shape[0]
        out_ref[start:stop, :] = out[start:stop] + nn(ref[...], x_ref[pair ^ 3])
        start = stop


def block_product(row, x_all):
    vmem = pl.BlockSpec(memory_space=pltpu.VMEM)
    pair = lax.axis_index("pair").astype(jnp.int32)[None]
    return pl.pallas_call(
        product_kernel,
        in_specs=[pl.BlockSpec(memory_space=pltpu.SMEM)] + [vmem] * (len(row) + 1),
        out_specs=vmem,
        out_shape=jax.ShapeDtypeStruct((row[0].shape[0], x_all.shape[2]), F32),
        compiler_params=pltpu.CompilerParams(vmem_limit_bytes=32 * 1024 * 1024),
        name="block_product",
    )(pair, x_all, *row)


def gather_ring(block, prepare, second):
    count = lax.axis_size("wide")
    if count > LONGEST_RING:
        line = lax.all_gather(block, "wide", axis=0, tiled=True)
        spread = [jnp.split(item, count) for item in spread_pair(jnp.concatenate(mirror(line)))]
        blocks = list(zip(*spread))
        x_all = jnp.concatenate(prepare(), axis=2)
        products = [block_product(row, x_all) for row in blocks]
        return blocks, products, mirror(lax.all_gather(second, "wide", axis=0, tiled=True)), x_all
    cut = half_of(block.shape[0])
    ring, by_x, by_y, upper, lower, products = [block], [], [], [], [], []
    halves = prepare()
    for step in range(count + 1):
        moved = {}
        if step < count:
            moved["x"] = swap_pair(ring[step], 1)
            moved["y"] = swap_pair(ring[step], 2)
        if step < count - 1:
            moved["z"] = next_wide(ring[step])
        if step > 0:
            moved["u"] = swap_pair(by_y[step - 1][:cut], 1)
            moved["l"] = swap_pair(by_x[step - 1][cut:], 2)
        if step == 0:
            moved["h"] = halves
        if step == count - 2:
            moved["s"] = second
        if step == count:
            moved["d"] = [next_wide(second, hops) for hops in range(2, count, 2)]
        if step == 2:
            moved["a"] = jnp.concatenate(halves, axis=2)
        if step > 2:
            done = step - 3
            row = (ring[done], by_x[done], by_y[done], upper[done], lower[done])
            moved["p"] = block_product(row, x_all)
        moved = gate(moved)
        if "z" in moved:
            ring.append(moved["z"])
        if "x" in moved:
            by_x.append(moved["x"])
            by_y.append(moved["y"])
        if "u" in moved:
            upper.append(moved["u"])
            lower.append(moved["l"])
        second = moved.get("s", second)
        halves = moved.get("h", halves)
        x_all = moved.get("a", None) if step <= 2 else x_all
        if "p" in moved:
            products.append(moved["p"])
    blocks = list(zip(ring, by_x, by_y, upper, lower))
    products += [block_product(row, x_all) for row in blocks[len(products) :]]
    line = [second] * count
    line[2::2] = moved["d"]
    line[1::2] = [next_wide(second, hops) for hops in range(1, count, 2)]
    return blocks, products, line, x_all


def split_kernel(chip_ref, cells_ref, mine_ref, other_ref):
    blocks = 2 * mine_ref.shape[0]
    total = cells_ref.shape[0]
    rows = total // blocks
    chip = chip_ref[0]
    tail = jnp.zeros((mine_ref.shape[1] - rows, cells_ref.shape[1]), F32)
    for block in range(blocks):
        start = block * rows
        first = start // 16 * 16
        last = min(-(-(start + rows) // 16) * 16, total)
        window = cells_ref[first:last, :].astype(F32)
        piece = window[start - first : start - first + rows]
        piece = jnp.concatenate([piece, tail], axis=0).astype(BF)

        @pl.when(chip == block % 2)
        def _():
            mine_ref[block // 2] = piece

        @pl.when(chip != block % 2)
        def _():
            other_ref[block // 2] = piece


def split_cells(cells_t, pairs, padded):
    vmem = pl.BlockSpec(memory_space=pltpu.VMEM)
    shape = jax.ShapeDtypeStruct((pairs, padded, cells_t.shape[1]), BF)
    return pl.pallas_call(
        split_kernel,
        in_specs=[pl.BlockSpec(memory_space=pltpu.SMEM), vmem],
        out_specs=[vmem, vmem],
        out_shape=[shape, shape],
        compiler_params=pltpu.CompilerParams(vmem_limit_bytes=40 * 1024 * 1024),
        name="split_cells",
    )(lax.axis_index("chip").astype(jnp.int32)[None], cells_t)


def unpack_kernel(where_ref, mine_ref, other_ref, *outs, starts, places):
    chip = where_ref[0]
    count, pairs = mine_ref.shape[:2]
    for w in range(count):
        for p in range(pairs):

            def put(ref, c):
                for out, start, place in zip(outs, starts, places):
                    at, width = place[2 * p + c]
                    out[w, :, at : at + width] = ref[w, p, :, start : start + width]

            for c in range(2):

                @pl.when(chip == c)
                def _():
                    put(mine_ref, c)
                    put(other_ref, 1 - c)


def unpack_small(mine, other, widths, totals):
    count, pairs = lax.axis_size("wide"), lax.axis_size("pair")
    shape = (count, pairs) + mine.shape[1:]
    where = lax.axis_index("chip").astype(jnp.int32)[None]
    starts = [sum(widths[:i]) for i in range(len(widths))]
    places = [
        [(min(block * width, total - width), width) for block in range(2 * pairs)]
        for width, total in zip(widths, totals)
    ]
    vmem = pl.BlockSpec(memory_space=pltpu.VMEM)
    outs = pl.pallas_call(
        functools.partial(unpack_kernel, starts=starts, places=places),
        in_specs=[pl.BlockSpec(memory_space=pltpu.SMEM), vmem, vmem],
        out_specs=[vmem] * len(widths),
        out_shape=[jax.ShapeDtypeStruct((count, shape[2], total), BF) for total in totals],
        compiler_params=pltpu.CompilerParams(vmem_limit_bytes=32 * 1024 * 1024),
        name="unpack_small",
    )(where, mine.reshape(shape), other.reshape(shape))
    return [item.reshape(count * shape[2], -1) for item in outs]


def send_odd(blocks):
    count = lax.axis_size("wide")
    if count > LONGEST_RING:
        order = jnp.stack(list(blocks)[-1:] + list(blocks)[:-1])
        line = jnp.stack(mirror(order.reshape((-1,) + order.shape[2:])))
        return [gate(lax.psum_scatter(line, "wide", scatter_dimension=0, tiled=True))[0]]
    return [next_wide(blocks[k - 1].astype(BF), -k) for k in range(1, count, 2)]


def send_even(blocks):
    count = lax.axis_size("wide")
    if count > LONGEST_RING:
        return []
    return [next_wide(blocks[k - 1].astype(BF), -k) for k in range(2, count, 2)]


def add_wide(blocks, odd, even):
    terms = list(odd) + list(even)
    if lax.axis_size("wide") <= LONGEST_RING:
        terms = list(blocks)[-1:] + terms
    return sum(item.astype(F32) for item in terms)


def scatter_wide(blocks, beside=None):
    odd, even = send_odd(blocks), send_even(blocks)
    if beside is not None:
        odd, beside = gate((odd, beside))
    return add_wide(blocks, odd, even), beside


def add_low(*terms):
    return sum(item.astype(F32) for item in terms).astype(BF)


def far_first(value):
    blocks = mirror(value)
    return blocks[1:] + blocks[:1]


def mirror(value):
    count = lax.axis_size("wide")
    me = lax.axis_index("wide")
    shaped = value.reshape((count, value.shape[0] // count) + value.shape[1:])
    return [
        lax.dynamic_index_in_dim(shaped, lax.rem(me - s + count, count), 0, keepdims=False)
        for s in range(count)
    ]


def share(value, axes=ALL):
    count = lax.axis_size(axes)
    return lax.all_to_all(
        jnp.broadcast_to(value[None], (count,) + value.shape), axes, 0, 0, tiled=True
    )


def pack_kernel(*refs):
    out_ref = refs[-1]
    chips, wide, pairs, units, _ = out_ref.shape
    start = 0
    for left_ref, right_ref in zip(refs[:-1:2], refs[1:-1:2]):
        rows = right_ref.shape[0] // (pairs * chips)
        product = nt(left_ref[...], right_ref[...])
        for w in range(wide):
            for p in range(pairs):
                for c in range(chips):
                    at = (p * chips + c) * rows
                    piece = product[w * units : (w + 1) * units, at : at + rows]
                    out_ref[c, w, p, :, start : start + rows] = piece.astype(BF)
        start += rows
    out_ref[:, :, :, :, start:] = jnp.zeros(out_ref.shape[:4] + (out_ref.shape[4] - start,), BF)


def pack_grads(*operands):
    wide, pairs = lax.axis_size("wide"), lax.axis_size("pair")
    shape = (2, wide, pairs, operands[0].shape[0] // wide, 256)
    return pl.pallas_call(
        pack_kernel,
        out_shape=jax.ShapeDtypeStruct(shape, BF),
        compiler_params=pltpu.CompilerParams(vmem_limit_bytes=40 * 1024 * 1024),
        name="pack_grads",
    )(*operands)


def add_chip(blocks):
    chip = lax.axis_index("chip")
    keep = lax.dynamic_index_in_dim(blocks, chip, 0, keepdims=False)
    send = lax.dynamic_index_in_dim(blocks, 1 - chip, 0, keepdims=False)
    return add_low(keep, swap_chip(send))


def input_kernel(*refs, scale):
    weights, (d_ref, kept_ref, own_ref, send_ref) = refs[:-4], refs[-4:]
    cells = own_ref.shape[1]
    grad, s, start = 0.0, 0, 0
    for weight in weights:
        rows = weight.shape[0]
        grad = grad + tn(weight[...], d_ref[s][start : start + rows])
        start += rows
        if start == d_ref.shape[1]:
            s, start = s + 1, 0
    grad = grad * scale - kept_ref[0].astype(F32)
    own_ref[...] = grad[:, :cells].astype(BF)
    send_ref[...] = grad[:, cells:].astype(BF)


def input_rows(weights, d_rel, kept, rel, scale):
    _, genes, cells = kept.shape
    half = jax.ShapeDtypeStruct((genes, cells // 2), BF)

    def whole(item):
        return pl.BlockSpec(item.shape, lambda i: (0,) * item.ndim)

    return pl.pallas_call(
        functools.partial(input_kernel, scale=scale),
        grid=(1,),
        in_specs=[whole(item) for item in weights]
        + [whole(d_rel), pl.BlockSpec((1, genes, cells), lambda i: (rel, 0, 0))],
        out_specs=[whole(half)] * 2,
        out_shape=[half, half],
        compiler_params=pltpu.CompilerParams(vmem_limit_bytes=32 * 1024 * 1024),
        name="input_rows",
    )(*weights, d_rel, kept)


def plane_kernel(wide_ref, plane_ref, swap_ref, *refs):
    pairs = 4
    x_refs, outs = refs[:pairs], refs[pairs:]
    count = plane_ref.shape[0]
    cells = plane_ref.shape[2] // pairs
    for k, out in enumerate(outs, 1):
        w = lax.rem(wide_ref[0] + count - k, count)
        total = 0.0
        for r, x_ref in enumerate(x_refs):
            at = slice(r * cells, (r + 1) * cells)
            total = total + nt(plane_ref[w, :, at], x_ref[:, :cells])
            total = total + nt(swap_ref[w, :, at], x_ref[:, cells:])
        out[...] = total.astype(BF)


def plane_grads(plane, swapped, x_plane):
    count = lax.axis_size("wide")
    shape = (count, plane.shape[0] // count, plane.shape[1])
    vmem = pl.BlockSpec(memory_space=pltpu.VMEM)
    where = lax.axis_index("wide").astype(jnp.int32)[None]
    return pl.pallas_call(
        plane_kernel,
        in_specs=[pl.BlockSpec(memory_space=pltpu.SMEM)] + [vmem] * (2 + len(x_plane)),
        out_specs=[vmem] * count,
        out_shape=[jax.ShapeDtypeStruct((shape[1], x_plane[0].shape[0]), BF)] * count,
        compiler_params=pltpu.CompilerParams(vmem_limit_bytes=48 * 1024 * 1024),
        name="plane_grads",
    )(where, plane.reshape(shape), swapped.reshape(shape), *x_plane)


def place_kernel(where_ref, own_ref, came_ref, out_ref):
    pair, chip = where_ref[0], where_ref[1]
    pairs = own_ref.shape[0]
    rows = out_ref.shape[0] // (2 * pairs)
    for p in range(pairs):
        rel = pair ^ p
        for c in range(2):
            at = pl.ds((2 * p + c) * rows, rows)

            @pl.when(chip == c)
            def _():
                out_ref[at, :] = own_ref[rel, :rows, :].astype(F32)

            @pl.when(chip != c)
            def _():
                out_ref[at, :] = came_ref[rel, :rows, :].astype(F32)


def place_rows(own, came, genes):
    where = jnp.stack([lax.axis_index("pair"), lax.axis_index("chip")]).astype(jnp.int32)
    return pl.pallas_call(
        place_kernel,
        in_specs=[
            pl.BlockSpec(memory_space=pltpu.SMEM),
            pl.BlockSpec(memory_space=pltpu.VMEM),
            pl.BlockSpec(memory_space=pltpu.VMEM),
        ],
        out_specs=pl.BlockSpec(memory_space=pltpu.VMEM),
        out_shape=jax.ShapeDtypeStruct((genes, own.shape[2]), F32),
        compiler_params=pltpu.CompilerParams(vmem_limit_bytes=40 * 1024 * 1024),
        name="place_rows",
    )(where, own, came)


def normalize(pre_act, gain, shift, rider=()):
    cells = pre_act.shape[1]
    count = lax.axis_size(ALL)
    local_mean = jnp.mean(pre_act, axis=1)
    local_square = jnp.sum(jnp.square(pre_act - local_mean[:, None]), axis=1)
    every, rider = gate((share(jnp.stack([local_mean, local_square])), rider))
    centre = jnp.mean(every[:, 0], axis=0)
    squares = jnp.sum(every[:, 1], axis=0) + cells * jnp.sum(
        jnp.square(every[:, 0] - centre), axis=0
    )
    variance = squares / (cells * count)
    inverse = lax.rsqrt(variance + EPSILON)
    scaled = (pre_act - centre[:, None]) * inverse[:, None]
    normed = None if gain is None else scaled * gain[:, None] + shift[:, None]
    return normed, scaled, inverse, centre, variance, rider


def norm_backward(upstream, normed, scaled, inverse, gain, extra=None, pieces=None, rider=()):
    count = lax.axis_size(ALL)
    units, cells = upstream.shape
    count_all = cells * count
    gate_value = jax.nn.sigmoid(normed)
    back_normed = upstream * gate_value * (1.0 + normed * (1.0 - gate_value))
    sums = [jnp.sum(back_normed, axis=1), jnp.sum(back_normed * scaled, axis=1)]
    if extra is not None:
        sums.append(extra)
    sums = jnp.concatenate(sums)
    sent = jnp.broadcast_to(sums[None], (count,) + sums.shape)
    if pieces is not None:
        sent = jnp.concatenate([sent, pieces], axis=1)
    every, rider = gate((lax.all_to_all(sent, ALL, 0, 0, tiled=True), rider))
    both = jnp.sum(every[:, : 2 * units], axis=0)
    shift_sum, gain_sum = both[:units], both[units:]
    back_pre = (gain * inverse)[:, None] * (
        back_normed - (shift_sum / count_all)[:, None] - scaled * (gain_sum / count_all)[:, None]
    )
    return back_pre.astype(BF), gain_sum, shift_sum, every[:, 2 * units :], rider


def output_kernel(
    pair_ref,
    h_ref,
    weight_ref,
    x_ref,
    mask_ref,
    indicator_ref,
    bias_ref,
    back_ref,
    kept_ref,
    bias_sum_ref,
    loss_ref,
    *refs,
    inv_count,
):
    grad_ref, out_ref, keep_ref, low_ref = refs
    step = pl.program_id(0)
    units, cells = h_ref.shape
    genes = x_ref.shape[1]
    weight = weight_ref[:, 0].reshape(units, genes)
    out_ref[...] = tn(weight, h_ref[...])
    keep_ref[...] = tn(mask_ref[0], indicator_ref[...])

    @pl.when(step == 0)
    def _():
        loss_ref[...] = jnp.zeros_like(loss_ref)

    rows = 64

    def chunk(i, total):
        at = pl.ds(pl.multiple_of(i * rows, rows), rows)
        out_pre = out_ref[at, :] + bias_ref[0, at, :]
        small = jnp.exp(-jnp.abs(out_pre))
        recon = jnp.maximum(out_pre, 0.0) + jnp.log1p(small)
        slope = jnp.where(out_pre >= 0, 1.0, small) / (1.0 + small)
        diff = recon - x_ref[0, at, :].astype(F32)
        kept = keep_ref[at, :] * diff
        low = (kept * slope * inv_count).astype(BF)
        kept_ref[0, at, :] = kept.astype(BF)
        low_ref[at, :] = low
        return total + jnp.sum(kept * diff, axis=0, keepdims=True)

    loss_ref[...] += lax.fori_loop(0, genes // rows, chunk, jnp.zeros((1, cells), F32), unroll=True)
    low = low_ref[...]
    bias_sum_ref[0] = nt(jnp.ones((8, cells), BF), low)
    grad_ref[...] = nt(h_ref[...], low).astype(BF).reshape(grad_ref.shape)
    back = nn(weight, low)

    @pl.when(step == 0)
    def _():
        back_ref[...] = back

    @pl.when(step > 0)
    def _():
        back_ref[...] += back


def output_layer(pair, hidden, weight, x_all, mask, indicator, bias, inv_count):
    units, cells = hidden.shape
    wide, pairs, block_units, genes = weight.shape
    labels = mask.shape[1]
    return pl.pallas_call(
        functools.partial(output_kernel, inv_count=inv_count),
        grid_spec=pltpu.PrefetchScalarGridSpec(
            num_scalar_prefetch=1,
            grid=(pairs,),
            in_specs=[
                pl.BlockSpec((units, cells), lambda r, me: (0, 0)),
                pl.BlockSpec((wide, 1, block_units, genes), lambda r, me: (0, me[0] ^ r, 0, 0)),
                pl.BlockSpec((1, genes, cells), lambda r, me: (me[0] ^ r, 0, 0)),
                pl.BlockSpec((1, labels, genes), lambda r, me: (me[0] ^ r, 0, 0)),
                pl.BlockSpec((labels, cells), lambda r, me: (0, 0)),
                pl.BlockSpec((1, genes, 1), lambda r, me: (me[0] ^ r, 0, 0)),
            ],
            out_specs=[
                pl.BlockSpec((units, cells), lambda r, me: (0, 0)),
                pl.BlockSpec((1, genes, cells), lambda r, me: (r, 0, 0)),
                pl.BlockSpec((1, 8, genes), lambda r, me: (me[0] ^ r, 0, 0)),
                pl.BlockSpec((1, cells), lambda r, me: (0, 0)),
                pl.BlockSpec((1, wide, block_units, genes), lambda r, me: (me[0] ^ r, 0, 0, 0)),
            ],
            scratch_shapes=[
                pltpu.VMEM((genes, cells), F32),
                pltpu.VMEM((genes, cells), F32),
                pltpu.VMEM((genes, cells), BF),
            ],
        ),
        out_shape=[
            jax.ShapeDtypeStruct((units, cells), F32),
            jax.ShapeDtypeStruct((pairs, genes, cells), BF),
            jax.ShapeDtypeStruct((pairs, 8, genes), F32),
            jax.ShapeDtypeStruct((1, cells), F32),
            jax.ShapeDtypeStruct((pairs, wide, block_units, genes), BF),
        ],
        compiler_params=pltpu.CompilerParams(vmem_limit_bytes=48 * 1024 * 1024),
        cost_estimate=pl.CostEstimate(
            flops=36 * units * cells * genes * pairs,
            bytes_accessed=48 * units * genes * pairs,
            transcendentals=3 * cells * genes * pairs,
        ),
        name="output_layer",
    )(pair[None], hidden, weight, x_all, mask, indicator, bias)


def on_device(
    expression,
    noise,
    study,
    measured_gene_mask,
    encoder_input_weight,
    enc_mid,
    heads,
    dec_in,
    dec_mid,
    dec_out,
    norm_params,
    head_bias,
    out_bias,
    running_stats,
):
    wide_count = lax.axis_size("wide")
    row_split = lax.axis_size(("pair", "chip"))
    pair_count = lax.axis_size("pair")
    cells, genes = expression.shape
    count_all = cells * lax.axis_size(ALL)
    inv_count = 1.0 / count_all
    latent = dec_in.shape[0]
    block_genes, block_units = encoder_input_weight.shape
    units = block_units * wide_count
    pair = lax.axis_index("pair")
    chip = lax.axis_index("chip")
    block_id = pair * 2 + chip

    piece = -(-latent // row_split)
    piece_start = jnp.minimum(piece * block_id, latent - piece)
    dec_in_piece = lax.dynamic_slice_in_dim(dec_in, piece_start, piece, 0)
    packed = jnp.concatenate(
        [enc_mid.T, dec_mid.T, heads.T, dec_in_piece.T, norm_params.T], axis=1
    )
    packed = jnp.pad(packed, ((0, 0), (0, 256 - packed.shape[1])))
    mid_rows = enc_mid.shape[0]
    head_rows = heads.shape[0]
    widths = (mid_rows, mid_rows, head_rows, piece, norm_params.shape[0])
    totals = (units, units, 2 * latent, latent, 8)
    padded = -(-block_genes // 128) * 128
    extra = padded - block_genes
    def own_blocks(rows, axis):
        shape = rows.shape[:axis] + (pair_count, 2, block_genes) + rows.shape[axis + 1 :]
        cut = lax.dynamic_index_in_dim(rows.reshape(shape), chip, axis + 1, keepdims=False)
        widths = [(0, 0)] * cut.ndim
        widths[axis + 1] = (0, extra)
        return jnp.pad(cut, widths)

    def prepare():
        x_mine, x_send = split_cells(expression.T, pair_count, padded)
        return x_mine, swap_chip(x_send)

    labels = measured_gene_mask.shape[0]
    indicator = (jnp.arange(labels, dtype=jnp.int32)[:, None] == study[None, :]).astype(BF)
    indicator = jnp.concatenate([indicator, swap_chip(indicator)], axis=1)
    mask_all = own_blocks(measured_gene_mask.astype(BF), 1).transpose(1, 0, 2)
    bias_all = own_blocks(out_bias, 0)[:, :, None]

    enc_block = jnp.pad(encoder_input_weight.T, ((0, 0), (0, extra)))
    dec_block = jnp.pad(dec_out.T, ((0, 0), (0, extra)))
    mine = lax.all_gather(packed, ("wide", "pair"))
    enc_blocks, rel_pre, dec_line, x_all = gather_ring(enc_block, prepare, dec_block)
    mids = unpack_small(mine, swap_chip(mine), widths, totals)
    part_one = jnp.concatenate(rel_pre, axis=0)
    x_rel = [
        lax.dynamic_index_in_dim(x_all, pair ^ r, 0, keepdims=False) for r in range(pair_count)
    ]
    x_near = [swap_pair(x_rel[r], r) for r in range(1, pair_count - 1)]
    pre_other, dec_line, x_near = gate((swap_chip(part_one[:, cells:]), dec_line, x_near))
    pre_one = jnp.concatenate(mirror(part_one[:, :cells] + pre_other), axis=0)
    dec_line = jnp.concatenate(mirror(jnp.concatenate(dec_line)))
    dec_all = lax.all_gather(
        dec_line.reshape(wide_count, block_units, padded), "pair", axis=1
    )
    normed_one, scaled_one, inverse_one, centre_one, spread_one, mids = normalize(
        pre_one, None, None, mids
    )
    w_enc_mid, w_dec_mid, w_heads, w_dec_in, norm_full = mids
    norm_full = norm_full.astype(F32)
    gains = [norm_full[:, k] for k in range(4)]
    shifts = [norm_full[:, 4 + k] for k in range(4)]
    normed_one = scaled_one * gains[0][:, None] + shifts[0][:, None]
    hidden_one = jax.nn.silu(normed_one).astype(BF)

    pre_two = nn(w_enc_mid, hidden_one)
    normed_two, scaled_two, inverse_two, centre_two, spread_two, _ = normalize(
        pre_two, gains[1], shifts[1]
    )
    hidden_two = jax.nn.silu(normed_two).astype(BF)
    encoded = tn(w_heads, hidden_two) + head_bias[:, None]
    latent_mean = encoded[:latent]
    logvar = encoded[latent:]
    noise_t = noise.T
    spread_factor = jnp.exp(0.5 * logvar)
    code = (latent_mean + spread_factor * noise_t).astype(BF)
    pre_three = nn(w_dec_in, code)
    normed_three, scaled_three, inverse_three, centre_three, spread_three, _ = normalize(
        pre_three, gains[2], shifts[2]
    )
    hidden_three = jax.nn.silu(normed_three).astype(BF)
    pre_four = nn(w_dec_mid, hidden_three)
    normed_four, scaled_four, inverse_four, centre_four, spread_four, _ = normalize(
        pre_four, gains[3], shifts[3]
    )
    hidden_four = jax.nn.silu(normed_four).astype(BF)

    h_chip = jnp.concatenate([hidden_four, swap_chip(hidden_four)], axis=1)
    back_all, kept_diff, bias_sums, recon_sums, dec_parts = output_layer(
        pair.astype(jnp.int32),
        h_chip,
        dec_all,
        x_all,
        mask_all,
        indicator,
        bias_all,
        inv_count,
    )
    exp_logvar = jnp.exp(logvar)
    kl_sum = jnp.sum(exp_logvar + latent_mean * latent_mean - 1.0 - logvar)
    loss_local = 0.5 * jnp.sum(recon_sums) + (0.5 * ALPHA) * kl_sum
    back_four = back_all[:, :cells] + swap_chip(back_all[:, cells:])

    bias_rows = jnp.zeros((pair_count, 2, block_genes), F32)
    bias_rows = lax.dynamic_update_slice_in_dim(
        bias_rows, bias_sums[:, :1, :block_genes], chip, 1
    ).reshape(-1)
    devices = lax.axis_size(ALL)
    share_size = -(-genes // (devices * 8)) * 8
    bias_rows = jnp.pad(bias_rows, (0, devices * share_size - genes)).reshape(devices, share_size)
    dec_line = lax.psum_scatter(dec_parts, "pair", scatter_dimension=0, tiled=True)
    bp_four, gain_four, shift_four, rest, _ = norm_backward(
        back_four,
        normed_four,
        scaled_four,
        inverse_four,
        gains[3],
        loss_local[None],
        bias_rows,
    )
    loss = jnp.sum(rest[:, 0]) * inv_count
    bias_share = jnp.sum(rest[:, 1:], axis=0)

    back_three = tn(w_dec_mid, bp_four)
    bp_three, gain_three, shift_three, rest, x_far = norm_backward(
        back_three, normed_three, scaled_three, inverse_three, gains[2], bias_share, rider=swap_pair(x_rel[3][: padded // 2], 3)
    )
    out_bias_grad = rest.reshape(-1)[:genes]
    back_code = tn(w_dec_in, bp_three)
    back_mean = back_code + ALPHA * inv_count * latent_mean
    back_logvar = (
        back_code * noise_t * spread_factor * 0.5
        + (ALPHA * 0.5 * inv_count) * (exp_logvar - 1.0)
    )
    back_enc = jnp.concatenate([back_mean, back_logvar], axis=0).astype(BF)
    head_sum = jnp.sum(back_enc.astype(F32), axis=1)
    back_two = nn(w_heads, back_enc)
    bp_two, gain_two, shift_two, rest, x_last = norm_backward(
        back_two, normed_two, scaled_two, inverse_two, gains[1], head_sum, rider=swap_pair(x_rel[3][padded // 2 :], 3)
    )
    head_bias_grad = jnp.sum(rest, axis=0)

    back_one = tn(w_enc_mid, bp_two)
    pad = piece * row_split - latent
    packs = add_chip(
        pack_grads(
            bp_four,
            hidden_three,
            bp_two,
            hidden_one,
            hidden_two,
            back_enc,
            bp_three,
            jnp.pad(code, ((0, pad), (0, 0))),
        )
    )
    bp_one, gain_one, shift_one, _, (dec_line, packs) = norm_backward(
        back_one, normed_one, scaled_one, inverse_one, gains[0], rider=(dec_line, packs)
    )

    dec_blocks = far_first(dec_line.reshape(units, padded))
    d_near, dec_blocks, packs, dec_near = gate(
        (
            [bp_one] + [swap_pair(bp_one, r) for r in range(1, pair_count)],
            dec_blocks,
            packs,
            send_odd(dec_blocks),
        )
    )
    dec_far = send_even(dec_blocks)
    d_plane = jnp.concatenate(d_near, axis=1)
    d_swap = swap_chip(d_plane)
    enc_low = plane_grads(
        d_plane, d_swap, [x_rel[0]] + x_near + [jnp.concatenate([x_far, x_last])]
    )
    packs = [
        lax.dynamic_index_in_dim(packs, pair ^ r, 1, keepdims=False) for r in range(pair_count)
    ]
    packs = [packs[0]] + [swap_pair(packs[r], r) for r in range(1, pair_count)]
    late_rows = [gain_one, gain_two, gain_three, gain_four]
    late_rows += [shift_one, shift_two, shift_three, shift_four]
    late_rows += [centre_one, centre_two, centre_three, centre_four]
    late_rows += [spread_one, spread_two, spread_three, spread_four]
    d_own = jnp.concatenate([d_plane[:, :cells], d_swap[:, :cells]], axis=1)
    enc_in_grad, (packs, late_rows, late_blocks, d_own, dec_far) = scatter_wide(
        enc_low, (packs, late_rows, enc_blocks, d_own, dec_far)
    )
    dec_out_grad = add_wide(dec_blocks, dec_near, dec_far)
    packs = add_low(*packs).reshape(units, packs[0].shape[2])
    mid_sum, _ = scatter_wide(far_first(packs))
    d_rel = far_first(d_own)
    d_rel = jnp.stack(d_rel[-1:] + d_rel[:-1])
    if wide_count > LONGEST_RING:
        late_blocks = [[jnp.concatenate(item) for item in zip(*late_blocks)]]
        d_rel = d_rel.reshape(1, units, 2 * cells)
    own_rows, send_rows = zip(
        *[
            input_rows(
                [item for row in late_blocks for item in (row[3:] if r == 3 else row[r : r + 1])],
                d_rel,
                kept_diff,
                r,
                count_all,
            )
            for r in range(pair_count)
        ]
    )
    own_rows, send_rows = jnp.stack(own_rows), jnp.stack(send_rows)
    input_grad = place_rows(own_rows, swap_chip(send_rows), genes).T

    wide_index = lax.axis_index("wide")
    per_row = 8 // row_split

    def mine_of(rows_full):
        stacked = jnp.stack(rows_full)
        return lax.dynamic_slice(
            stacked, (block_id * per_row, wide_index * block_units), (per_row, block_units)
        )

    norm_grad = mine_of(late_rows[:8])
    unbias = count_all / (count_all - 1.0)
    stats = mine_of(late_rows[8:12] + [item * unbias for item in late_rows[12:]])
    running_next = (1.0 - MOMENTUM) * running_stats + MOMENTUM * stats

    dec_mid_grad = mid_sum[:, :mid_rows]
    enc_mid_grad = mid_sum[:, mid_rows : 2 * mid_rows]
    in_start = 2 * mid_rows + head_rows
    heads_grad = mid_sum[:, 2 * mid_rows : in_start]
    in_piece, input_grad = gate((mid_sum[:, in_start : in_start + piece], input_grad))
    in_pieces = share(in_piece, ("pair", "chip"))
    dec_in_grad = in_pieces.transpose(0, 2, 1).reshape(row_split * piece, block_units)[:latent]
    enc_in_grad = enc_in_grad[:, :block_genes]


    return (
        loss,
        input_grad,
        enc_in_grad.T,
        enc_mid_grad.T,
        heads_grad.T,
        dec_in_grad,
        dec_mid_grad.T,
        dec_out_grad[:, :block_genes].T,
        norm_grad,
        head_bias_grad,
        out_bias_grad,
        running_next,
    )


def solution(mesh):
    split = P(("pair", "chip"), "wide")
    by_cell = P(("wide", "pair", "chip"), None)
    return jax.shard_map(
        on_device,
        mesh=mesh,
        in_specs=(
            by_cell,
            by_cell,
            P(("wide", "pair", "chip")),
            P(),
            split,
            split,
            split,
            P(None, "wide"),
            split,
            split,
            split,
            P(),
            P(),
            split,
        ),
        out_specs=(
            P(),
            by_cell,
            split,
            split,
            split,
            P(None, "wide"),
            split,
            split,
            split,
            P(),
            P(),
            split,
        ),
        check_vma=False,
    )
```

```python
import functools

import jax
import jax.numpy as jnp
from jax import lax
from jax.experimental import pallas as pl
from jax.experimental.pallas import tpu as pltpu
from jax.sharding import PartitionSpec as P

ALPHA = 0.005
EPSILON = 1e-05
MOMENTUM = 0.1
LONGEST_RING = 4
ALL = ("wide", "pair", "chip")
BF = jnp.bfloat16
F32 = jnp.float32


def dot(left, right, dims):
    return lax.dot_general(left, right, (dims, ((), ())), preferred_element_type=F32)


def nn(left, right):
    return dot(left, right, ((1,), (0,)))


def nt(left, right):
    return dot(left, right, ((1,), (1,)))


def tn(left, right):
    return dot(left, right, ((0,), (0,)))


def swap_pair(value, bits):
    count = lax.axis_size("pair")
    return lax.ppermute(value, "pair", [(i, i ^ bits) for i in range(count)])


def swap_chip(value):
    return lax.ppermute(value, "chip", [(0, 1), (1, 0)])


def next_wide(value, hops=1):
    count = lax.axis_size("wide")
    return lax.ppermute(value, "wide", [(i, (i + hops) % count) for i in range(count)])


def half_of(units):
    return max(units // 2 // 8 * 8, 1)


def gate(value):
    return lax.optimization_barrier(value)


def spread_pair(block):
    cut = half_of(block.shape[0])
    by_x = swap_pair(block, 1)
    by_y = swap_pair(block, 2)
    upper = swap_pair(by_y[:cut], 1)
    lower = swap_pair(by_x[cut:], 2)
    return [block, by_x, by_y, jnp.concatenate([upper, lower], axis=0)]


def product_kernel(pair_ref, x_ref, own_ref, by_x_ref, by_y_ref, *refs):
    pair = pair_ref[0]
    diag_refs, out_ref = refs[:-1], refs[-1]
    out = nn(own_ref[...], x_ref[pair]) + nn(by_x_ref[...], x_ref[pair ^ 1])
    out = out + nn(by_y_ref[...], x_ref[pair ^ 2])
    start = 0
    for ref in diag_refs:
        stop = start + ref.shape[0]
        out_ref[start:stop, :] = out[start:stop] + nn(ref[...], x_ref[pair ^ 3])
        start = stop


def block_product(row, x_all):
    vmem = pl.BlockSpec(memory_space=pltpu.VMEM)
    pair = lax.axis_index("pair").astype(jnp.int32)[None]
    return pl.pallas_call(
        product_kernel,
        in_specs=[pl.BlockSpec(memory_space=pltpu.SMEM)] + [vmem] * (len(row) + 1),
        out_specs=vmem,
        out_shape=jax.ShapeDtypeStruct((row[0].shape[0], x_all.shape[2]), F32),
        compiler_params=pltpu.CompilerParams(vmem_limit_bytes=32 * 1024 * 1024),
        name="block_product",
    )(pair, x_all, *row)


def gather_ring(block, prepare, second):
    count = lax.axis_size("wide")
    if count > LONGEST_RING:
        line = lax.all_gather(block, "wide", axis=0, tiled=True)
        spread = [jnp.split(item, count) for item in spread_pair(jnp.concatenate(mirror(line)))]
        blocks = list(zip(*spread))
        x_all = jnp.concatenate(prepare(), axis=2)
        products = [block_product(row, x_all) for row in blocks]
        line = mirror(lax.all_gather(second, "wide", axis=0, tiled=True))
        return blocks, products, line, x_all
    cut = half_of(block.shape[0])
    ring, by_x, by_y, upper, lower, products = [block], [], [], [], [], []
    halves = prepare()
    for step in range(count + 1):
        moved = {}
        if step < count:
            moved["x"] = swap_pair(ring[step], 1)
            moved["y"] = swap_pair(ring[step], 2)
        if step < count - 1:
            moved["z"] = next_wide(ring[step])
        if step > 0:
            moved["u"] = swap_pair(by_y[step - 1][:cut], 1)
            moved["l"] = swap_pair(by_x[step - 1][cut:], 2)
        if step == 0:
            moved["h"] = halves
        if step == count - 2:
            moved["s"] = second
        if step > 1 and step > count - 2:
            moved["d"] = next_wide(seconds[-1])
        if step == 2:
            moved["a"] = jnp.concatenate(halves, axis=2)
        if step > 2:
            done = step - 3
            row = (ring[done], by_x[done], by_y[done], upper[done], lower[done])
            moved["p"] = block_product(row, x_all)
        moved = gate(moved)
        if "z" in moved:
            ring.append(moved["z"])
        if "x" in moved:
            by_x.append(moved["x"])
            by_y.append(moved["y"])
        if "u" in moved:
            upper.append(moved["u"])
            lower.append(moved["l"])
        if "s" in moved:
            seconds = [moved["s"]]
        if "d" in moved:
            seconds.append(moved["d"])
        halves = moved.get("h", halves)
        x_all = moved.get("a", None) if step <= 2 else x_all
        if "p" in moved:
            products.append(moved["p"])
    blocks = list(zip(ring, by_x, by_y, upper, lower))
    products += [block_product(row, x_all) for row in blocks[len(products) :]]
    while len(seconds) < count:
        seconds.append(next_wide(seconds[-1]))
    return blocks, products, seconds, x_all


def split_kernel(chip_ref, cells_ref, mine_ref, other_ref):
    blocks = 2 * mine_ref.shape[0]
    total = cells_ref.shape[0]
    rows = total // blocks
    chip = chip_ref[0]
    tail = jnp.zeros((mine_ref.shape[1] - rows, cells_ref.shape[1]), F32)
    for block in range(blocks):
        start = block * rows
        first = start // 16 * 16
        last = min(-(-(start + rows) // 16) * 16, total)
        window = cells_ref[first:last, :].astype(F32)
        piece = window[start - first : start - first + rows]
        piece = jnp.concatenate([piece, tail], axis=0).astype(BF)

        @pl.when(chip == block % 2)
        def _():
            mine_ref[block // 2] = piece

        @pl.when(chip != block % 2)
        def _():
            other_ref[block // 2] = piece


def split_cells(cells_t, pairs, padded):
    vmem = pl.BlockSpec(memory_space=pltpu.VMEM)
    shape = jax.ShapeDtypeStruct((pairs, padded, cells_t.shape[1]), BF)
    return pl.pallas_call(
        split_kernel,
        in_specs=[pl.BlockSpec(memory_space=pltpu.SMEM), vmem],
        out_specs=[vmem, vmem],
        out_shape=[shape, shape],
        compiler_params=pltpu.CompilerParams(vmem_limit_bytes=40 * 1024 * 1024),
        name="split_cells",
    )(lax.axis_index("chip").astype(jnp.int32)[None], cells_t)


def unpack_kernel(where_ref, mine_ref, other_ref, *outs, starts, places):
    chip = where_ref[0]
    count, pairs = mine_ref.shape[:2]
    for w in range(count):
        for p in range(pairs):

            def put(ref, c):
                for out, start, place in zip(outs, starts, places):
                    at, width = place[2 * p + c]
                    out[w, :, at : at + width] = ref[w, p, :, start : start + width]

            for c in range(2):

                @pl.when(chip == c)
                def _():
                    put(mine_ref, c)
                    put(other_ref, 1 - c)


def unpack_small(mine, other, widths, totals):
    count, pairs = lax.axis_size("wide"), lax.axis_size("pair")
    shape = (count, pairs) + mine.shape[1:]
    where = lax.axis_index("chip").astype(jnp.int32)[None]
    starts = [sum(widths[:i]) for i in range(len(widths))]
    places = [
        [(min(block * width, total - width), width) for block in range(2 * pairs)]
        for width, total in zip(widths, totals)
    ]
    vmem = pl.BlockSpec(memory_space=pltpu.VMEM)
    outs = pl.pallas_call(
        functools.partial(unpack_kernel, starts=starts, places=places),
        in_specs=[pl.BlockSpec(memory_space=pltpu.SMEM), vmem, vmem],
        out_specs=[vmem] * len(widths),
        out_shape=[jax.ShapeDtypeStruct((count, shape[2], total), BF) for total in totals],
        compiler_params=pltpu.CompilerParams(vmem_limit_bytes=32 * 1024 * 1024),
        name="unpack_small",
    )(where, mine.reshape(shape), other.reshape(shape))
    return [item.reshape(count * shape[2], -1) for item in outs]


def send_odd(blocks):
    count = lax.axis_size("wide")
    if count > LONGEST_RING:
        order = jnp.stack(list(blocks)[-1:] + list(blocks)[:-1])
        line = jnp.stack(mirror(order.reshape((-1,) + order.shape[2:])))
        return [gate(lax.psum_scatter(line, "wide", scatter_dimension=0, tiled=True))[0]]
    return [next_wide(blocks[k - 1].astype(BF), -k) for k in range(1, count, 2)]


def send_even(blocks):
    count = lax.axis_size("wide")
    if count > LONGEST_RING:
        return []
    return [next_wide(blocks[k - 1].astype(BF), -k) for k in range(2, count, 2)]


def add_wide(blocks, odd, even):
    terms = list(odd) + list(even)
    if lax.axis_size("wide") <= LONGEST_RING:
        terms = list(blocks)[-1:] + terms
    return sum(item.astype(F32) for item in terms)


def scatter_wide(blocks):
    return add_wide(blocks, send_odd(blocks), send_even(blocks))


def add_low(*terms):
    return sum(item.astype(F32) for item in terms).astype(BF)


def far_first(value):
    blocks = mirror(value)
    return blocks[1:] + blocks[:1]


def mirror(value):
    count = lax.axis_size("wide")
    me = lax.axis_index("wide")
    shaped = value.reshape((count, value.shape[0] // count) + value.shape[1:])
    return [
        lax.dynamic_index_in_dim(shaped, lax.rem(me - s + count, count), 0, keepdims=False)
        for s in range(count)
    ]


def share(value, axes=ALL):
    count = lax.axis_size(axes)
    return lax.all_to_all(
        jnp.broadcast_to(value[None], (count,) + value.shape), axes, 0, 0, tiled=True
    )


def pack_kernel(*refs):
    out_ref = refs[-1]
    chips, pairs, wide, units, _ = out_ref.shape
    start = 0
    operands = list(zip(refs[:-1:2], refs[1:-1:2]))
    for left_ref, right_ref in operands:
        whole = right_ref is operands[-1][1]
        rows = right_ref.shape[0] // (1 if whole else pairs * chips)
        product = nt(left_ref[...], right_ref[...])
        for w in range(wide):
            for p in range(pairs):
                for c in range(chips):
                    at = 0 if whole else (p * chips + c) * rows
                    piece = product[w * units : (w + 1) * units, at : at + rows]
                    out_ref[c, p, w, :, start : start + rows] = piece.astype(BF)
        start += rows
    out_ref[:, :, :, :, start:] = jnp.zeros(out_ref.shape[:4] + (out_ref.shape[4] - start,), BF)


def pack_grads(*operands):
    wide, pairs = lax.axis_size("wide"), lax.axis_size("pair")
    rows = sum(item.shape[0] for item in operands[1:-1:2]) // (2 * pairs) + operands[-1].shape[0]
    shape = (2, pairs, wide, operands[0].shape[0] // wide, -(-rows // 128) * 128)
    return pl.pallas_call(
        pack_kernel,
        out_shape=jax.ShapeDtypeStruct(shape, BF),
        compiler_params=pltpu.CompilerParams(vmem_limit_bytes=40 * 1024 * 1024),
        name="pack_grads",
    )(*operands)


def add_chip(blocks):
    chip = lax.axis_index("chip")
    keep = lax.dynamic_index_in_dim(blocks, chip, 0, keepdims=False)
    send = lax.dynamic_index_in_dim(blocks, 1 - chip, 0, keepdims=False)
    return add_low(keep, swap_chip(send))


def input_kernel(*refs, scale):
    weights, (d_ref, kept_ref, own_ref, send_ref) = refs[:-4], refs[-4:]
    cells = own_ref.shape[1]
    grad, s, start = 0.0, 0, 0
    for weight in weights:
        rows = weight.shape[0]
        grad = grad + tn(weight[...], d_ref[s][start : start + rows])
        start += rows
        if start == d_ref.shape[1]:
            s, start = s + 1, 0
    grad = grad * scale - kept_ref[0].astype(F32)
    own_ref[...] = grad[:, :cells].astype(BF)
    send_ref[...] = grad[:, cells:].astype(BF)


def input_rows(weights, d_rel, kept, rel, scale):
    _, genes, cells = kept.shape
    half = jax.ShapeDtypeStruct((genes, cells // 2), BF)

    def whole(item):
        return pl.BlockSpec(item.shape, lambda i: (0,) * item.ndim)

    return pl.pallas_call(
        functools.partial(input_kernel, scale=scale),
        grid=(1,),
        in_specs=[whole(item) for item in weights]
        + [whole(d_rel), pl.BlockSpec((1, genes, cells), lambda i: (rel, 0, 0))],
        out_specs=[whole(half)] * 2,
        out_shape=[half, half],
        compiler_params=pltpu.CompilerParams(vmem_limit_bytes=32 * 1024 * 1024),
        name="input_rows",
    )(*weights, d_rel, kept)


def plane_kernel(wide_ref, *refs):
    pairs = 4
    d_refs, swap_refs, x_refs = (refs[i * pairs : (i + 1) * pairs] for i in range(3))
    outs = refs[3 * pairs :]
    count, _, cells = d_refs[0].shape
    for k, out in enumerate(outs, 1):
        w = lax.rem(wide_ref[0] + count - k, count)
        total = 0.0
        for d_ref, swap_ref, x_ref in zip(d_refs, swap_refs, x_refs):
            total = total + nt(d_ref[w], x_ref[:, :cells])
            total = total + nt(swap_ref[w], x_ref[:, cells:])
        out[...] = total.astype(BF)


def plane_grads(plane, swapped, x_plane):
    count = lax.axis_size("wide")
    shape = (count, plane[0].shape[0] // count, plane[0].shape[1])
    vmem = pl.BlockSpec(memory_space=pltpu.VMEM)
    where = lax.axis_index("wide").astype(jnp.int32)[None]
    return pl.pallas_call(
        plane_kernel,
        in_specs=[pl.BlockSpec(memory_space=pltpu.SMEM)] + [vmem] * (3 * len(plane)),
        out_specs=[vmem] * count,
        out_shape=[jax.ShapeDtypeStruct((shape[1], x_plane[0].shape[0]), BF)] * count,
        compiler_params=pltpu.CompilerParams(vmem_limit_bytes=48 * 1024 * 1024),
        name="plane_grads",
    )(where, *[item.reshape(shape) for item in list(plane) + list(swapped)], *x_plane)


def place_kernel(where_ref, own_ref, came_ref, out_ref):
    pair, chip = where_ref[0], where_ref[1]
    pairs = own_ref.shape[0]
    rows = out_ref.shape[0] // (2 * pairs)
    for p in range(pairs):
        rel = pair ^ p
        for c in range(2):
            at = pl.ds((2 * p + c) * rows, rows)

            @pl.when(chip == c)
            def _():
                out_ref[at, :] = own_ref[rel, :rows, :].astype(F32)

            @pl.when(chip != c)
            def _():
                out_ref[at, :] = came_ref[rel, :rows, :].astype(F32)


def place_rows(own, came, genes):
    where = jnp.stack([lax.axis_index("pair"), lax.axis_index("chip")]).astype(jnp.int32)
    return pl.pallas_call(
        place_kernel,
        in_specs=[
            pl.BlockSpec(memory_space=pltpu.SMEM),
            pl.BlockSpec(memory_space=pltpu.VMEM),
            pl.BlockSpec(memory_space=pltpu.VMEM),
        ],
        out_specs=pl.BlockSpec(memory_space=pltpu.VMEM),
        out_shape=jax.ShapeDtypeStruct((genes, own.shape[2]), F32),
        compiler_params=pltpu.CompilerParams(vmem_limit_bytes=40 * 1024 * 1024),
        name="place_rows",
    )(where, own, came)


def normalize(pre_act, gain, shift, rider=()):
    cells = pre_act.shape[1]
    count = lax.axis_size(ALL)
    local_mean = jnp.mean(pre_act, axis=1)
    local_square = jnp.sum(jnp.square(pre_act - local_mean[:, None]), axis=1)
    every, rider = gate((share(jnp.stack([local_mean, local_square])), rider))
    centre = jnp.mean(every[:, 0], axis=0)
    squares = jnp.sum(every[:, 1], axis=0) + cells * jnp.sum(
        jnp.square(every[:, 0] - centre), axis=0
    )
    variance = squares / (cells * count)
    inverse = lax.rsqrt(variance + EPSILON)
    scaled = (pre_act - centre[:, None]) * inverse[:, None]
    normed = None if gain is None else scaled * gain[:, None] + shift[:, None]
    return normed, scaled, inverse, centre, variance, rider


def norm_backward(upstream, normed, scaled, inverse, gain, extra=None, pieces=None, rider=()):
    count = lax.axis_size(ALL)
    units, cells = upstream.shape
    count_all = cells * count
    gate_value = jax.nn.sigmoid(normed)
    back_normed = upstream * gate_value * (1.0 + normed * (1.0 - gate_value))
    sums = [jnp.sum(back_normed, axis=1), jnp.sum(back_normed * scaled, axis=1)]
    if extra is not None:
        sums.append(extra)
    sums = jnp.concatenate(sums)
    sent = jnp.broadcast_to(sums[None], (count,) + sums.shape)
    if pieces is not None:
        sent = jnp.concatenate([sent, pieces], axis=1)
    every, rider = gate((lax.all_to_all(sent, ALL, 0, 0, tiled=True), rider))
    both = jnp.sum(every[:, : 2 * units], axis=0)
    shift_sum, gain_sum = both[:units], both[units:]
    back_pre = (gain * inverse)[:, None] * (
        back_normed - (shift_sum / count_all)[:, None] - scaled * (gain_sum / count_all)[:, None]
    )
    return back_pre.astype(BF), gain_sum, shift_sum, every[:, 2 * units :], rider


def output_kernel(
    pair_ref,
    h_ref,
    weight_ref,
    x_ref,
    mask_ref,
    indicator_ref,
    bias_ref,
    back_ref,
    kept_ref,
    bias_sum_ref,
    loss_ref,
    *refs,
    inv_count,
):
    grad_ref, out_ref, keep_ref, low_ref = refs
    step = pl.program_id(0)
    units, cells = h_ref.shape
    genes = x_ref.shape[1]
    weight = weight_ref[:, 0].reshape(units, genes)
    out_ref[...] = tn(weight, h_ref[...])
    keep_ref[...] = tn(mask_ref[0], indicator_ref[...])

    @pl.when(step == 0)
    def _():
        loss_ref[...] = jnp.zeros_like(loss_ref)

    rows = 64

    def chunk(i, total):
        at = pl.ds(pl.multiple_of(i * rows, rows), rows)
        out_pre = out_ref[at, :] + bias_ref[0, at, :]
        small = jnp.exp(-jnp.abs(out_pre))
        recon = jnp.maximum(out_pre, 0.0) + jnp.log1p(small)
        slope = jnp.where(out_pre >= 0, 1.0, small) / (1.0 + small)
        diff = recon - x_ref[0, at, :].astype(F32)
        kept = keep_ref[at, :] * diff
        low = (kept * slope * inv_count).astype(BF)
        kept_ref[0, at, :] = kept.astype(BF)
        low_ref[at, :] = low
        return total + jnp.sum(kept * diff, axis=0, keepdims=True)

    loss_ref[...] += lax.fori_loop(0, genes // rows, chunk, jnp.zeros((1, cells), F32), unroll=True)
    low = low_ref[...]
    bias_sum_ref[0] = nt(jnp.ones((8, cells), BF), low)
    grad_ref[...] = nt(h_ref[...], low).astype(BF).reshape(grad_ref.shape)
    back = nn(weight, low)

    @pl.when(step == 0)
    def _():
        back_ref[...] = back

    @pl.when(step > 0)
    def _():
        back_ref[...] += back


def output_layer(pair, hidden, weight, x_all, mask, indicator, bias, inv_count):
    units, cells = hidden.shape
    wide, pairs, block_units, genes = weight.shape
    labels = mask.shape[1]
    return pl.pallas_call(
        functools.partial(output_kernel, inv_count=inv_count),
        grid_spec=pltpu.PrefetchScalarGridSpec(
            num_scalar_prefetch=1,
            grid=(pairs,),
            in_specs=[
                pl.BlockSpec((units, cells), lambda r, me: (0, 0)),
                pl.BlockSpec((wide, 1, block_units, genes), lambda r, me: (0, me[0] ^ r, 0, 0)),
                pl.BlockSpec((1, genes, cells), lambda r, me: (me[0] ^ r, 0, 0)),
                pl.BlockSpec((1, labels, genes), lambda r, me: (me[0] ^ r, 0, 0)),
                pl.BlockSpec((labels, cells), lambda r, me: (0, 0)),
                pl.BlockSpec((1, genes, 1), lambda r, me: (me[0] ^ r, 0, 0)),
            ],
            out_specs=[
                pl.BlockSpec((units, cells), lambda r, me: (0, 0)),
                pl.BlockSpec((1, genes, cells), lambda r, me: (r, 0, 0)),
                pl.BlockSpec((1, 8, genes), lambda r, me: (me[0] ^ r, 0, 0)),
                pl.BlockSpec((1, cells), lambda r, me: (0, 0)),
                pl.BlockSpec((1, wide, block_units, genes), lambda r, me: (me[0] ^ r, 0, 0, 0)),
            ],
            scratch_shapes=[
                pltpu.VMEM((genes, cells), F32),
                pltpu.VMEM((genes, cells), F32),
                pltpu.VMEM((genes, cells), BF),
            ],
        ),
        out_shape=[
            jax.ShapeDtypeStruct((units, cells), F32),
            jax.ShapeDtypeStruct((pairs, genes, cells), BF),
            jax.ShapeDtypeStruct((pairs, 8, genes), F32),
            jax.ShapeDtypeStruct((1, cells), F32),
            jax.ShapeDtypeStruct((pairs, wide, block_units, genes), BF),
        ],
        compiler_params=pltpu.CompilerParams(vmem_limit_bytes=48 * 1024 * 1024),
        cost_estimate=pl.CostEstimate(
            flops=36 * units * cells * genes * pairs,
            bytes_accessed=48 * units * genes * pairs,
            transcendentals=3 * cells * genes * pairs,
        ),
        name="output_layer",
    )(pair[None], hidden, weight, x_all, mask, indicator, bias)


def on_device(
    expression,
    noise,
    study,
    measured_gene_mask,
    encoder_input_weight,
    enc_mid,
    heads,
    dec_in,
    dec_mid,
    dec_out,
    norm_params,
    head_bias,
    out_bias,
    running_stats,
):
    wide_count = lax.axis_size("wide")
    row_split = lax.axis_size(("pair", "chip"))
    pair_count = lax.axis_size("pair")
    cells, genes = expression.shape
    count_all = cells * lax.axis_size(ALL)
    inv_count = 1.0 / count_all
    latent = dec_in.shape[0]
    block_genes, block_units = encoder_input_weight.shape
    units = block_units * wide_count
    pair = lax.axis_index("pair")
    chip = lax.axis_index("chip")
    block_id = pair * 2 + chip

    piece = -(-latent // row_split)
    piece_start = jnp.minimum(piece * block_id, latent - piece)
    dec_in_piece = lax.dynamic_slice_in_dim(dec_in, piece_start, piece, 0)
    packed = jnp.concatenate(
        [enc_mid.T, dec_mid.T, heads.T, dec_in_piece.T, norm_params.T], axis=1
    )
    packed = jnp.pad(packed, ((0, 0), (0, 256 - packed.shape[1])))
    mid_rows = enc_mid.shape[0]
    head_rows = heads.shape[0]
    widths = (mid_rows, mid_rows, head_rows, piece, norm_params.shape[0])
    totals = (units, units, 2 * latent, latent, 8)
    padded = -(-block_genes // 128) * 128
    extra = padded - block_genes
    def own_blocks(rows, axis):
        shape = rows.shape[:axis] + (pair_count, 2, block_genes) + rows.shape[axis + 1 :]
        cut = lax.dynamic_index_in_dim(rows.reshape(shape), chip, axis + 1, keepdims=False)
        widths = [(0, 0)] * cut.ndim
        widths[axis + 1] = (0, extra)
        return jnp.pad(cut, widths)

    def prepare():
        x_mine, x_send = split_cells(expression.T, pair_count, padded)
        return x_mine, swap_chip(x_send)

    labels = measured_gene_mask.shape[0]
    indicator = (jnp.arange(labels, dtype=jnp.int32)[:, None] == study[None, :]).astype(BF)
    indicator = jnp.concatenate([indicator, swap_chip(indicator)], axis=1)
    mask_all = own_blocks(measured_gene_mask.astype(BF), 1).transpose(1, 0, 2)
    bias_all = own_blocks(out_bias, 0)[:, :, None]

    enc_block = jnp.pad(encoder_input_weight.T, ((0, 0), (0, extra)))
    dec_block = jnp.pad(dec_out.T, ((0, 0), (0, extra)))
    mine = lax.all_gather(packed, ("wide", "pair"))
    enc_blocks, rel_pre, dec_line, x_all = gather_ring(enc_block, prepare, dec_block)
    mids = unpack_small(mine, swap_chip(mine), widths, totals)
    part_one = jnp.concatenate(rel_pre, axis=0)
    x_rel = [
        lax.dynamic_index_in_dim(x_all, pair ^ r, 0, keepdims=False) for r in range(pair_count)
    ]
    x_near = [swap_pair(x_rel[r], r) for r in range(1, pair_count - 1)]
    pre_other, dec_line, x_near = gate((swap_chip(part_one[:, cells:]), dec_line, x_near))
    pre_one = jnp.concatenate(mirror(part_one[:, :cells] + pre_other), axis=0)
    dec_line = jnp.concatenate(mirror(jnp.concatenate(dec_line)))
    dec_all = lax.all_gather(
        dec_line.reshape(wide_count, block_units, padded), "pair", axis=1
    )
    normed_one, scaled_one, inverse_one, centre_one, spread_one, mids = normalize(
        pre_one, None, None, mids
    )
    w_enc_mid, w_dec_mid, w_heads, w_dec_in, norm_full = mids
    norm_full = norm_full.astype(F32)
    gains = [norm_full[:, k] for k in range(4)]
    shifts = [norm_full[:, 4 + k] for k in range(4)]
    normed_one = scaled_one * gains[0][:, None] + shifts[0][:, None]
    hidden_one = jax.nn.silu(normed_one).astype(BF)

    pre_two = nn(w_enc_mid, hidden_one)
    normed_two, scaled_two, inverse_two, centre_two, spread_two, _ = normalize(
        pre_two, gains[1], shifts[1]
    )
    hidden_two = jax.nn.silu(normed_two).astype(BF)
    encoded = tn(w_heads, hidden_two) + head_bias[:, None]
    latent_mean = encoded[:latent]
    logvar = encoded[latent:]
    noise_t = noise.T
    spread_factor = jnp.exp(0.5 * logvar)
    code = (latent_mean + spread_factor * noise_t).astype(BF)
    pre_three = nn(w_dec_in, code)
    normed_three, scaled_three, inverse_three, centre_three, spread_three, _ = normalize(
        pre_three, gains[2], shifts[2]
    )
    hidden_three = jax.nn.silu(normed_three).astype(BF)
    pre_four = nn(w_dec_mid, hidden_three)
    normed_four, scaled_four, inverse_four, centre_four, spread_four, _ = normalize(
        pre_four, gains[3], shifts[3]
    )
    hidden_four = jax.nn.silu(normed_four).astype(BF)

    h_chip = jnp.concatenate([hidden_four, swap_chip(hidden_four)], axis=1)
    back_all, kept_diff, bias_sums, recon_sums, dec_parts = output_layer(
        pair.astype(jnp.int32),
        h_chip,
        dec_all,
        x_all,
        mask_all,
        indicator,
        bias_all,
        inv_count,
    )
    exp_logvar = jnp.exp(logvar)
    kl_sum = jnp.sum(exp_logvar + latent_mean * latent_mean - 1.0 - logvar)
    loss_local = 0.5 * jnp.sum(recon_sums) + (0.5 * ALPHA) * kl_sum
    back_four = back_all[:, :cells] + swap_chip(back_all[:, cells:])

    bias_rows = jnp.zeros((pair_count, 2, block_genes), F32)
    bias_rows = lax.dynamic_update_slice_in_dim(
        bias_rows, bias_sums[:, :1, :block_genes], chip, 1
    ).reshape(-1)
    devices = lax.axis_size(ALL)
    share_size = -(-genes // (devices * 8)) * 8
    bias_rows = jnp.pad(bias_rows, (0, devices * share_size - genes)).reshape(devices, share_size)
    dec_line = lax.psum_scatter(dec_parts, "pair", scatter_dimension=0, tiled=True)
    bp_four, gain_four, shift_four, _, _ = norm_backward(
        back_four, normed_four, scaled_four, inverse_four, gains[3]
    )

    back_three = tn(w_dec_mid, bp_four)
    bp_three, gain_three, shift_three, rest, x_far = norm_backward(
        back_three,
        normed_three,
        scaled_three,
        inverse_three,
        gains[2],
        loss_local[None],
        bias_rows,
        rider=swap_pair(x_rel[3][: padded // 2], 3),
    )
    loss = jnp.sum(rest[:, 0]) * inv_count
    bias_share = jnp.sum(rest[:, 1:], axis=0)
    back_code = tn(w_dec_in, bp_three)
    back_mean = back_code + ALPHA * inv_count * latent_mean
    back_logvar = (
        back_code * noise_t * spread_factor * 0.5
        + (ALPHA * 0.5 * inv_count) * (exp_logvar - 1.0)
    )
    back_enc = jnp.concatenate([back_mean, back_logvar], axis=0).astype(BF)
    head_sum = jnp.sum(back_enc.astype(F32), axis=1)
    back_two = nn(w_heads, back_enc)
    bp_two, gain_two, shift_two, rest, _ = norm_backward(
        back_two, normed_two, scaled_two, inverse_two, gains[1], jnp.concatenate([head_sum, bias_share])
    )
    head_bias_grad = jnp.sum(rest[:, : 2 * latent], axis=0)
    out_bias_grad = rest[:, 2 * latent :].reshape(-1)[:genes]

    back_one = tn(w_enc_mid, bp_two)
    x_last = swap_pair(x_rel[3][padded // 2 :], 3)
    bp_one, gain_one, shift_one, _, (dec_line, x_last) = norm_backward(
        back_one, normed_one, scaled_one, inverse_one, gains[0], rider=(dec_line, x_last)
    )

    dec_blocks = far_first(dec_line.reshape(units, padded))
    mid_in = gate((bp_four, hidden_three, bp_two, hidden_one, hidden_two, back_enc, bp_three, code, bp_one))
    packs = pack_grads(*mid_in[:8])
    d_other = swap_chip(bp_one)
    late_blocks, d_own = gate((enc_blocks, jnp.concatenate([bp_one, d_other], axis=1)))
    d_rel = far_first(d_own)
    d_rel = jnp.stack(d_rel[-1:] + d_rel[:-1])
    if wide_count > LONGEST_RING:
        late_blocks = [[jnp.concatenate(item) for item in zip(*late_blocks)]]
        d_rel = d_rel.reshape(1, units, 2 * cells)
    own_rows, send_rows = zip(
        *[
            input_rows(
                [item for row in late_blocks for item in (row[3:] if r == 3 else row[r : r + 1])],
                d_rel,
                kept_diff,
                r,
                count_all,
            )
            for r in range(pair_count)
        ]
    )
    own_rows, send_rows = jnp.stack(own_rows), jnp.stack(send_rows)
    d_near, d_other, own_rows, send_rows, dec_blocks, packs, dec_near, x_far = gate(
        (
            [bp_one] + [swap_pair(bp_one, r) for r in range(1, pair_count)],
            d_other,
            own_rows,
            send_rows,
            dec_blocks,
            packs,
            send_odd(dec_blocks),
            jnp.concatenate([x_far, x_last]),
        )
    )
    dec_far = send_even(dec_blocks)
    d_swap = [d_other] + [swap_chip(item) for item in d_near[1:]]
    mid_line = lax.psum_scatter(add_chip(packs), "pair", scatter_dimension=0, tiled=True)
    enc_low = plane_grads(d_near, d_swap, [x_rel[0]] + x_near + [x_far])
    late_rows = [gain_one, gain_two, gain_three, gain_four]
    late_rows += [shift_one, shift_two, shift_three, shift_four]
    late_rows += [centre_one, centre_two, centre_three, centre_four]
    late_rows += [spread_one, spread_two, spread_three, spread_four]
    enc_near, enc_far, mid_line, late_rows, dec_far = gate(
        (send_odd(enc_low), send_even(enc_low), mid_line, late_rows, dec_far)
    )
    enc_in_grad = add_wide(enc_low, enc_near, enc_far)
    dec_out_grad = add_wide(dec_blocks, dec_near, dec_far)
    mid_sum = scatter_wide(far_first(mid_line.reshape(units, mid_line.shape[3])))
    input_grad = place_rows(own_rows, swap_chip(send_rows), genes).T

    wide_index = lax.axis_index("wide")
    per_row = 8 // row_split

    def mine_of(rows_full):
        stacked = jnp.stack(rows_full)
        return lax.dynamic_slice(
            stacked, (block_id * per_row, wide_index * block_units), (per_row, block_units)
        )

    norm_grad = mine_of(late_rows[:8])
    unbias = count_all / (count_all - 1.0)
    stats = mine_of(late_rows[8:12] + [item * unbias for item in late_rows[12:]])
    running_next = (1.0 - MOMENTUM) * running_stats + MOMENTUM * stats

    dec_mid_grad = mid_sum[:, :mid_rows]
    enc_mid_grad = mid_sum[:, mid_rows : 2 * mid_rows]
    in_start = 2 * mid_rows + head_rows
    heads_grad = mid_sum[:, 2 * mid_rows : in_start]
    dec_in_grad = mid_sum[:, in_start : in_start + latent].T
    enc_in_grad = enc_in_grad[:, :block_genes]


    return (
        loss,
        input_grad,
        enc_in_grad.T,
        enc_mid_grad.T,
        heads_grad.T,
        dec_in_grad,
        dec_mid_grad.T,
        dec_out_grad[:, :block_genes].T,
        norm_grad,
        head_bias_grad,
        out_bias_grad,
        running_next,
    )


def solution(mesh):
    split = P(("pair", "chip"), "wide")
    by_cell = P(("wide", "pair", "chip"), None)
    return jax.shard_map(
        on_device,
        mesh=mesh,
        in_specs=(
            by_cell,
            by_cell,
            P(("wide", "pair", "chip")),
            P(),
            split,
            split,
            split,
            P(None, "wide"),
            split,
            split,
            split,
            P(),
            P(),
            split,
        ),
        out_specs=(
            P(),
            by_cell,
            split,
            split,
            split,
            P(None, "wide"),
            split,
            split,
            split,
            P(),
            P(),
            split,
        ),
        check_vma=False,
    )
```

```python
import functools

import jax
import jax.numpy as jnp
from jax import lax
from jax.experimental import pallas as pl
from jax.experimental.pallas import tpu as pltpu
from jax.sharding import PartitionSpec as P

ALPHA = 0.005
EPSILON = 1e-05
MOMENTUM = 0.1
LONGEST_RING = 4
ALL = ("wide", "pair", "chip")
BF = jnp.bfloat16
F32 = jnp.float32


def dot(left, right, dims):
    return lax.dot_general(left, right, (dims, ((), ())), preferred_element_type=F32)


def nn(left, right):
    return dot(left, right, ((1,), (0,)))


def nt(left, right):
    return dot(left, right, ((1,), (1,)))


def tn(left, right):
    return dot(left, right, ((0,), (0,)))


def swap_pair(value, bits):
    count = lax.axis_size("pair")
    return lax.ppermute(value, "pair", [(i, i ^ bits) for i in range(count)])


def swap_chip(value):
    return lax.ppermute(value, "chip", [(0, 1), (1, 0)])


def next_wide(value, hops=1):
    count = lax.axis_size("wide")
    return lax.ppermute(value, "wide", [(i, (i + hops) % count) for i in range(count)])


def half_of(units):
    return max(units // 2 // 8 * 8, 1)


def gate(value):
    return lax.optimization_barrier(value)


def spread_pair(block):
    cut = half_of(block.shape[0])
    by_x = swap_pair(block, 1)
    by_y = swap_pair(block, 2)
    upper = swap_pair(by_y[:cut], 1)
    lower = swap_pair(by_x[cut:], 2)
    return [block, by_x, by_y, jnp.concatenate([upper, lower], axis=0)]


def product_kernel(pair_ref, x_ref, own_ref, by_x_ref, by_y_ref, *refs):
    pair = pair_ref[0]
    diag_refs, out_ref = refs[:-1], refs[-1]
    out = nn(own_ref[...], x_ref[pair]) + nn(by_x_ref[...], x_ref[pair ^ 1])
    out = out + nn(by_y_ref[...], x_ref[pair ^ 2])
    start = 0
    for ref in diag_refs:
        stop = start + ref.shape[0]
        out_ref[start:stop, :] = out[start:stop] + nn(ref[...], x_ref[pair ^ 3])
        start = stop


def block_product(row, x_all):
    vmem = pl.BlockSpec(memory_space=pltpu.VMEM)
    pair = lax.axis_index("pair").astype(jnp.int32)[None]
    return pl.pallas_call(
        product_kernel,
        in_specs=[pl.BlockSpec(memory_space=pltpu.SMEM)] + [vmem] * (len(row) + 1),
        out_specs=vmem,
        out_shape=jax.ShapeDtypeStruct((row[0].shape[0], x_all.shape[2]), F32),
        compiler_params=pltpu.CompilerParams(vmem_limit_bytes=32 * 1024 * 1024),
        name="block_product",
    )(pair, x_all, *row)


def gather_ring(block, prepare, second):
    count = lax.axis_size("wide")
    if count > LONGEST_RING:
        line = lax.all_gather(block, "wide", axis=0, tiled=True)
        spread = [jnp.split(item, count) for item in spread_pair(jnp.concatenate(mirror(line)))]
        blocks = list(zip(*spread))
        x_all = jnp.concatenate(prepare(), axis=2)
        products = [block_product(row, x_all) for row in blocks]
        line = mirror(lax.all_gather(second, "wide", axis=0, tiled=True))
        return blocks, products, line, x_all
    cut = half_of(block.shape[0])
    ring, by_x, by_y, upper, lower, products = [block], [], [], [], [], []
    halves = prepare()
    for step in range(count + 1):
        moved = {}
        if step < count:
            moved["x"] = swap_pair(ring[step], 1)
            moved["y"] = swap_pair(ring[step], 2)
        if step < count - 1:
            moved["z"] = next_wide(ring[step])
        if step > 0:
            moved["u"] = swap_pair(by_y[step - 1][:cut], 1)
            moved["l"] = swap_pair(by_x[step - 1][cut:], 2)
        if step == 0:
            moved["h"] = halves
        if step == count - 2:
            moved["s"] = second
        if step > 1 and step > count - 2:
            moved["d"] = next_wide(seconds[-1])
        if step == 2:
            moved["a"] = jnp.concatenate(halves, axis=2)
        if step > 2:
            done = step - 3
            row = (ring[done], by_x[done], by_y[done], upper[done], lower[done])
            moved["p"] = block_product(row, x_all)
        moved = gate(moved)
        if "z" in moved:
            ring.append(moved["z"])
        if "x" in moved:
            by_x.append(moved["x"])
            by_y.append(moved["y"])
        if "u" in moved:
            upper.append(moved["u"])
            lower.append(moved["l"])
        if "s" in moved:
            seconds = [moved["s"]]
        if "d" in moved:
            seconds.append(moved["d"])
        halves = moved.get("h", halves)
        x_all = moved.get("a", None) if step <= 2 else x_all
        if "p" in moved:
            products.append(moved["p"])
    blocks = list(zip(ring, by_x, by_y, upper, lower))
    products += [block_product(row, x_all) for row in blocks[len(products) :]]
    while len(seconds) < count:
        seconds.append(next_wide(seconds[-1]))
    return blocks, products, seconds, x_all


def split_kernel(chip_ref, cells_ref, mine_ref, other_ref):
    blocks = 2 * mine_ref.shape[0]
    total = cells_ref.shape[0]
    rows = total // blocks
    chip = chip_ref[0]
    tail = jnp.zeros((mine_ref.shape[1] - rows, cells_ref.shape[1]), F32)
    for block in range(blocks):
        start = block * rows
        first = start // 16 * 16
        last = min(-(-(start + rows) // 16) * 16, total)
        window = cells_ref[first:last, :].astype(F32)
        piece = window[start - first : start - first + rows]
        piece = jnp.concatenate([piece, tail], axis=0).astype(BF)

        @pl.when(chip == block % 2)
        def _():
            mine_ref[block // 2] = piece

        @pl.when(chip != block % 2)
        def _():
            other_ref[block // 2] = piece


def split_cells(cells_t, pairs, padded):
    vmem = pl.BlockSpec(memory_space=pltpu.VMEM)
    shape = jax.ShapeDtypeStruct((pairs, padded, cells_t.shape[1]), BF)
    return pl.pallas_call(
        split_kernel,
        in_specs=[pl.BlockSpec(memory_space=pltpu.SMEM), vmem],
        out_specs=[vmem, vmem],
        out_shape=[shape, shape],
        compiler_params=pltpu.CompilerParams(vmem_limit_bytes=40 * 1024 * 1024),
        name="split_cells",
    )(lax.axis_index("chip").astype(jnp.int32)[None], cells_t)


def unpack_kernel(where_ref, mine_ref, other_ref, *outs, starts, places):
    chip = where_ref[0]
    count, pairs = mine_ref.shape[:2]
    for w in range(count):
        for p in range(pairs):

            def put(ref, c):
                for out, start, place in zip(outs, starts, places):
                    at, width = place[2 * p + c]
                    out[w, :, at : at + width] = ref[w, p, :, start : start + width]

            for c in range(2):

                @pl.when(chip == c)
                def _():
                    put(mine_ref, c)
                    put(other_ref, 1 - c)


def unpack_small(mine, other, widths, totals):
    count, pairs = lax.axis_size("wide"), lax.axis_size("pair")
    shape = (count, pairs) + mine.shape[1:]
    where = lax.axis_index("chip").astype(jnp.int32)[None]
    starts = [sum(widths[:i]) for i in range(len(widths))]
    places = [
        [(min(block * width, total - width), width) for block in range(2 * pairs)]
        for width, total in zip(widths, totals)
    ]
    vmem = pl.BlockSpec(memory_space=pltpu.VMEM)
    outs = pl.pallas_call(
        functools.partial(unpack_kernel, starts=starts, places=places),
        in_specs=[pl.BlockSpec(memory_space=pltpu.SMEM), vmem, vmem],
        out_specs=[vmem] * len(widths),
        out_shape=[jax.ShapeDtypeStruct((count, shape[2], total), BF) for total in totals],
        compiler_params=pltpu.CompilerParams(vmem_limit_bytes=32 * 1024 * 1024),
        name="unpack_small",
    )(where, mine.reshape(shape), other.reshape(shape))
    return [item.reshape(count * shape[2], -1) for item in outs]


def send_odd(blocks):
    count = lax.axis_size("wide")
    if count > LONGEST_RING:
        order = jnp.stack(list(blocks)[-1:] + list(blocks)[:-1])
        line = jnp.stack(mirror(order.reshape((-1,) + order.shape[2:])))
        return [gate(lax.psum_scatter(line, "wide", scatter_dimension=0, tiled=True))[0]]
    return [next_wide(blocks[k - 1].astype(BF), -k) for k in range(1, count, 2)]


def send_even(blocks):
    count = lax.axis_size("wide")
    if count > LONGEST_RING:
        return []
    return [next_wide(blocks[k - 1].astype(BF), -k) for k in range(2, count, 2)]


def add_wide(blocks, odd, even):
    terms = list(odd) + list(even)
    if lax.axis_size("wide") <= LONGEST_RING:
        terms = list(blocks)[-1:] + terms
    return sum(item.astype(F32) for item in terms)


def scatter_wide(blocks):
    return add_wide(blocks, send_odd(blocks), send_even(blocks))


def add_low(*terms):
    return sum(item.astype(F32) for item in terms).astype(BF)


def far_first(value):
    blocks = mirror(value)
    return blocks[1:] + blocks[:1]


def mirror(value):
    count = lax.axis_size("wide")
    me = lax.axis_index("wide")
    shaped = value.reshape((count, value.shape[0] // count) + value.shape[1:])
    return [
        lax.dynamic_index_in_dim(shaped, lax.rem(me - s + count, count), 0, keepdims=False)
        for s in range(count)
    ]


def share(value, axes=ALL):
    count = lax.axis_size(axes)
    return lax.all_to_all(
        jnp.broadcast_to(value[None], (count,) + value.shape), axes, 0, 0, tiled=True
    )


def pack_kernel(*refs):
    out_ref = refs[-1]
    chips, pairs, wide, units, _ = out_ref.shape
    start = 0
    operands = list(zip(refs[:-1:2], refs[1:-1:2]))
    for left_ref, right_ref in operands:
        whole = right_ref is operands[-1][1]
        rows = right_ref.shape[0] // (1 if whole else pairs * chips)
        product = nt(left_ref[...], right_ref[...])
        for w in range(wide):
            for p in range(pairs):
                for c in range(chips):
                    at = 0 if whole else (p * chips + c) * rows
                    piece = product[w * units : (w + 1) * units, at : at + rows]
                    out_ref[c, p, w, :, start : start + rows] = piece.astype(BF)
        start += rows
    out_ref[:, :, :, :, start:] = jnp.zeros(out_ref.shape[:4] + (out_ref.shape[4] - start,), BF)


def pack_grads(*operands):
    wide, pairs = lax.axis_size("wide"), lax.axis_size("pair")
    rows = sum(item.shape[0] for item in operands[1:-1:2]) // (2 * pairs) + operands[-1].shape[0]
    shape = (2, pairs, wide, operands[0].shape[0] // wide, -(-rows // 128) * 128)
    return pl.pallas_call(
        pack_kernel,
        out_shape=jax.ShapeDtypeStruct(shape, BF),
        compiler_params=pltpu.CompilerParams(vmem_limit_bytes=40 * 1024 * 1024),
        name="pack_grads",
    )(*operands)


def add_chip(blocks):
    chip = lax.axis_index("chip")
    keep = lax.dynamic_index_in_dim(blocks, chip, 0, keepdims=False)
    send = lax.dynamic_index_in_dim(blocks, 1 - chip, 0, keepdims=False)
    return add_low(keep, swap_chip(send))


def input_kernel(*refs, scale):
    weights, (d_ref, kept_ref, own_ref, send_ref) = refs[:-4], refs[-4:]
    cells = own_ref.shape[1]
    grad, s, start = 0.0, 0, 0
    for weight in weights:
        rows = weight.shape[0]
        grad = grad + tn(weight[...], d_ref[s][start : start + rows])
        start += rows
        if start == d_ref.shape[1]:
            s, start = s + 1, 0
    grad = grad * scale - kept_ref[0].astype(F32)
    own_ref[...] = grad[:, :cells].astype(BF)
    send_ref[...] = grad[:, cells:].astype(BF)


def input_rows(weights, d_rel, kept, rel, scale):
    _, genes, cells = kept.shape
    half = jax.ShapeDtypeStruct((genes, cells // 2), BF)

    def whole(item):
        return pl.BlockSpec(item.shape, lambda i: (0,) * item.ndim)

    return pl.pallas_call(
        functools.partial(input_kernel, scale=scale),
        grid=(1,),
        in_specs=[whole(item) for item in weights]
        + [whole(d_rel), pl.BlockSpec((1, genes, cells), lambda i: (rel, 0, 0))],
        out_specs=[whole(half)] * 2,
        out_shape=[half, half],
        compiler_params=pltpu.CompilerParams(vmem_limit_bytes=32 * 1024 * 1024),
        name="input_rows",
    )(*weights, d_rel, kept)


def plane_kernel(wide_ref, *refs):
    pairs = 4
    d_refs, swap_refs, x_refs = (refs[i * pairs : (i + 1) * pairs] for i in range(3))
    outs = refs[3 * pairs :]
    count, _, cells = d_refs[0].shape
    for k, out in enumerate(outs, 1):
        w = lax.rem(wide_ref[0] + count - k, count)
        total = 0.0
        for d_ref, swap_ref, x_ref in zip(d_refs, swap_refs, x_refs):
            total = total + nt(d_ref[w], x_ref[:, :cells])
            total = total + nt(swap_ref[w], x_ref[:, cells:])
        out[...] = total.astype(BF)


def plane_grads(plane, swapped, x_plane):
    count = lax.axis_size("wide")
    shape = (count, plane[0].shape[0] // count, plane[0].shape[1])
    vmem = pl.BlockSpec(memory_space=pltpu.VMEM)
    where = lax.axis_index("wide").astype(jnp.int32)[None]
    return pl.pallas_call(
        plane_kernel,
        in_specs=[pl.BlockSpec(memory_space=pltpu.SMEM)] + [vmem] * (3 * len(plane)),
        out_specs=[vmem] * count,
        out_shape=[jax.ShapeDtypeStruct((shape[1], x_plane[0].shape[0]), BF)] * count,
        compiler_params=pltpu.CompilerParams(vmem_limit_bytes=48 * 1024 * 1024),
        name="plane_grads",
    )(where, *[item.reshape(shape) for item in list(plane) + list(swapped)], *x_plane)


def place_kernel(where_ref, own_ref, came_ref, out_ref):
    pair, chip = where_ref[0], where_ref[1]
    pairs = own_ref.shape[0]
    rows = out_ref.shape[0] // (2 * pairs)
    for p in range(pairs):
        rel = pair ^ p
        for c in range(2):
            at = pl.ds((2 * p + c) * rows, rows)

            @pl.when(chip == c)
            def _():
                out_ref[at, :] = own_ref[rel, :rows, :].astype(F32)

            @pl.when(chip != c)
            def _():
                out_ref[at, :] = came_ref[rel, :rows, :].astype(F32)


def place_rows(own, came, genes):
    where = jnp.stack([lax.axis_index("pair"), lax.axis_index("chip")]).astype(jnp.int32)
    return pl.pallas_call(
        place_kernel,
        in_specs=[
            pl.BlockSpec(memory_space=pltpu.SMEM),
            pl.BlockSpec(memory_space=pltpu.VMEM),
            pl.BlockSpec(memory_space=pltpu.VMEM),
        ],
        out_specs=pl.BlockSpec(memory_space=pltpu.VMEM),
        out_shape=jax.ShapeDtypeStruct((genes, own.shape[2]), F32),
        compiler_params=pltpu.CompilerParams(vmem_limit_bytes=40 * 1024 * 1024),
        name="place_rows",
    )(where, own, came)


def normalize(pre_act, gain, shift, rider=()):
    cells = pre_act.shape[1]
    count = lax.axis_size(ALL)
    local_mean = jnp.mean(pre_act, axis=1)
    local_square = jnp.sum(jnp.square(pre_act - local_mean[:, None]), axis=1)
    every, rider = gate((share(jnp.stack([local_mean, local_square])), rider))
    centre = jnp.mean(every[:, 0], axis=0)
    squares = jnp.sum(every[:, 1], axis=0) + cells * jnp.sum(
        jnp.square(every[:, 0] - centre), axis=0
    )
    variance = squares / (cells * count)
    inverse = lax.rsqrt(variance + EPSILON)
    scaled = (pre_act - centre[:, None]) * inverse[:, None]
    normed = None if gain is None else scaled * gain[:, None] + shift[:, None]
    return normed, scaled, inverse, centre, variance, rider


def norm_backward(upstream, normed, scaled, inverse, gain, extra=None, pieces=None, rider=()):
    count = lax.axis_size(ALL)
    units, cells = upstream.shape
    count_all = cells * count
    gate_value = jax.nn.sigmoid(normed)
    back_normed = upstream * gate_value * (1.0 + normed * (1.0 - gate_value))
    sums = [jnp.sum(back_normed, axis=1), jnp.sum(back_normed * scaled, axis=1)]
    if extra is not None:
        sums.append(extra)
    sums = jnp.concatenate(sums)
    sent = jnp.broadcast_to(sums[None], (count,) + sums.shape)
    if pieces is not None:
        sent = jnp.concatenate([sent, pieces], axis=1)
    every, rider = gate((lax.all_to_all(sent, ALL, 0, 0, tiled=True), rider))
    both = jnp.sum(every[:, : 2 * units], axis=0)
    shift_sum, gain_sum = both[:units], both[units:]
    back_pre = (gain * inverse)[:, None] * (
        back_normed - (shift_sum / count_all)[:, None] - scaled * (gain_sum / count_all)[:, None]
    )
    return back_pre.astype(BF), gain_sum, shift_sum, every[:, 2 * units :], rider


def output_kernel(
    pair_ref,
    h_ref,
    weight_ref,
    x_ref,
    mask_ref,
    indicator_ref,
    bias_ref,
    back_ref,
    kept_ref,
    bias_sum_ref,
    loss_ref,
    *refs,
    inv_count,
):
    grad_ref, out_ref, keep_ref, low_ref = refs
    step = pl.program_id(0)
    units, cells = h_ref.shape
    genes = x_ref.shape[1]
    weight = weight_ref[:, 0].reshape(units, genes)
    out_ref[...] = tn(weight, h_ref[...])
    keep_ref[...] = tn(mask_ref[0], indicator_ref[...])

    @pl.when(step == 0)
    def _():
        loss_ref[...] = jnp.zeros_like(loss_ref)

    rows = 64

    def chunk(i, total):
        at = pl.ds(pl.multiple_of(i * rows, rows), rows)
        out_pre = out_ref[at, :] + bias_ref[0, at, :]
        small = jnp.exp(-jnp.abs(out_pre))
        recon = jnp.maximum(out_pre, 0.0) + jnp.log1p(small)
        slope = jnp.where(out_pre >= 0, 1.0, small) / (1.0 + small)
        diff = recon - x_ref[0, at, :].astype(F32)
        kept = keep_ref[at, :] * diff
        low = (kept * slope * inv_count).astype(BF)
        kept_ref[0, at, :] = kept.astype(BF)
        low_ref[at, :] = low
        return total + jnp.sum(kept * diff, axis=0, keepdims=True)

    loss_ref[...] += lax.fori_loop(0, genes // rows, chunk, jnp.zeros((1, cells), F32), unroll=True)
    low = low_ref[...]
    bias_sum_ref[0] = nt(jnp.ones((8, cells), BF), low)
    grad_ref[...] = nt(h_ref[...], low).astype(BF).reshape(grad_ref.shape)
    back = nn(weight, low)

    @pl.when(step == 0)
    def _():
        back_ref[...] = back

    @pl.when(step > 0)
    def _():
        back_ref[...] += back


def output_layer(pair, hidden, weight, x_all, mask, indicator, bias, inv_count):
    units, cells = hidden.shape
    wide, pairs, block_units, genes = weight.shape
    labels = mask.shape[1]
    return pl.pallas_call(
        functools.partial(output_kernel, inv_count=inv_count),
        grid_spec=pltpu.PrefetchScalarGridSpec(
            num_scalar_prefetch=1,
            grid=(pairs,),
            in_specs=[
                pl.BlockSpec((units, cells), lambda r, me: (0, 0)),
                pl.BlockSpec((wide, 1, block_units, genes), lambda r, me: (0, me[0] ^ r, 0, 0)),
                pl.BlockSpec((1, genes, cells), lambda r, me: (me[0] ^ r, 0, 0)),
                pl.BlockSpec((1, labels, genes), lambda r, me: (me[0] ^ r, 0, 0)),
                pl.BlockSpec((labels, cells), lambda r, me: (0, 0)),
                pl.BlockSpec((1, genes, 1), lambda r, me: (me[0] ^ r, 0, 0)),
            ],
            out_specs=[
                pl.BlockSpec((units, cells), lambda r, me: (0, 0)),
                pl.BlockSpec((1, genes, cells), lambda r, me: (r, 0, 0)),
                pl.BlockSpec((1, 8, genes), lambda r, me: (me[0] ^ r, 0, 0)),
                pl.BlockSpec((1, cells), lambda r, me: (0, 0)),
                pl.BlockSpec((1, wide, block_units, genes), lambda r, me: (me[0] ^ r, 0, 0, 0)),
            ],
            scratch_shapes=[
                pltpu.VMEM((genes, cells), F32),
                pltpu.VMEM((genes, cells), F32),
                pltpu.VMEM((genes, cells), BF),
            ],
        ),
        out_shape=[
            jax.ShapeDtypeStruct((units, cells), F32),
            jax.ShapeDtypeStruct((pairs, genes, cells), BF),
            jax.ShapeDtypeStruct((pairs, 8, genes), F32),
            jax.ShapeDtypeStruct((1, cells), F32),
            jax.ShapeDtypeStruct((pairs, wide, block_units, genes), BF),
        ],
        compiler_params=pltpu.CompilerParams(vmem_limit_bytes=48 * 1024 * 1024),
        cost_estimate=pl.CostEstimate(
            flops=36 * units * cells * genes * pairs,
            bytes_accessed=48 * units * genes * pairs,
            transcendentals=3 * cells * genes * pairs,
        ),
        name="output_layer",
    )(pair[None], hidden, weight, x_all, mask, indicator, bias)


def on_device(
    expression,
    noise,
    study,
    measured_gene_mask,
    encoder_input_weight,
    enc_mid,
    heads,
    dec_in,
    dec_mid,
    dec_out,
    norm_params,
    head_bias,
    out_bias,
    running_stats,
):
    wide_count = lax.axis_size("wide")
    row_split = lax.axis_size(("pair", "chip"))
    pair_count = lax.axis_size("pair")
    cells, genes = expression.shape
    count_all = cells * lax.axis_size(ALL)
    inv_count = 1.0 / count_all
    latent = dec_in.shape[0]
    block_genes, block_units = encoder_input_weight.shape
    units = block_units * wide_count
    pair = lax.axis_index("pair")
    chip = lax.axis_index("chip")
    block_id = pair * 2 + chip

    piece = -(-latent // row_split)
    piece_start = jnp.minimum(piece * block_id, latent - piece)
    dec_in_piece = lax.dynamic_slice_in_dim(dec_in, piece_start, piece, 0)
    packed = jnp.concatenate(
        [enc_mid.T, dec_mid.T, heads.T, dec_in_piece.T, norm_params.T], axis=1
    )
    packed = jnp.pad(packed, ((0, 0), (0, 256 - packed.shape[1])))
    mid_rows = enc_mid.shape[0]
    head_rows = heads.shape[0]
    widths = (mid_rows, mid_rows, head_rows, piece, norm_params.shape[0])
    totals = (units, units, 2 * latent, latent, 8)
    padded = -(-block_genes // 128) * 128
    extra = padded - block_genes
    def own_blocks(rows, axis):
        shape = rows.shape[:axis] + (pair_count, 2, block_genes) + rows.shape[axis + 1 :]
        cut = lax.dynamic_index_in_dim(rows.reshape(shape), chip, axis + 1, keepdims=False)
        widths = [(0, 0)] * cut.ndim
        widths[axis + 1] = (0, extra)
        return jnp.pad(cut, widths)

    def prepare():
        x_mine, x_send = split_cells(expression.T, pair_count, padded)
        return x_mine, swap_chip(x_send)

    labels = measured_gene_mask.shape[0]
    indicator = (jnp.arange(labels, dtype=jnp.int32)[:, None] == study[None, :]).astype(BF)
    indicator = jnp.concatenate([indicator, swap_chip(indicator)], axis=1)
    mask_all = own_blocks(measured_gene_mask.astype(BF), 1).transpose(1, 0, 2)
    bias_all = own_blocks(out_bias, 0)[:, :, None]

    enc_block = jnp.pad(encoder_input_weight.T, ((0, 0), (0, extra)))
    dec_block = jnp.pad(dec_out.T, ((0, 0), (0, extra)))
    mine = lax.all_gather(packed, ("wide", "pair"))
    enc_blocks, rel_pre, dec_line, x_all = gather_ring(enc_block, prepare, dec_block)
    mids = unpack_small(mine, swap_chip(mine), widths, totals)
    part_one = jnp.concatenate(rel_pre, axis=0)
    x_rel = [
        lax.dynamic_index_in_dim(x_all, pair ^ r, 0, keepdims=False) for r in range(pair_count)
    ]
    x_near = [swap_pair(x_rel[r], r) for r in range(1, pair_count - 1)]
    part_one, dec_line = gate((part_one, dec_line))
    pre_one = part_one[:, :cells] + swap_chip(part_one[:, cells:])
    pre_one = jnp.concatenate(mirror(pre_one), axis=0)
    dec_line = jnp.concatenate(mirror(jnp.concatenate(dec_line)))
    dec_all = lax.all_gather(
        dec_line.reshape(wide_count, block_units, padded), "pair", axis=1
    )
    normed_one, scaled_one, inverse_one, centre_one, spread_one, (mids, x_near) = normalize(
        pre_one, None, None, (mids, x_near)
    )
    w_enc_mid, w_dec_mid, w_heads, w_dec_in, norm_full = mids
    norm_full = norm_full.astype(F32)
    gains = [norm_full[:, k] for k in range(4)]
    shifts = [norm_full[:, 4 + k] for k in range(4)]
    normed_one = scaled_one * gains[0][:, None] + shifts[0][:, None]
    hidden_one = jax.nn.silu(normed_one).astype(BF)

    pre_two = nn(w_enc_mid, hidden_one)
    normed_two, scaled_two, inverse_two, centre_two, spread_two, _ = normalize(
        pre_two, gains[1], shifts[1]
    )
    hidden_two = jax.nn.silu(normed_two).astype(BF)
    encoded = tn(w_heads, hidden_two) + head_bias[:, None]
    latent_mean = encoded[:latent]
    logvar = encoded[latent:]
    noise_t = noise.T
    spread_factor = jnp.exp(0.5 * logvar)
    code = (latent_mean + spread_factor * noise_t).astype(BF)
    pre_three = nn(w_dec_in, code)
    normed_three, scaled_three, inverse_three, centre_three, spread_three, _ = normalize(
        pre_three, gains[2], shifts[2]
    )
    hidden_three = jax.nn.silu(normed_three).astype(BF)
    pre_four = nn(w_dec_mid, hidden_three)
    normed_four, scaled_four, inverse_four, centre_four, spread_four, _ = normalize(
        pre_four, gains[3], shifts[3]
    )
    hidden_four = jax.nn.silu(normed_four).astype(BF)

    h_chip = jnp.concatenate([hidden_four, swap_chip(hidden_four)], axis=1)
    back_all, kept_diff, bias_sums, recon_sums, dec_parts = output_layer(
        pair.astype(jnp.int32),
        h_chip,
        dec_all,
        x_all,
        mask_all,
        indicator,
        bias_all,
        inv_count,
    )
    exp_logvar = jnp.exp(logvar)
    kl_sum = jnp.sum(exp_logvar + latent_mean * latent_mean - 1.0 - logvar)
    loss_local = 0.5 * jnp.sum(recon_sums) + (0.5 * ALPHA) * kl_sum
    back_four = back_all[:, :cells] + swap_chip(back_all[:, cells:])

    bias_rows = jnp.zeros((pair_count, 2, block_genes), F32)
    bias_rows = lax.dynamic_update_slice_in_dim(
        bias_rows, bias_sums[:, :1, :block_genes], chip, 1
    ).reshape(-1)
    devices = lax.axis_size(ALL)
    share_size = -(-genes // (devices * 8)) * 8
    bias_rows = jnp.pad(bias_rows, (0, devices * share_size - genes)).reshape(devices, share_size)
    dec_line = lax.psum_scatter(dec_parts, "pair", scatter_dimension=0, tiled=True)
    bp_four, gain_four, shift_four, _, _ = norm_backward(
        back_four, normed_four, scaled_four, inverse_four, gains[3]
    )

    back_three = tn(w_dec_mid, bp_four)
    bp_three, gain_three, shift_three, rest, x_far = norm_backward(
        back_three,
        normed_three,
        scaled_three,
        inverse_three,
        gains[2],
        loss_local[None],
        bias_rows,
        rider=swap_pair(x_rel[3][: padded // 2], 3),
    )
    loss = jnp.sum(rest[:, 0]) * inv_count
    bias_share = jnp.sum(rest[:, 1:], axis=0)
    back_code = tn(w_dec_in, bp_three)
    back_mean = back_code + ALPHA * inv_count * latent_mean
    back_logvar = (
        back_code * noise_t * spread_factor * 0.5
        + (ALPHA * 0.5 * inv_count) * (exp_logvar - 1.0)
    )
    back_enc = jnp.concatenate([back_mean, back_logvar], axis=0).astype(BF)
    head_sum = jnp.sum(back_enc.astype(F32), axis=1)
    back_two = nn(w_heads, back_enc)
    bp_two, gain_two, shift_two, rest, _ = norm_backward(
        back_two, normed_two, scaled_two, inverse_two, gains[1], jnp.concatenate([head_sum, bias_share])
    )
    head_bias_grad = jnp.sum(rest[:, : 2 * latent], axis=0)
    out_bias_grad = rest[:, 2 * latent :].reshape(-1)[:genes]

    back_one = tn(w_enc_mid, bp_two)
    x_last = swap_pair(x_rel[3][padded // 2 :], 3)
    bp_one, gain_one, shift_one, _, (dec_line, x_last) = norm_backward(
        back_one, normed_one, scaled_one, inverse_one, gains[0], rider=(dec_line, x_last)
    )

    dec_blocks = far_first(dec_line.reshape(units, padded))
    mid_in = gate((bp_four, hidden_three, bp_two, hidden_one, hidden_two, back_enc, bp_three, code, bp_one))
    packs = pack_grads(*mid_in[:8])
    d_other = swap_chip(bp_one)
    late_blocks, d_own = gate((enc_blocks, jnp.concatenate([bp_one, d_other], axis=1)))
    d_rel = far_first(d_own)
    d_rel = jnp.stack(d_rel[-1:] + d_rel[:-1])
    if wide_count > LONGEST_RING:
        late_blocks = [[jnp.concatenate(item) for item in zip(*late_blocks)]]
        d_rel = d_rel.reshape(1, units, 2 * cells)
    own_rows, send_rows = zip(
        *[
            input_rows(
                [item for row in late_blocks for item in (row[3:] if r == 3 else row[r : r + 1])],
                d_rel,
                kept_diff,
                r,
                count_all,
            )
            for r in range(pair_count)
        ]
    )
    own_rows, send_rows = jnp.stack(own_rows), jnp.stack(send_rows)
    d_near, d_other, own_rows, send_rows, dec_blocks, packs, dec_near, x_far = gate(
        (
            [bp_one] + [swap_pair(bp_one, r) for r in range(1, pair_count)],
            d_other,
            own_rows,
            send_rows,
            dec_blocks,
            packs,
            send_odd(dec_blocks),
            jnp.concatenate([x_far, x_last]),
        )
    )
    dec_far = send_even(dec_blocks)
    d_swap = [d_other] + [swap_chip(item) for item in d_near[1:]]
    mid_line = lax.psum_scatter(add_chip(packs), "pair", scatter_dimension=0, tiled=True)
    enc_low = plane_grads(d_near, d_swap, [x_rel[0]] + x_near + [x_far])
    late_rows = [gain_one, gain_two, gain_three, gain_four]
    late_rows += [shift_one, shift_two, shift_three, shift_four]
    late_rows += [centre_one, centre_two, centre_three, centre_four]
    late_rows += [spread_one, spread_two, spread_three, spread_four]
    enc_near, enc_far, mid_line, late_rows, dec_far = gate(
        (send_odd(enc_low), send_even(enc_low), mid_line, late_rows, dec_far)
    )
    enc_in_grad = add_wide(enc_low, enc_near, enc_far)
    dec_out_grad = add_wide(dec_blocks, dec_near, dec_far)
    mid_sum = scatter_wide(far_first(mid_line.reshape(units, mid_line.shape[3])))
    input_grad = place_rows(own_rows, swap_chip(send_rows), genes).T

    wide_index = lax.axis_index("wide")
    per_row = 8 // row_split

    def mine_of(rows_full):
        stacked = jnp.stack(rows_full)
        return lax.dynamic_slice(
            stacked, (block_id * per_row, wide_index * block_units), (per_row, block_units)
        )

    norm_grad = mine_of(late_rows[:8])
    unbias = count_all / (count_all - 1.0)
    stats = mine_of(late_rows[8:12] + [item * unbias for item in late_rows[12:]])
    running_next = (1.0 - MOMENTUM) * running_stats + MOMENTUM * stats

    dec_mid_grad = mid_sum[:, :mid_rows]
    enc_mid_grad = mid_sum[:, mid_rows : 2 * mid_rows]
    in_start = 2 * mid_rows + head_rows
    heads_grad = mid_sum[:, 2 * mid_rows : in_start]
    dec_in_grad = mid_sum[:, in_start : in_start + latent].T
    enc_in_grad = enc_in_grad[:, :block_genes]


    return (
        loss,
        input_grad,
        enc_in_grad.T,
        enc_mid_grad.T,
        heads_grad.T,
        dec_in_grad,
        dec_mid_grad.T,
        dec_out_grad[:, :block_genes].T,
        norm_grad,
        head_bias_grad,
        out_bias_grad,
        running_next,
    )


def solution(mesh):
    split = P(("pair", "chip"), "wide")
    by_cell = P(("wide", "pair", "chip"), None)
    return jax.shard_map(
        on_device,
        mesh=mesh,
        in_specs=(
            by_cell,
            by_cell,
            P(("wide", "pair", "chip")),
            P(),
            split,
            split,
            split,
            P(None, "wide"),
            split,
            split,
            split,
            P(),
            P(),
            split,
        ),
        out_specs=(
            P(),
            by_cell,
            split,
            split,
            split,
            P(None, "wide"),
            split,
            split,
            split,
            P(),
            P(),
            split,
        ),
        check_vma=False,
    )
```

```python
import functools

import jax
import jax.numpy as jnp
from jax import lax
from jax.experimental import pallas as pl
from jax.experimental.pallas import tpu as pltpu
from jax.sharding import PartitionSpec as P

ALPHA = 0.005
EPSILON = 1e-05
MOMENTUM = 0.1
LONGEST_RING = 4
ALL = ("wide", "pair", "chip")
BF = jnp.bfloat16
F32 = jnp.float32


def dot(left, right, dims):
    return lax.dot_general(left, right, (dims, ((), ())), preferred_element_type=F32)


def nn(left, right):
    return dot(left, right, ((1,), (0,)))


def nt(left, right):
    return dot(left, right, ((1,), (1,)))


def tn(left, right):
    return dot(left, right, ((0,), (0,)))


def swap_pair(value, bits):
    count = lax.axis_size("pair")
    return lax.ppermute(value, "pair", [(i, i ^ bits) for i in range(count)])


def swap_chip(value):
    return lax.ppermute(value, "chip", [(0, 1), (1, 0)])


def next_wide(value, hops=1):
    count = lax.axis_size("wide")
    return lax.ppermute(value, "wide", [(i, (i + hops) % count) for i in range(count)])


def half_of(units):
    return max(units // 2 // 8 * 8, 1)


def gate(value):
    return lax.optimization_barrier(value)


def spread_pair(block):
    cut = half_of(block.shape[0])
    by_x = swap_pair(block, 1)
    by_y = swap_pair(block, 2)
    upper = swap_pair(by_y[:cut], 1)
    lower = swap_pair(by_x[cut:], 2)
    return [block, by_x, by_y, jnp.concatenate([upper, lower], axis=0)]


def product_kernel(pair_ref, x_ref, own_ref, by_x_ref, by_y_ref, *refs):
    pair = pair_ref[0]
    diag_refs, out_ref = refs[:-1], refs[-1]
    out = nn(own_ref[...], x_ref[pair]) + nn(by_x_ref[...], x_ref[pair ^ 1])
    out = out + nn(by_y_ref[...], x_ref[pair ^ 2])
    start = 0
    for ref in diag_refs:
        stop = start + ref.shape[0]
        out_ref[start:stop, :] = out[start:stop] + nn(ref[...], x_ref[pair ^ 3])
        start = stop


def block_product(row, x_all):
    vmem = pl.BlockSpec(memory_space=pltpu.VMEM)
    pair = lax.axis_index("pair").astype(jnp.int32)[None]
    return pl.pallas_call(
        product_kernel,
        in_specs=[pl.BlockSpec(memory_space=pltpu.SMEM)] + [vmem] * (len(row) + 1),
        out_specs=vmem,
        out_shape=jax.ShapeDtypeStruct((row[0].shape[0], x_all.shape[2]), F32),
        compiler_params=pltpu.CompilerParams(vmem_limit_bytes=32 * 1024 * 1024),
        name="block_product",
    )(pair, x_all, *row)


def gather_ring(block, prepare, second):
    count = lax.axis_size("wide")
    if count > LONGEST_RING:
        line = lax.all_gather(block, "wide", axis=0, tiled=True)
        spread = [jnp.split(item, count) for item in spread_pair(jnp.concatenate(mirror(line)))]
        blocks = list(zip(*spread))
        x_all = jnp.concatenate(prepare(), axis=2)
        products = [block_product(row, x_all) for row in blocks]
        line = mirror(lax.all_gather(second, "wide", axis=0, tiled=True))
        return blocks, products, line, x_all
    cut = half_of(block.shape[0])
    ring, by_x, by_y, upper, lower, products = [block], [], [], [], [], []
    halves = prepare()
    for step in range(count + 1):
        moved = {}
        if step < count:
            moved["x"] = swap_pair(ring[step], 1)
            moved["y"] = swap_pair(ring[step], 2)
        if step < count - 1:
            moved["z"] = next_wide(ring[step])
        if step > 0:
            moved["u"] = swap_pair(by_y[step - 1][:cut], 1)
            moved["l"] = swap_pair(by_x[step - 1][cut:], 2)
        if step == 0:
            moved["h"] = halves
        if step == count - 2:
            moved["s"] = second
        if step > 1 and step > count - 2:
            moved["d"] = next_wide(seconds[-1])
        if step == 2:
            moved["a"] = jnp.concatenate(halves, axis=2)
        if step > 2:
            done = step - 3
            row = (ring[done], by_x[done], by_y[done], upper[done], lower[done])
            moved["p"] = block_product(row, x_all)
        moved = gate(moved)
        if "z" in moved:
            ring.append(moved["z"])
        if "x" in moved:
            by_x.append(moved["x"])
            by_y.append(moved["y"])
        if "u" in moved:
            upper.append(moved["u"])
            lower.append(moved["l"])
        if "s" in moved:
            seconds = [moved["s"]]
        if "d" in moved:
            seconds.append(moved["d"])
        halves = moved.get("h", halves)
        x_all = moved.get("a", None) if step <= 2 else x_all
        if "p" in moved:
            products.append(moved["p"])
    blocks = list(zip(ring, by_x, by_y, upper, lower))
    products += [block_product(row, x_all) for row in blocks[len(products) :]]
    while len(seconds) < count:
        seconds.append(next_wide(seconds[-1]))
    return blocks, products, seconds, x_all


def split_kernel(chip_ref, cells_ref, mine_ref, other_ref):
    blocks = 2 * mine_ref.shape[0]
    total = cells_ref.shape[0]
    rows = total // blocks
    chip = chip_ref[0]
    tail = jnp.zeros((mine_ref.shape[1] - rows, cells_ref.shape[1]), F32)
    for block in range(blocks):
        start = block * rows
        first = start // 16 * 16
        last = min(-(-(start + rows) // 16) * 16, total)
        window = cells_ref[first:last, :].astype(F32)
        piece = window[start - first : start - first + rows]
        piece = jnp.concatenate([piece, tail], axis=0).astype(BF)

        @pl.when(chip == block % 2)
        def _():
            mine_ref[block // 2] = piece

        @pl.when(chip != block % 2)
        def _():
            other_ref[block // 2] = piece


def split_cells(cells_t, pairs, padded):
    vmem = pl.BlockSpec(memory_space=pltpu.VMEM)
    shape = jax.ShapeDtypeStruct((pairs, padded, cells_t.shape[1]), BF)
    return pl.pallas_call(
        split_kernel,
        in_specs=[pl.BlockSpec(memory_space=pltpu.SMEM), vmem],
        out_specs=[vmem, vmem],
        out_shape=[shape, shape],
        compiler_params=pltpu.CompilerParams(vmem_limit_bytes=40 * 1024 * 1024),
        name="split_cells",
    )(lax.axis_index("chip").astype(jnp.int32)[None], cells_t)


def unpack_kernel(where_ref, mine_ref, other_ref, *outs, starts, places):
    chip = where_ref[0]
    count, pairs = mine_ref.shape[:2]
    for w in range(count):
        for p in range(pairs):

            def put(ref, c):
                for out, start, place in zip(outs, starts, places):
                    at, width = place[2 * p + c]
                    out[w, :, at : at + width] = ref[w, p, :, start : start + width]

            for c in range(2):

                @pl.when(chip == c)
                def _():
                    put(mine_ref, c)
                    put(other_ref, 1 - c)


def unpack_small(mine, other, widths, totals):
    count, pairs = lax.axis_size("wide"), lax.axis_size("pair")
    shape = (count, pairs) + mine.shape[1:]
    where = lax.axis_index("chip").astype(jnp.int32)[None]
    starts = [sum(widths[:i]) for i in range(len(widths))]
    places = [
        [(min(block * width, total - width), width) for block in range(2 * pairs)]
        for width, total in zip(widths, totals)
    ]
    vmem = pl.BlockSpec(memory_space=pltpu.VMEM)
    outs = pl.pallas_call(
        functools.partial(unpack_kernel, starts=starts, places=places),
        in_specs=[pl.BlockSpec(memory_space=pltpu.SMEM), vmem, vmem],
        out_specs=[vmem] * len(widths),
        out_shape=[jax.ShapeDtypeStruct((count, shape[2], total), BF) for total in totals],
        compiler_params=pltpu.CompilerParams(vmem_limit_bytes=32 * 1024 * 1024),
        name="unpack_small",
    )(where, mine.reshape(shape), other.reshape(shape))
    return [item.reshape(count * shape[2], -1) for item in outs]


def send_odd(blocks):
    count = lax.axis_size("wide")
    if count > LONGEST_RING:
        order = jnp.stack(list(blocks)[-1:] + list(blocks)[:-1])
        line = jnp.stack(mirror(order.reshape((-1,) + order.shape[2:])))
        return [gate(lax.psum_scatter(line, "wide", scatter_dimension=0, tiled=True))[0]]
    return [next_wide(blocks[k - 1].astype(BF), -k) for k in range(1, count, 2)]


def send_even(blocks):
    count = lax.axis_size("wide")
    if count > LONGEST_RING:
        return []
    return [next_wide(blocks[k - 1].astype(BF), -k) for k in range(2, count, 2)]


def add_wide(blocks, odd, even):
    terms = list(odd) + list(even)
    if lax.axis_size("wide") <= LONGEST_RING:
        terms = list(blocks)[-1:] + terms
    return sum(item.astype(F32) for item in terms)


def scatter_wide(blocks):
    return add_wide(blocks, send_odd(blocks), send_even(blocks))


def add_low(*terms):
    return sum(item.astype(F32) for item in terms).astype(BF)


def far_first(value):
    blocks = mirror(value)
    return blocks[1:] + blocks[:1]


def mirror(value):
    count = lax.axis_size("wide")
    me = lax.axis_index("wide")
    shaped = value.reshape((count, value.shape[0] // count) + value.shape[1:])
    return [
        lax.dynamic_index_in_dim(shaped, lax.rem(me - s + count, count), 0, keepdims=False)
        for s in range(count)
    ]


def share(value, axes=ALL):
    count = lax.axis_size(axes)
    return lax.all_to_all(
        jnp.broadcast_to(value[None], (count,) + value.shape), axes, 0, 0, tiled=True
    )


def pack_kernel(*refs):
    out_ref = refs[-1]
    chips, pairs, wide, units, _ = out_ref.shape
    start = 0
    operands = list(zip(refs[:-1:2], refs[1:-1:2]))
    for left_ref, right_ref in operands:
        whole = right_ref is operands[-1][1]
        rows = right_ref.shape[0] // (1 if whole else pairs * chips)
        product = nt(left_ref[...], right_ref[...])
        for w in range(wide):
            for p in range(pairs):
                for c in range(chips):
                    at = 0 if whole else (p * chips + c) * rows
                    piece = product[w * units : (w + 1) * units, at : at + rows]
                    out_ref[c, p, w, :, start : start + rows] = piece.astype(BF)
        start += rows
    out_ref[:, :, :, :, start:] = jnp.zeros(out_ref.shape[:4] + (out_ref.shape[4] - start,), BF)


def pack_grads(*operands):
    wide, pairs = lax.axis_size("wide"), lax.axis_size("pair")
    rows = sum(item.shape[0] for item in operands[1:-1:2]) // (2 * pairs) + operands[-1].shape[0]
    shape = (2, pairs, wide, operands[0].shape[0] // wide, -(-rows // 128) * 128)
    return pl.pallas_call(
        pack_kernel,
        out_shape=jax.ShapeDtypeStruct(shape, BF),
        compiler_params=pltpu.CompilerParams(vmem_limit_bytes=40 * 1024 * 1024),
        name="pack_grads",
    )(*operands)


def add_chip(blocks):
    chip = lax.axis_index("chip")
    keep = lax.dynamic_index_in_dim(blocks, chip, 0, keepdims=False)
    send = lax.dynamic_index_in_dim(blocks, 1 - chip, 0, keepdims=False)
    return add_low(keep, swap_chip(send))


def input_kernel(*refs, scale):
    weights, (d_ref, kept_ref, own_ref, send_ref) = refs[:-4], refs[-4:]
    cells = own_ref.shape[1]
    grad, s, start = 0.0, 0, 0
    for weight in weights:
        rows = weight.shape[0]
        grad = grad + tn(weight[...], d_ref[s][start : start + rows])
        start += rows
        if start == d_ref.shape[1]:
            s, start = s + 1, 0
    grad = grad * scale - kept_ref[0].astype(F32)
    own_ref[...] = grad[:, :cells].astype(BF)
    send_ref[...] = grad[:, cells:].astype(BF)


def input_rows(weights, d_rel, kept, rel, scale):
    _, genes, cells = kept.shape
    half = jax.ShapeDtypeStruct((genes, cells // 2), BF)

    def whole(item):
        return pl.BlockSpec(item.shape, lambda i: (0,) * item.ndim)

    return pl.pallas_call(
        functools.partial(input_kernel, scale=scale),
        grid=(1,),
        in_specs=[whole(item) for item in weights]
        + [whole(d_rel), pl.BlockSpec((1, genes, cells), lambda i: (rel, 0, 0))],
        out_specs=[whole(half)] * 2,
        out_shape=[half, half],
        compiler_params=pltpu.CompilerParams(vmem_limit_bytes=32 * 1024 * 1024),
        name="input_rows",
    )(*weights, d_rel, kept)


def plane_kernel(wide_ref, *refs):
    pairs = 4
    d_refs, swap_refs, x_refs = (refs[i * pairs : (i + 1) * pairs] for i in range(3))
    outs = refs[3 * pairs :]
    count, _, cells = d_refs[0].shape
    for k, out in enumerate(outs, 1):
        w = lax.rem(wide_ref[0] + count - k, count)
        total = 0.0
        for d_ref, swap_ref, x_ref in zip(d_refs, swap_refs, x_refs):
            total = total + nt(d_ref[w], x_ref[:, :cells])
            total = total + nt(swap_ref[w], x_ref[:, cells:])
        out[...] = total.astype(BF)


def plane_grads(plane, swapped, x_plane):
    count = lax.axis_size("wide")
    shape = (count, plane[0].shape[0] // count, plane[0].shape[1])
    vmem = pl.BlockSpec(memory_space=pltpu.VMEM)
    where = lax.axis_index("wide").astype(jnp.int32)[None]
    return pl.pallas_call(
        plane_kernel,
        in_specs=[pl.BlockSpec(memory_space=pltpu.SMEM)] + [vmem] * (3 * len(plane)),
        out_specs=[vmem] * count,
        out_shape=[jax.ShapeDtypeStruct((shape[1], x_plane[0].shape[0]), BF)] * count,
        compiler_params=pltpu.CompilerParams(vmem_limit_bytes=48 * 1024 * 1024),
        name="plane_grads",
    )(where, *[item.reshape(shape) for item in list(plane) + list(swapped)], *x_plane)


def place_kernel(where_ref, own_ref, came_ref, out_ref):
    pair, chip = where_ref[0], where_ref[1]
    pairs = own_ref.shape[0]
    rows = out_ref.shape[0] // (2 * pairs)
    for p in range(pairs):
        rel = pair ^ p
        for c in range(2):
            at = pl.ds((2 * p + c) * rows, rows)

            @pl.when(chip == c)
            def _():
                out_ref[at, :] = own_ref[rel, :rows, :].astype(F32)

            @pl.when(chip != c)
            def _():
                out_ref[at, :] = came_ref[rel, :rows, :].astype(F32)


def place_rows(own, came, genes):
    where = jnp.stack([lax.axis_index("pair"), lax.axis_index("chip")]).astype(jnp.int32)
    return pl.pallas_call(
        place_kernel,
        in_specs=[
            pl.BlockSpec(memory_space=pltpu.SMEM),
            pl.BlockSpec(memory_space=pltpu.VMEM),
            pl.BlockSpec(memory_space=pltpu.VMEM),
        ],
        out_specs=pl.BlockSpec(memory_space=pltpu.VMEM),
        out_shape=jax.ShapeDtypeStruct((genes, own.shape[2]), F32),
        compiler_params=pltpu.CompilerParams(vmem_limit_bytes=40 * 1024 * 1024),
        name="place_rows",
    )(where, own, came)


def normalize(pre_act, gain, shift, rider=()):
    cells = pre_act.shape[1]
    count = lax.axis_size(ALL)
    local_mean = jnp.mean(pre_act, axis=1)
    local_square = jnp.sum(jnp.square(pre_act - local_mean[:, None]), axis=1)
    every, rider = gate((share(jnp.stack([local_mean, local_square])), rider))
    centre = jnp.mean(every[:, 0], axis=0)
    squares = jnp.sum(every[:, 1], axis=0) + cells * jnp.sum(
        jnp.square(every[:, 0] - centre), axis=0
    )
    variance = squares / (cells * count)
    inverse = lax.rsqrt(variance + EPSILON)
    scaled = (pre_act - centre[:, None]) * inverse[:, None]
    normed = None if gain is None else scaled * gain[:, None] + shift[:, None]
    return normed, scaled, inverse, centre, variance, rider


def norm_backward(upstream, normed, scaled, inverse, gain, extra=None, pieces=None, rider=()):
    count = lax.axis_size(ALL)
    units, cells = upstream.shape
    count_all = cells * count
    gate_value = jax.nn.sigmoid(normed)
    back_normed = upstream * gate_value * (1.0 + normed * (1.0 - gate_value))
    sums = [jnp.sum(back_normed, axis=1), jnp.sum(back_normed * scaled, axis=1)]
    if extra is not None:
        sums.append(extra)
    sums = jnp.concatenate(sums)
    sent = jnp.broadcast_to(sums[None], (count,) + sums.shape)
    if pieces is not None:
        sent = jnp.concatenate([sent, pieces], axis=1)
    every, rider = gate((lax.all_to_all(sent, ALL, 0, 0, tiled=True), rider))
    both = jnp.sum(every[:, : 2 * units], axis=0)
    shift_sum, gain_sum = both[:units], both[units:]
    back_pre = (gain * inverse)[:, None] * (
        back_normed - (shift_sum / count_all)[:, None] - scaled * (gain_sum / count_all)[:, None]
    )
    return back_pre.astype(BF), gain_sum, shift_sum, every[:, 2 * units :], rider


def output_kernel(
    pair_ref,
    h_ref,
    weight_ref,
    x_ref,
    mask_ref,
    indicator_ref,
    bias_ref,
    back_ref,
    kept_ref,
    bias_sum_ref,
    loss_ref,
    *refs,
    inv_count,
):
    grad_ref, out_ref, keep_ref, low_ref = refs
    step = pl.program_id(0)
    units, cells = h_ref.shape
    genes = x_ref.shape[1]
    weight = weight_ref[:, 0].reshape(units, genes)
    out_ref[...] = tn(weight, h_ref[...])
    keep_ref[...] = tn(mask_ref[0], indicator_ref[...])

    @pl.when(step == 0)
    def _():
        loss_ref[...] = jnp.zeros_like(loss_ref)

    rows = 64

    def chunk(i, total):
        at = pl.ds(pl.multiple_of(i * rows, rows), rows)
        out_pre = out_ref[at, :] + bias_ref[0, at, :]
        small = jnp.exp(-jnp.abs(out_pre))
        recon = jnp.maximum(out_pre, 0.0) + jnp.log1p(small)
        slope = jnp.where(out_pre >= 0, 1.0, small) / (1.0 + small)
        diff = recon - x_ref[0, at, :].astype(F32)
        kept = keep_ref[at, :] * diff
        low = (kept * slope * inv_count).astype(BF)
        kept_ref[0, at, :] = kept.astype(BF)
        low_ref[at, :] = low
        return total + jnp.sum(kept * diff, axis=0, keepdims=True)

    loss_ref[...] += lax.fori_loop(0, genes // rows, chunk, jnp.zeros((1, cells), F32), unroll=True)
    low = low_ref[...]
    bias_sum_ref[0] = nt(jnp.ones((8, cells), BF), low)
    grad_ref[...] = nt(h_ref[...], low).astype(BF).reshape(grad_ref.shape)
    back = nn(weight, low)

    @pl.when(step == 0)
    def _():
        back_ref[...] = back

    @pl.when(step > 0)
    def _():
        back_ref[...] += back


def output_layer(pair, hidden, weight, x_all, mask, indicator, bias, inv_count):
    units, cells = hidden.shape
    wide, pairs, block_units, genes = weight.shape
    labels = mask.shape[1]
    return pl.pallas_call(
        functools.partial(output_kernel, inv_count=inv_count),
        grid_spec=pltpu.PrefetchScalarGridSpec(
            num_scalar_prefetch=1,
            grid=(pairs,),
            in_specs=[
                pl.BlockSpec((units, cells), lambda r, me: (0, 0)),
                pl.BlockSpec((wide, 1, block_units, genes), lambda r, me: (0, me[0] ^ r, 0, 0)),
                pl.BlockSpec((1, genes, cells), lambda r, me: (me[0] ^ r, 0, 0)),
                pl.BlockSpec((1, labels, genes), lambda r, me: (me[0] ^ r, 0, 0)),
                pl.BlockSpec((labels, cells), lambda r, me: (0, 0)),
                pl.BlockSpec((1, genes, 1), lambda r, me: (me[0] ^ r, 0, 0)),
            ],
            out_specs=[
                pl.BlockSpec((units, cells), lambda r, me: (0, 0)),
                pl.BlockSpec((1, genes, cells), lambda r, me: (r, 0, 0)),
                pl.BlockSpec((1, 8, genes), lambda r, me: (me[0] ^ r, 0, 0)),
                pl.BlockSpec((1, cells), lambda r, me: (0, 0)),
                pl.BlockSpec((1, wide, block_units, genes), lambda r, me: (me[0] ^ r, 0, 0, 0)),
            ],
            scratch_shapes=[
                pltpu.VMEM((genes, cells), F32),
                pltpu.VMEM((genes, cells), F32),
                pltpu.VMEM((genes, cells), BF),
            ],
        ),
        out_shape=[
            jax.ShapeDtypeStruct((units, cells), F32),
            jax.ShapeDtypeStruct((pairs, genes, cells), BF),
            jax.ShapeDtypeStruct((pairs, 8, genes), F32),
            jax.ShapeDtypeStruct((1, cells), F32),
            jax.ShapeDtypeStruct((pairs, wide, block_units, genes), BF),
        ],
        compiler_params=pltpu.CompilerParams(vmem_limit_bytes=48 * 1024 * 1024),
        cost_estimate=pl.CostEstimate(
            flops=36 * units * cells * genes * pairs,
            bytes_accessed=48 * units * genes * pairs,
            transcendentals=3 * cells * genes * pairs,
        ),
        name="output_layer",
    )(pair[None], hidden, weight, x_all, mask, indicator, bias)


def on_device(
    expression,
    noise,
    study,
    measured_gene_mask,
    encoder_input_weight,
    enc_mid,
    heads,
    dec_in,
    dec_mid,
    dec_out,
    norm_params,
    head_bias,
    out_bias,
    running_stats,
):
    wide_count = lax.axis_size("wide")
    row_split = lax.axis_size(("pair", "chip"))
    pair_count = lax.axis_size("pair")
    cells, genes = expression.shape
    count_all = cells * lax.axis_size(ALL)
    inv_count = 1.0 / count_all
    latent = dec_in.shape[0]
    block_genes, block_units = encoder_input_weight.shape
    units = block_units * wide_count
    pair = lax.axis_index("pair")
    chip = lax.axis_index("chip")
    block_id = pair * 2 + chip

    piece = -(-latent // row_split)
    piece_start = jnp.minimum(piece * block_id, latent - piece)
    dec_in_piece = lax.dynamic_slice_in_dim(dec_in, piece_start, piece, 0)
    packed = jnp.concatenate(
        [enc_mid.T, dec_mid.T, heads.T, dec_in_piece.T, norm_params.T], axis=1
    )
    packed = jnp.pad(packed, ((0, 0), (0, 256 - packed.shape[1])))
    mid_rows = enc_mid.shape[0]
    head_rows = heads.shape[0]
    widths = (mid_rows, mid_rows, head_rows, piece, norm_params.shape[0])
    totals = (units, units, 2 * latent, latent, 8)
    padded = -(-block_genes // 128) * 128
    extra = padded - block_genes
    def own_blocks(rows, axis):
        shape = rows.shape[:axis] + (pair_count, 2, block_genes) + rows.shape[axis + 1 :]
        cut = lax.dynamic_index_in_dim(rows.reshape(shape), chip, axis + 1, keepdims=False)
        widths = [(0, 0)] * cut.ndim
        widths[axis + 1] = (0, extra)
        return jnp.pad(cut, widths)

    def prepare():
        x_mine, x_send = split_cells(expression.T, pair_count, padded)
        return x_mine, swap_chip(x_send)

    labels = measured_gene_mask.shape[0]
    indicator = (jnp.arange(labels, dtype=jnp.int32)[:, None] == study[None, :]).astype(BF)
    indicator = jnp.concatenate([indicator, swap_chip(indicator)], axis=1)
    mask_all = own_blocks(measured_gene_mask.astype(BF), 1).transpose(1, 0, 2)
    bias_all = own_blocks(out_bias, 0)[:, :, None]

    enc_block = jnp.pad(encoder_input_weight.T, ((0, 0), (0, extra)))
    dec_block = jnp.pad(dec_out.T, ((0, 0), (0, extra)))
    mine = lax.all_gather(packed, ("wide", "pair"))
    enc_blocks, rel_pre, dec_line, x_all = gather_ring(enc_block, prepare, dec_block)
    mids = unpack_small(mine, swap_chip(mine), widths, totals)
    part_one = jnp.concatenate(rel_pre, axis=0)
    x_rel = [
        lax.dynamic_index_in_dim(x_all, pair ^ r, 0, keepdims=False) for r in range(pair_count)
    ]
    part_one, dec_line, x_rel = gate((part_one, dec_line, x_rel))
    x_near = [swap_pair(x_rel[r], r) for r in range(1, pair_count - 1)]
    pre_one = part_one[:, :cells] + swap_chip(part_one[:, cells:])
    pre_one = jnp.concatenate(mirror(pre_one), axis=0)
    dec_line = jnp.concatenate(mirror(jnp.concatenate(dec_line)))
    dec_all = lax.all_gather(
        dec_line.reshape(wide_count, block_units, padded), "pair", axis=1
    )
    normed_one, scaled_one, inverse_one, centre_one, spread_one, (mids, x_near) = normalize(
        pre_one, None, None, (mids, x_near)
    )
    w_enc_mid, w_dec_mid, w_heads, w_dec_in, norm_full = mids
    norm_full = norm_full.astype(F32)
    gains = [norm_full[:, k] for k in range(4)]
    shifts = [norm_full[:, 4 + k] for k in range(4)]
    normed_one = scaled_one * gains[0][:, None] + shifts[0][:, None]
    hidden_one = jax.nn.silu(normed_one).astype(BF)

    pre_two = nn(w_enc_mid, hidden_one)
    normed_two, scaled_two, inverse_two, centre_two, spread_two, _ = normalize(
        pre_two, gains[1], shifts[1]
    )
    hidden_two = jax.nn.silu(normed_two).astype(BF)
    encoded = tn(w_heads, hidden_two) + head_bias[:, None]
    latent_mean = encoded[:latent]
    logvar = encoded[latent:]
    noise_t = noise.T
    spread_factor = jnp.exp(0.5 * logvar)
    code = (latent_mean + spread_factor * noise_t).astype(BF)
    pre_three = nn(w_dec_in, code)
    normed_three, scaled_three, inverse_three, centre_three, spread_three, _ = normalize(
        pre_three, gains[2], shifts[2]
    )
    hidden_three = jax.nn.silu(normed_three).astype(BF)
    pre_four = nn(w_dec_mid, hidden_three)
    normed_four, scaled_four, inverse_four, centre_four, spread_four, _ = normalize(
        pre_four, gains[3], shifts[3]
    )
    hidden_four = jax.nn.silu(normed_four).astype(BF)

    h_chip = jnp.concatenate([hidden_four, swap_chip(hidden_four)], axis=1)
    back_all, kept_diff, bias_sums, recon_sums, dec_parts = output_layer(
        pair.astype(jnp.int32),
        h_chip,
        dec_all,
        x_all,
        mask_all,
        indicator,
        bias_all,
        inv_count,
    )
    exp_logvar = jnp.exp(logvar)
    kl_sum = jnp.sum(exp_logvar + latent_mean * latent_mean - 1.0 - logvar)
    loss_local = 0.5 * jnp.sum(recon_sums) + (0.5 * ALPHA) * kl_sum
    back_four = back_all[:, :cells] + swap_chip(back_all[:, cells:])

    bias_rows = jnp.zeros((pair_count, 2, block_genes), F32)
    bias_rows = lax.dynamic_update_slice_in_dim(
        bias_rows, bias_sums[:, :1, :block_genes], chip, 1
    ).reshape(-1)
    devices = lax.axis_size(ALL)
    share_size = -(-genes // (devices * 8)) * 8
    bias_rows = jnp.pad(bias_rows, (0, devices * share_size - genes)).reshape(devices, share_size)
    dec_line = lax.psum_scatter(dec_parts, "pair", scatter_dimension=0, tiled=True)
    bp_four, gain_four, shift_four, _, _ = norm_backward(
        back_four, normed_four, scaled_four, inverse_four, gains[3]
    )

    back_three = tn(w_dec_mid, bp_four)
    bp_three, gain_three, shift_three, rest, x_far = norm_backward(
        back_three,
        normed_three,
        scaled_three,
        inverse_three,
        gains[2],
        loss_local[None],
        bias_rows,
        rider=swap_pair(x_rel[3][: padded // 2], 3),
    )
    loss = jnp.sum(rest[:, 0]) * inv_count
    bias_share = jnp.sum(rest[:, 1:], axis=0)
    back_code = tn(w_dec_in, bp_three)
    back_mean = back_code + ALPHA * inv_count * latent_mean
    back_logvar = (
        back_code * noise_t * spread_factor * 0.5
        + (ALPHA * 0.5 * inv_count) * (exp_logvar - 1.0)
    )
    back_enc = jnp.concatenate([back_mean, back_logvar], axis=0).astype(BF)
    head_sum = jnp.sum(back_enc.astype(F32), axis=1)
    back_two = nn(w_heads, back_enc)
    bp_two, gain_two, shift_two, rest, _ = norm_backward(
        back_two, normed_two, scaled_two, inverse_two, gains[1], jnp.concatenate([head_sum, bias_share])
    )
    head_bias_grad = jnp.sum(rest[:, : 2 * latent], axis=0)
    out_bias_grad = rest[:, 2 * latent :].reshape(-1)[:genes]

    back_one = tn(w_enc_mid, bp_two)
    x_last = swap_pair(x_rel[3][padded // 2 :], 3)
    bp_one, gain_one, shift_one, _, (dec_line, x_last) = norm_backward(
        back_one, normed_one, scaled_one, inverse_one, gains[0], rider=(dec_line, x_last)
    )

    dec_blocks = far_first(dec_line.reshape(units, padded))
    mid_in = gate((bp_four, hidden_three, bp_two, hidden_one, hidden_two, back_enc, bp_three, code, bp_one))
    packs = pack_grads(*mid_in[:8])
    d_other = swap_chip(bp_one)
    late_blocks, d_own = gate((enc_blocks, jnp.concatenate([bp_one, d_other], axis=1)))
    d_rel = far_first(d_own)
    d_rel = jnp.stack(d_rel[-1:] + d_rel[:-1])
    if wide_count > LONGEST_RING:
        late_blocks = [[jnp.concatenate(item) for item in zip(*late_blocks)]]
        d_rel = d_rel.reshape(1, units, 2 * cells)
    own_rows, send_rows = zip(
        *[
            input_rows(
                [item for row in late_blocks for item in (row[3:] if r == 3 else row[r : r + 1])],
                d_rel,
                kept_diff,
                r,
                count_all,
            )
            for r in range(pair_count)
        ]
    )
    own_rows, send_rows = jnp.stack(own_rows), jnp.stack(send_rows)
    d_near, d_other, own_rows, send_rows, dec_blocks, packs, dec_near, x_far = gate(
        (
            [bp_one] + [swap_pair(bp_one, r) for r in range(1, pair_count)],
            d_other,
            own_rows,
            send_rows,
            dec_blocks,
            packs,
            send_odd(dec_blocks),
            jnp.concatenate([x_far, x_last]),
        )
    )
    dec_far = send_even(dec_blocks)
    d_swap = [d_other] + [swap_chip(item) for item in d_near[1:]]
    mid_line = lax.psum_scatter(add_chip(packs), "pair", scatter_dimension=0, tiled=True)
    enc_low = plane_grads(d_near, d_swap, [x_rel[0]] + x_near + [x_far])
    late_rows = [gain_one, gain_two, gain_three, gain_four]
    late_rows += [shift_one, shift_two, shift_three, shift_four]
    late_rows += [centre_one, centre_two, centre_three, centre_four]
    late_rows += [spread_one, spread_two, spread_three, spread_four]
    enc_near, enc_far, mid_line, late_rows, dec_far = gate(
        (send_odd(enc_low), send_even(enc_low), mid_line, late_rows, dec_far)
    )
    enc_in_grad = add_wide(enc_low, enc_near, enc_far)
    dec_out_grad = add_wide(dec_blocks, dec_near, dec_far)
    mid_sum = scatter_wide(far_first(mid_line.reshape(units, mid_line.shape[3])))
    input_grad = place_rows(own_rows, swap_chip(send_rows), genes).T

    wide_index = lax.axis_index("wide")
    per_row = 8 // row_split

    def mine_of(rows_full):
        stacked = jnp.stack(rows_full)
        return lax.dynamic_slice(
            stacked, (block_id * per_row, wide_index * block_units), (per_row, block_units)
        )

    norm_grad = mine_of(late_rows[:8])
    unbias = count_all / (count_all - 1.0)
    stats = mine_of(late_rows[8:12] + [item * unbias for item in late_rows[12:]])
    running_next = (1.0 - MOMENTUM) * running_stats + MOMENTUM * stats

    dec_mid_grad = mid_sum[:, :mid_rows]
    enc_mid_grad = mid_sum[:, mid_rows : 2 * mid_rows]
    in_start = 2 * mid_rows + head_rows
    heads_grad = mid_sum[:, 2 * mid_rows : in_start]
    dec_in_grad = mid_sum[:, in_start : in_start + latent].T
    enc_in_grad = enc_in_grad[:, :block_genes]


    return (
        loss,
        input_grad,
        enc_in_grad.T,
        enc_mid_grad.T,
        heads_grad.T,
        dec_in_grad,
        dec_mid_grad.T,
        dec_out_grad[:, :block_genes].T,
        norm_grad,
        head_bias_grad,
        out_bias_grad,
        running_next,
    )


def solution(mesh):
    split = P(("pair", "chip"), "wide")
    by_cell = P(("wide", "pair", "chip"), None)
    return jax.shard_map(
        on_device,
        mesh=mesh,
        in_specs=(
            by_cell,
            by_cell,
            P(("wide", "pair", "chip")),
            P(),
            split,
            split,
            split,
            P(None, "wide"),
            split,
            split,
            split,
            P(),
            P(),
            split,
        ),
        out_specs=(
            P(),
            by_cell,
            split,
            split,
            split,
            P(None, "wide"),
            split,
            split,
            split,
            P(),
            P(),
            split,
        ),
        check_vma=False,
    )
```

```python
import functools

import jax
import jax.numpy as jnp
from jax import lax
from jax.experimental import pallas as pl
from jax.experimental.pallas import tpu as pltpu
from jax.sharding import PartitionSpec as P

ALPHA = 0.005
EPSILON = 1e-05
MOMENTUM = 0.1
LONGEST_RING = 4
ALL = ("wide", "pair", "chip")
BF = jnp.bfloat16
F32 = jnp.float32


def dot(left, right, dims):
    return lax.dot_general(left, right, (dims, ((), ())), preferred_element_type=F32)


def nn(left, right):
    return dot(left, right, ((1,), (0,)))


def nt(left, right):
    return dot(left, right, ((1,), (1,)))


def tn(left, right):
    return dot(left, right, ((0,), (0,)))


def swap_pair(value, bits):
    count = lax.axis_size("pair")
    return lax.ppermute(value, "pair", [(i, i ^ bits) for i in range(count)])


def swap_chip(value):
    return lax.ppermute(value, "chip", [(0, 1), (1, 0)])


def next_wide(value, hops=1):
    count = lax.axis_size("wide")
    return lax.ppermute(value, "wide", [(i, (i + hops) % count) for i in range(count)])


def half_of(units):
    return max(units // 2 // 8 * 8, 1)


def gate(value):
    return lax.optimization_barrier(value)


def spread_pair(block):
    cut = half_of(block.shape[0])
    by_x = swap_pair(block, 1)
    by_y = swap_pair(block, 2)
    upper = swap_pair(by_y[:cut], 1)
    lower = swap_pair(by_x[cut:], 2)
    return [block, by_x, by_y, jnp.concatenate([upper, lower], axis=0)]


def product_kernel(pair_ref, x_ref, own_ref, by_x_ref, by_y_ref, *refs):
    pair = pair_ref[0]
    diag_refs, out_ref = refs[:-1], refs[-1]
    out = nn(own_ref[...], x_ref[pair]) + nn(by_x_ref[...], x_ref[pair ^ 1])
    out = out + nn(by_y_ref[...], x_ref[pair ^ 2])
    start = 0
    for ref in diag_refs:
        stop = start + ref.shape[0]
        out_ref[start:stop, :] = out[start:stop] + nn(ref[...], x_ref[pair ^ 3])
        start = stop


def block_product(row, x_all):
    vmem = pl.BlockSpec(memory_space=pltpu.VMEM)
    pair = lax.axis_index("pair").astype(jnp.int32)[None]
    return pl.pallas_call(
        product_kernel,
        in_specs=[pl.BlockSpec(memory_space=pltpu.SMEM)] + [vmem] * (len(row) + 1),
        out_specs=vmem,
        out_shape=jax.ShapeDtypeStruct((row[0].shape[0], x_all.shape[2]), F32),
        compiler_params=pltpu.CompilerParams(vmem_limit_bytes=32 * 1024 * 1024),
        name="block_product",
    )(pair, x_all, *row)


def gather_ring(block, prepare, second):
    count = lax.axis_size("wide")
    if count > LONGEST_RING:
        line = lax.all_gather(block, "wide", axis=0, tiled=True)
        spread = [jnp.split(item, count) for item in spread_pair(jnp.concatenate(mirror(line)))]
        blocks = list(zip(*spread))
        x_all = jnp.concatenate(prepare(), axis=2)
        products = [block_product(row, x_all) for row in blocks]
        line = mirror(lax.all_gather(second, "wide", axis=0, tiled=True))
        return blocks, products, line, x_all
    cut = half_of(block.shape[0])
    ring, by_x, by_y, upper, lower, products = [block], [], [], [], [], []
    halves = prepare()
    for step in range(count + 1):
        moved = {}
        if step < count:
            moved["x"] = swap_pair(ring[step], 1)
            moved["y"] = swap_pair(ring[step], 2)
        if step < count - 1:
            moved["z"] = next_wide(ring[step])
        if step > 0:
            moved["u"] = swap_pair(by_y[step - 1][:cut], 1)
            moved["l"] = swap_pair(by_x[step - 1][cut:], 2)
        if step == 0:
            moved["h"] = halves
        if step == count - 2:
            moved["s"] = second
        if step > 1 and step > count - 2:
            moved["d"] = next_wide(seconds[-1])
        if step == 2:
            moved["a"] = jnp.concatenate(halves, axis=2)
        if step > 2:
            done = step - 3
            row = (ring[done], by_x[done], by_y[done], upper[done], lower[done])
            moved["p"] = block_product(row, x_all)
        moved = gate(moved)
        if "z" in moved:
            ring.append(moved["z"])
        if "x" in moved:
            by_x.append(moved["x"])
            by_y.append(moved["y"])
        if "u" in moved:
            upper.append(moved["u"])
            lower.append(moved["l"])
        if "s" in moved:
            seconds = [moved["s"]]
        if "d" in moved:
            seconds.append(moved["d"])
        halves = moved.get("h", halves)
        x_all = moved.get("a", None) if step <= 2 else x_all
        if "p" in moved:
            products.append(moved["p"])
    blocks = list(zip(ring, by_x, by_y, upper, lower))
    products += [block_product(row, x_all) for row in blocks[len(products) :]]
    while len(seconds) < count:
        seconds.append(next_wide(seconds[-1]))
    return blocks, products, seconds, x_all


def split_kernel(chip_ref, cells_ref, mine_ref, other_ref):
    blocks = 2 * mine_ref.shape[0]
    total = cells_ref.shape[0]
    rows = total // blocks
    chip = chip_ref[0]
    tail = jnp.zeros((mine_ref.shape[1] - rows, cells_ref.shape[1]), F32)
    for block in range(blocks):
        start = block * rows
        first = start // 16 * 16
        last = min(-(-(start + rows) // 16) * 16, total)
        window = cells_ref[first:last, :].astype(F32)
        piece = window[start - first : start - first + rows]
        piece = jnp.concatenate([piece, tail], axis=0).astype(BF)

        @pl.when(chip == block % 2)
        def _():
            mine_ref[block // 2] = piece

        @pl.when(chip != block % 2)
        def _():
            other_ref[block // 2] = piece


def split_cells(cells_t, pairs, padded):
    vmem = pl.BlockSpec(memory_space=pltpu.VMEM)
    shape = jax.ShapeDtypeStruct((pairs, padded, cells_t.shape[1]), BF)
    return pl.pallas_call(
        split_kernel,
        in_specs=[pl.BlockSpec(memory_space=pltpu.SMEM), vmem],
        out_specs=[vmem, vmem],
        out_shape=[shape, shape],
        compiler_params=pltpu.CompilerParams(vmem_limit_bytes=40 * 1024 * 1024),
        name="split_cells",
    )(lax.axis_index("chip").astype(jnp.int32)[None], cells_t)


def unpack_kernel(where_ref, mine_ref, other_ref, *outs, starts, places):
    chip = where_ref[0]
    count, pairs = mine_ref.shape[:2]
    for w in range(count):
        for p in range(pairs):

            def put(ref, c):
                for out, start, place in zip(outs, starts, places):
                    at, width = place[2 * p + c]
                    out[w, :, at : at + width] = ref[w, p, :, start : start + width]

            for c in range(2):

                @pl.when(chip == c)
                def _():
                    put(mine_ref, c)
                    put(other_ref, 1 - c)


def unpack_small(mine, other, widths, totals):
    count, pairs = lax.axis_size("wide"), lax.axis_size("pair")
    shape = (count, pairs) + mine.shape[1:]
    where = lax.axis_index("chip").astype(jnp.int32)[None]
    starts = [sum(widths[:i]) for i in range(len(widths))]
    places = [
        [(min(block * width, total - width), width) for block in range(2 * pairs)]
        for width, total in zip(widths, totals)
    ]
    vmem = pl.BlockSpec(memory_space=pltpu.VMEM)
    outs = pl.pallas_call(
        functools.partial(unpack_kernel, starts=starts, places=places),
        in_specs=[pl.BlockSpec(memory_space=pltpu.SMEM), vmem, vmem],
        out_specs=[vmem] * len(widths),
        out_shape=[jax.ShapeDtypeStruct((count, shape[2], total), BF) for total in totals],
        compiler_params=pltpu.CompilerParams(vmem_limit_bytes=32 * 1024 * 1024),
        name="unpack_small",
    )(where, mine.reshape(shape), other.reshape(shape))
    return [item.reshape(count * shape[2], -1) for item in outs]


def send_odd(blocks):
    count = lax.axis_size("wide")
    if count > LONGEST_RING:
        order = jnp.stack(list(blocks)[-1:] + list(blocks)[:-1])
        line = jnp.stack(mirror(order.reshape((-1,) + order.shape[2:])))
        return [gate(lax.psum_scatter(line, "wide", scatter_dimension=0, tiled=True))[0]]
    return [next_wide(blocks[k - 1].astype(BF), -k) for k in range(1, count, 2)]


def send_even(blocks):
    count = lax.axis_size("wide")
    if count > LONGEST_RING:
        return []
    return [next_wide(blocks[k - 1].astype(BF), -k) for k in range(2, count, 2)]


def add_wide(blocks, odd, even):
    terms = list(odd) + list(even)
    if lax.axis_size("wide") <= LONGEST_RING:
        terms = list(blocks)[-1:] + terms
    return sum(item.astype(F32) for item in terms)


def scatter_wide(blocks):
    return add_wide(blocks, send_odd(blocks), send_even(blocks))


def add_low(*terms):
    return sum(item.astype(F32) for item in terms).astype(BF)


def far_first(value):
    blocks = mirror(value)
    return blocks[1:] + blocks[:1]


def mirror(value):
    count = lax.axis_size("wide")
    me = lax.axis_index("wide")
    shaped = value.reshape((count, value.shape[0] // count) + value.shape[1:])
    return [
        lax.dynamic_index_in_dim(shaped, lax.rem(me - s + count, count), 0, keepdims=False)
        for s in range(count)
    ]


def share(value, axes=ALL):
    count = lax.axis_size(axes)
    return lax.all_to_all(
        jnp.broadcast_to(value[None], (count,) + value.shape), axes, 0, 0, tiled=True
    )


def pack_kernel(*refs):
    out_ref = refs[-1]
    chips, pairs, wide, units, _ = out_ref.shape
    start = 0
    operands = list(zip(refs[:-1:2], refs[1:-1:2]))
    for left_ref, right_ref in operands:
        whole = right_ref is operands[-1][1]
        rows = right_ref.shape[0] // (1 if whole else pairs * chips)
        product = nt(left_ref[...], right_ref[...])
        for w in range(wide):
            for p in range(pairs):
                for c in range(chips):
                    at = 0 if whole else (p * chips + c) * rows
                    piece = product[w * units : (w + 1) * units, at : at + rows]
                    out_ref[c, p, w, :, start : start + rows] = piece.astype(BF)
        start += rows
    out_ref[:, :, :, :, start:] = jnp.zeros(out_ref.shape[:4] + (out_ref.shape[4] - start,), BF)


def pack_grads(*operands):
    wide, pairs = lax.axis_size("wide"), lax.axis_size("pair")
    rows = sum(item.shape[0] for item in operands[1:-1:2]) // (2 * pairs) + operands[-1].shape[0]
    shape = (2, pairs, wide, operands[0].shape[0] // wide, -(-rows // 128) * 128)
    return pl.pallas_call(
        pack_kernel,
        out_shape=jax.ShapeDtypeStruct(shape, BF),
        compiler_params=pltpu.CompilerParams(vmem_limit_bytes=40 * 1024 * 1024),
        name="pack_grads",
    )(*operands)


def add_chip(blocks):
    chip = lax.axis_index("chip")
    keep = lax.dynamic_index_in_dim(blocks, chip, 0, keepdims=False)
    send = lax.dynamic_index_in_dim(blocks, 1 - chip, 0, keepdims=False)
    return add_low(keep, swap_chip(send))


def input_kernel(*refs, scale):
    weights, (d_ref, kept_ref, own_ref, send_ref) = refs[:-4], refs[-4:]
    cells = own_ref.shape[1]
    grad, s, start = 0.0, 0, 0
    for weight in weights:
        rows = weight.shape[0]
        grad = grad + tn(weight[...], d_ref[s][start : start + rows])
        start += rows
        if start == d_ref.shape[1]:
            s, start = s + 1, 0
    grad = grad * scale - kept_ref[0].astype(F32)
    own_ref[...] = grad[:, :cells].astype(BF)
    send_ref[...] = grad[:, cells:].astype(BF)


def input_rows(weights, d_rel, kept, rel, scale):
    _, genes, cells = kept.shape
    half = jax.ShapeDtypeStruct((genes, cells // 2), BF)

    def whole(item):
        return pl.BlockSpec(item.shape, lambda i: (0,) * item.ndim)

    return pl.pallas_call(
        functools.partial(input_kernel, scale=scale),
        grid=(1,),
        in_specs=[whole(item) for item in weights]
        + [whole(d_rel), pl.BlockSpec((1, genes, cells), lambda i: (rel, 0, 0))],
        out_specs=[whole(half)] * 2,
        out_shape=[half, half],
        compiler_params=pltpu.CompilerParams(vmem_limit_bytes=32 * 1024 * 1024),
        name="input_rows",
    )(*weights, d_rel, kept)


def plane_kernel(wide_ref, *refs):
    pairs = 4
    d_refs, swap_refs, x_refs = (refs[i * pairs : (i + 1) * pairs] for i in range(3))
    last_ref, *outs = refs[3 * pairs :]
    count, _, cells = d_refs[0].shape
    for k, out in enumerate(outs, 1):
        w = lax.rem(wide_ref[0] + count - k, count)
        total = 0.0
        for d_ref, swap_ref, x_ref in zip(d_refs[:-1], swap_refs, x_refs):
            total = total + nt(d_ref[w], x_ref[:, :cells])
            total = total + nt(swap_ref[w], x_ref[:, cells:])
        start = 0
        for x_ref in (x_refs[-1], last_ref):
            part = nt(d_refs[-1][w], x_ref[:, :cells]) + nt(swap_refs[-1][w], x_ref[:, cells:])
            stop = start + x_ref.shape[0]
            out[:, start:stop] = (total[:, start:stop] + part).astype(BF)
            start = stop


def plane_grads(plane, swapped, x_plane):
    count = lax.axis_size("wide")
    shape = (count, plane[0].shape[0] // count, plane[0].shape[1])
    vmem = pl.BlockSpec(memory_space=pltpu.VMEM)
    where = lax.axis_index("wide").astype(jnp.int32)[None]
    return pl.pallas_call(
        plane_kernel,
        in_specs=[pl.BlockSpec(memory_space=pltpu.SMEM)] + [vmem] * (3 * len(plane) + 1),
        out_specs=[vmem] * count,
        out_shape=[jax.ShapeDtypeStruct((shape[1], x_plane[0].shape[0]), BF)] * count,
        compiler_params=pltpu.CompilerParams(vmem_limit_bytes=48 * 1024 * 1024),
        name="plane_grads",
    )(where, *[item.reshape(shape) for item in list(plane) + list(swapped)], *x_plane)


def place_kernel(where_ref, own_ref, came_ref, out_ref):
    pair, chip = where_ref[0], where_ref[1]
    pairs = own_ref.shape[0]
    rows = out_ref.shape[0] // (2 * pairs)
    for p in range(pairs):
        rel = pair ^ p
        for c in range(2):
            at = pl.ds((2 * p + c) * rows, rows)

            @pl.when(chip == c)
            def _():
                out_ref[at, :] = own_ref[rel, :rows, :].astype(F32)

            @pl.when(chip != c)
            def _():
                out_ref[at, :] = came_ref[rel, :rows, :].astype(F32)


def place_rows(own, came, genes):
    where = jnp.stack([lax.axis_index("pair"), lax.axis_index("chip")]).astype(jnp.int32)
    return pl.pallas_call(
        place_kernel,
        in_specs=[
            pl.BlockSpec(memory_space=pltpu.SMEM),
            pl.BlockSpec(memory_space=pltpu.VMEM),
            pl.BlockSpec(memory_space=pltpu.VMEM),
        ],
        out_specs=pl.BlockSpec(memory_space=pltpu.VMEM),
        out_shape=jax.ShapeDtypeStruct((genes, own.shape[2]), F32),
        compiler_params=pltpu.CompilerParams(vmem_limit_bytes=40 * 1024 * 1024),
        name="place_rows",
    )(where, own, came)


def normalize(pre_act, gain, shift, rider=()):
    cells = pre_act.shape[1]
    count = lax.axis_size(ALL)
    local_mean = jnp.mean(pre_act, axis=1)
    local_square = jnp.sum(jnp.square(pre_act - local_mean[:, None]), axis=1)
    every, rider = gate((share(jnp.stack([local_mean, local_square])), rider))
    centre = jnp.mean(every[:, 0], axis=0)
    squares = jnp.sum(every[:, 1], axis=0) + cells * jnp.sum(
        jnp.square(every[:, 0] - centre), axis=0
    )
    variance = squares / (cells * count)
    inverse = lax.rsqrt(variance + EPSILON)
    scaled = (pre_act - centre[:, None]) * inverse[:, None]
    normed = None if gain is None else scaled * gain[:, None] + shift[:, None]
    return normed, scaled, inverse, centre, variance, rider


def norm_backward(upstream, normed, scaled, inverse, gain, extra=None, pieces=None, rider=()):
    count = lax.axis_size(ALL)
    units, cells = upstream.shape
    count_all = cells * count
    gate_value = jax.nn.sigmoid(normed)
    back_normed = upstream * gate_value * (1.0 + normed * (1.0 - gate_value))
    sums = [jnp.sum(back_normed, axis=1), jnp.sum(back_normed * scaled, axis=1)]
    if extra is not None:
        sums.append(extra)
    sums = jnp.concatenate(sums)
    sent = jnp.broadcast_to(sums[None], (count,) + sums.shape)
    if pieces is not None:
        sent = jnp.concatenate([sent, pieces], axis=1)
    every, rider = gate((lax.all_to_all(sent, ALL, 0, 0, tiled=True), rider))
    both = jnp.sum(every[:, : 2 * units], axis=0)
    shift_sum, gain_sum = both[:units], both[units:]
    back_pre = (gain * inverse)[:, None] * (
        back_normed - (shift_sum / count_all)[:, None] - scaled * (gain_sum / count_all)[:, None]
    )
    return back_pre.astype(BF), gain_sum, shift_sum, every[:, 2 * units :], rider


def output_kernel(
    pair_ref,
    h_ref,
    weight_ref,
    x_ref,
    mask_ref,
    indicator_ref,
    bias_ref,
    back_ref,
    kept_ref,
    bias_sum_ref,
    loss_ref,
    *refs,
    inv_count,
):
    grad_ref, out_ref, keep_ref, low_ref = refs
    step = pl.program_id(0)
    units, cells = h_ref.shape
    genes = x_ref.shape[1]
    weight = weight_ref[:, 0].reshape(units, genes)
    out_ref[...] = tn(weight, h_ref[...])
    keep_ref[...] = tn(mask_ref[0], indicator_ref[...])

    @pl.when(step == 0)
    def _():
        loss_ref[...] = jnp.zeros_like(loss_ref)

    rows = 64

    def chunk(i, total):
        at = pl.ds(pl.multiple_of(i * rows, rows), rows)
        out_pre = out_ref[at, :] + bias_ref[0, at, :]
        small = jnp.exp(-jnp.abs(out_pre))
        recon = jnp.maximum(out_pre, 0.0) + jnp.log1p(small)
        slope = jnp.where(out_pre >= 0, 1.0, small) / (1.0 + small)
        diff = recon - x_ref[0, at, :].astype(F32)
        kept = keep_ref[at, :] * diff
        low = (kept * slope * inv_count).astype(BF)
        kept_ref[0, at, :] = kept.astype(BF)
        low_ref[at, :] = low
        return total + jnp.sum(kept * diff, axis=0, keepdims=True)

    loss_ref[...] += lax.fori_loop(0, genes // rows, chunk, jnp.zeros((1, cells), F32), unroll=True)
    low = low_ref[...]
    bias_sum_ref[0] = nt(jnp.ones((8, cells), BF), low)
    grad_ref[...] = nt(h_ref[...], low).astype(BF).reshape(grad_ref.shape)
    back = nn(weight, low)

    @pl.when(step == 0)
    def _():
        back_ref[...] = back

    @pl.when(step > 0)
    def _():
        back_ref[...] += back


def output_layer(pair, hidden, weight, x_all, mask, indicator, bias, inv_count):
    units, cells = hidden.shape
    wide, pairs, block_units, genes = weight.shape
    labels = mask.shape[1]
    return pl.pallas_call(
        functools.partial(output_kernel, inv_count=inv_count),
        grid_spec=pltpu.PrefetchScalarGridSpec(
            num_scalar_prefetch=1,
            grid=(pairs,),
            in_specs=[
                pl.BlockSpec((units, cells), lambda r, me: (0, 0)),
                pl.BlockSpec((wide, 1, block_units, genes), lambda r, me: (0, me[0] ^ r, 0, 0)),
                pl.BlockSpec((1, genes, cells), lambda r, me: (me[0] ^ r, 0, 0)),
                pl.BlockSpec((1, labels, genes), lambda r, me: (me[0] ^ r, 0, 0)),
                pl.BlockSpec((labels, cells), lambda r, me: (0, 0)),
                pl.BlockSpec((1, genes, 1), lambda r, me: (me[0] ^ r, 0, 0)),
            ],
            out_specs=[
                pl.BlockSpec((units, cells), lambda r, me: (0, 0)),
                pl.BlockSpec((1, genes, cells), lambda r, me: (r, 0, 0)),
                pl.BlockSpec((1, 8, genes), lambda r, me: (me[0] ^ r, 0, 0)),
                pl.BlockSpec((1, cells), lambda r, me: (0, 0)),
                pl.BlockSpec((1, wide, block_units, genes), lambda r, me: (me[0] ^ r, 0, 0, 0)),
            ],
            scratch_shapes=[
                pltpu.VMEM((genes, cells), F32),
                pltpu.VMEM((genes, cells), F32),
                pltpu.VMEM((genes, cells), BF),
            ],
        ),
        out_shape=[
            jax.ShapeDtypeStruct((units, cells), F32),
            jax.ShapeDtypeStruct((pairs, genes, cells), BF),
            jax.ShapeDtypeStruct((pairs, 8, genes), F32),
            jax.ShapeDtypeStruct((1, cells), F32),
            jax.ShapeDtypeStruct((pairs, wide, block_units, genes), BF),
        ],
        compiler_params=pltpu.CompilerParams(vmem_limit_bytes=48 * 1024 * 1024),
        cost_estimate=pl.CostEstimate(
            flops=36 * units * cells * genes * pairs,
            bytes_accessed=48 * units * genes * pairs,
            transcendentals=3 * cells * genes * pairs,
        ),
        name="output_layer",
    )(pair[None], hidden, weight, x_all, mask, indicator, bias)


def on_device(
    expression,
    noise,
    study,
    measured_gene_mask,
    encoder_input_weight,
    enc_mid,
    heads,
    dec_in,
    dec_mid,
    dec_out,
    norm_params,
    head_bias,
    out_bias,
    running_stats,
):
    wide_count = lax.axis_size("wide")
    row_split = lax.axis_size(("pair", "chip"))
    pair_count = lax.axis_size("pair")
    cells, genes = expression.shape
    count_all = cells * lax.axis_size(ALL)
    inv_count = 1.0 / count_all
    latent = dec_in.shape[0]
    block_genes, block_units = encoder_input_weight.shape
    units = block_units * wide_count
    pair = lax.axis_index("pair")
    chip = lax.axis_index("chip")
    block_id = pair * 2 + chip

    piece = -(-latent // row_split)
    piece_start = jnp.minimum(piece * block_id, latent - piece)
    dec_in_piece = lax.dynamic_slice_in_dim(dec_in, piece_start, piece, 0)
    packed = jnp.concatenate(
        [enc_mid.T, dec_mid.T, heads.T, dec_in_piece.T, norm_params.T], axis=1
    )
    packed = jnp.pad(packed, ((0, 0), (0, 256 - packed.shape[1])))
    mid_rows = enc_mid.shape[0]
    head_rows = heads.shape[0]
    widths = (mid_rows, mid_rows, head_rows, piece, norm_params.shape[0])
    totals = (units, units, 2 * latent, latent, 8)
    padded = -(-block_genes // 128) * 128
    extra = padded - block_genes
    def own_blocks(rows, axis):
        shape = rows.shape[:axis] + (pair_count, 2, block_genes) + rows.shape[axis + 1 :]
        cut = lax.dynamic_index_in_dim(rows.reshape(shape), chip, axis + 1, keepdims=False)
        widths = [(0, 0)] * cut.ndim
        widths[axis + 1] = (0, extra)
        return jnp.pad(cut, widths)

    def prepare():
        x_mine, x_send = split_cells(expression.T, pair_count, padded)
        return x_mine, swap_chip(x_send)

    labels = measured_gene_mask.shape[0]
    indicator = (jnp.arange(labels, dtype=jnp.int32)[:, None] == study[None, :]).astype(BF)
    indicator = jnp.concatenate([indicator, swap_chip(indicator)], axis=1)
    mask_all = own_blocks(measured_gene_mask.astype(BF), 1).transpose(1, 0, 2)
    bias_all = own_blocks(out_bias, 0)[:, :, None]

    enc_block = jnp.pad(encoder_input_weight.T, ((0, 0), (0, extra)))
    dec_block = jnp.pad(dec_out.T, ((0, 0), (0, extra)))
    mine = lax.all_gather(packed, ("wide", "pair"))
    enc_blocks, rel_pre, dec_line, x_all = gather_ring(enc_block, prepare, dec_block)
    mids = unpack_small(mine, swap_chip(mine), widths, totals)
    part_one = jnp.concatenate(rel_pre, axis=0)
    x_rel = [
        lax.dynamic_index_in_dim(x_all, pair ^ r, 0, keepdims=False) for r in range(pair_count)
    ]
    part_one, dec_line, x_rel = gate((part_one, dec_line, x_rel))
    x_near = [swap_pair(x_rel[r], r) for r in range(1, pair_count - 1)]
    pre_one = part_one[:, :cells] + swap_chip(part_one[:, cells:])
    pre_one = jnp.concatenate(mirror(pre_one), axis=0)
    dec_line = jnp.concatenate(mirror(jnp.concatenate(dec_line)))
    dec_all = lax.all_gather(
        dec_line.reshape(wide_count, block_units, padded), "pair", axis=1
    )
    normed_one, scaled_one, inverse_one, centre_one, spread_one, (mids, x_near) = normalize(
        pre_one, None, None, (mids, x_near)
    )
    w_enc_mid, w_dec_mid, w_heads, w_dec_in, norm_full = mids
    norm_full = norm_full.astype(F32)
    gains = [norm_full[:, k] for k in range(4)]
    shifts = [norm_full[:, 4 + k] for k in range(4)]
    normed_one = scaled_one * gains[0][:, None] + shifts[0][:, None]
    hidden_one = jax.nn.silu(normed_one).astype(BF)

    pre_two = nn(w_enc_mid, hidden_one)
    normed_two, scaled_two, inverse_two, centre_two, spread_two, _ = normalize(
        pre_two, gains[1], shifts[1]
    )
    hidden_two = jax.nn.silu(normed_two).astype(BF)
    encoded = tn(w_heads, hidden_two) + head_bias[:, None]
    latent_mean = encoded[:latent]
    logvar = encoded[latent:]
    noise_t = noise.T
    spread_factor = jnp.exp(0.5 * logvar)
    code = (latent_mean + spread_factor * noise_t).astype(BF)
    pre_three = nn(w_dec_in, code)
    normed_three, scaled_three, inverse_three, centre_three, spread_three, _ = normalize(
        pre_three, gains[2], shifts[2]
    )
    hidden_three = jax.nn.silu(normed_three).astype(BF)
    pre_four = nn(w_dec_mid, hidden_three)
    normed_four, scaled_four, inverse_four, centre_four, spread_four, _ = normalize(
        pre_four, gains[3], shifts[3]
    )
    hidden_four = jax.nn.silu(normed_four).astype(BF)

    h_chip = jnp.concatenate([hidden_four, swap_chip(hidden_four)], axis=1)
    back_all, kept_diff, bias_sums, recon_sums, dec_parts = output_layer(
        pair.astype(jnp.int32),
        h_chip,
        dec_all,
        x_all,
        mask_all,
        indicator,
        bias_all,
        inv_count,
    )
    exp_logvar = jnp.exp(logvar)
    kl_sum = jnp.sum(exp_logvar + latent_mean * latent_mean - 1.0 - logvar)
    loss_local = 0.5 * jnp.sum(recon_sums) + (0.5 * ALPHA) * kl_sum
    back_four = back_all[:, :cells] + swap_chip(back_all[:, cells:])

    bias_rows = jnp.zeros((pair_count, 2, block_genes), F32)
    bias_rows = lax.dynamic_update_slice_in_dim(
        bias_rows, bias_sums[:, :1, :block_genes], chip, 1
    ).reshape(-1)
    devices = lax.axis_size(ALL)
    share_size = -(-genes // (devices * 8)) * 8
    bias_rows = jnp.pad(bias_rows, (0, devices * share_size - genes)).reshape(devices, share_size)
    x_cut = padded // 256 * 128
    dec_line = lax.psum_scatter(dec_parts, "pair", scatter_dimension=0, tiled=True)
    bp_four, gain_four, shift_four, _, _ = norm_backward(
        back_four, normed_four, scaled_four, inverse_four, gains[3]
    )

    back_three = tn(w_dec_mid, bp_four)
    bp_three, gain_three, shift_three, rest, x_far = norm_backward(
        back_three,
        normed_three,
        scaled_three,
        inverse_three,
        gains[2],
        loss_local[None],
        bias_rows,
        rider=swap_pair(x_rel[3][:x_cut], 3),
    )
    loss = jnp.sum(rest[:, 0]) * inv_count
    bias_share = jnp.sum(rest[:, 1:], axis=0)
    back_code = tn(w_dec_in, bp_three)
    back_mean = back_code + ALPHA * inv_count * latent_mean
    back_logvar = (
        back_code * noise_t * spread_factor * 0.5
        + (ALPHA * 0.5 * inv_count) * (exp_logvar - 1.0)
    )
    back_enc = jnp.concatenate([back_mean, back_logvar], axis=0).astype(BF)
    head_sum = jnp.sum(back_enc.astype(F32), axis=1)
    back_two = nn(w_heads, back_enc)
    bp_two, gain_two, shift_two, rest, _ = norm_backward(
        back_two, normed_two, scaled_two, inverse_two, gains[1], jnp.concatenate([head_sum, bias_share])
    )
    head_bias_grad = jnp.sum(rest[:, : 2 * latent], axis=0)
    out_bias_grad = rest[:, 2 * latent :].reshape(-1)[:genes]

    back_one = tn(w_enc_mid, bp_two)
    x_last = swap_pair(x_rel[3][x_cut:], 3)
    bp_one, gain_one, shift_one, _, (dec_line, x_last) = norm_backward(
        back_one, normed_one, scaled_one, inverse_one, gains[0], rider=(dec_line, x_last)
    )

    dec_blocks = far_first(dec_line.reshape(units, padded))
    mid_in = gate((bp_four, hidden_three, bp_two, hidden_one, hidden_two, back_enc, bp_three, code, bp_one))
    packs = pack_grads(*mid_in[:8])
    d_other = swap_chip(bp_one)
    late_blocks, d_own = gate((enc_blocks, jnp.concatenate([bp_one, d_other], axis=1)))
    d_rel = far_first(d_own)
    d_rel = jnp.stack(d_rel[-1:] + d_rel[:-1])
    if wide_count > LONGEST_RING:
        late_blocks = [[jnp.concatenate(item) for item in zip(*late_blocks)]]
        d_rel = d_rel.reshape(1, units, 2 * cells)
    own_rows, send_rows = zip(
        *[
            input_rows(
                [item for row in late_blocks for item in (row[3:] if r == 3 else row[r : r + 1])],
                d_rel,
                kept_diff,
                r,
                count_all,
            )
            for r in range(pair_count)
        ]
    )
    own_rows, send_rows = jnp.stack(own_rows), jnp.stack(send_rows)
    d_near, d_other, own_rows, send_rows, dec_blocks, packs, dec_near = gate(
        (
            [bp_one] + [swap_pair(bp_one, r) for r in range(1, pair_count)],
            d_other,
            own_rows,
            send_rows,
            dec_blocks,
            packs,
            send_odd(dec_blocks),
        )
    )
    dec_far = send_even(dec_blocks)
    d_swap = [d_other] + [swap_chip(item) for item in d_near[1:]]
    mid_line = lax.psum_scatter(add_chip(packs), "pair", scatter_dimension=0, tiled=True)
    enc_low = plane_grads(d_near, d_swap, [x_rel[0]] + x_near + [x_far, x_last])
    late_rows = [gain_one, gain_two, gain_three, gain_four]
    late_rows += [shift_one, shift_two, shift_three, shift_four]
    late_rows += [centre_one, centre_two, centre_three, centre_four]
    late_rows += [spread_one, spread_two, spread_three, spread_four]
    enc_near, enc_far, mid_line, late_rows, dec_far = gate(
        (send_odd(enc_low), send_even(enc_low), mid_line, late_rows, dec_far)
    )
    enc_in_grad = add_wide(enc_low, enc_near, enc_far)
    dec_out_grad = add_wide(dec_blocks, dec_near, dec_far)
    mid_sum = scatter_wide(far_first(mid_line.reshape(units, mid_line.shape[3])))
    input_grad = place_rows(own_rows, swap_chip(send_rows), genes).T

    wide_index = lax.axis_index("wide")
    per_row = 8 // row_split

    def mine_of(rows_full):
        stacked = jnp.stack(rows_full)
        return lax.dynamic_slice(
            stacked, (block_id * per_row, wide_index * block_units), (per_row, block_units)
        )

    norm_grad = mine_of(late_rows[:8])
    unbias = count_all / (count_all - 1.0)
    stats = mine_of(late_rows[8:12] + [item * unbias for item in late_rows[12:]])
    running_next = (1.0 - MOMENTUM) * running_stats + MOMENTUM * stats

    dec_mid_grad = mid_sum[:, :mid_rows]
    enc_mid_grad = mid_sum[:, mid_rows : 2 * mid_rows]
    in_start = 2 * mid_rows + head_rows
    heads_grad = mid_sum[:, 2 * mid_rows : in_start]
    dec_in_grad = mid_sum[:, in_start : in_start + latent].T
    enc_in_grad = enc_in_grad[:, :block_genes]


    return (
        loss,
        input_grad,
        enc_in_grad.T,
        enc_mid_grad.T,
        heads_grad.T,
        dec_in_grad,
        dec_mid_grad.T,
        dec_out_grad[:, :block_genes].T,
        norm_grad,
        head_bias_grad,
        out_bias_grad,
        running_next,
    )


def solution(mesh):
    split = P(("pair", "chip"), "wide")
    by_cell = P(("wide", "pair", "chip"), None)
    return jax.shard_map(
        on_device,
        mesh=mesh,
        in_specs=(
            by_cell,
            by_cell,
            P(("wide", "pair", "chip")),
            P(),
            split,
            split,
            split,
            P(None, "wide"),
            split,
            split,
            split,
            P(),
            P(),
            split,
        ),
        out_specs=(
            P(),
            by_cell,
            split,
            split,
            split,
            P(None, "wide"),
            split,
            split,
            split,
            P(),
            P(),
            split,
        ),
        check_vma=False,
    )
```
